256 devices in a mesh: vocab: 16 (over x_lo, y, core), seq: 8 (over z), grp: 2 (over x_hi).
Axes of the slice: x: 4 (x_hi: 2, x_lo: 2; x = x_hi * 2 + x_lo), y: 4, z: 8, core: 2. Of those that a mesh axis runs over, the one named last changes fastest.
Arguments:
- decoder_states: bfloat16 [1024, 2048], P('seq'), may hold values from -64 to 64
- encoder_states: bfloat16 [2048, 2048], P(('seq', 'grp')), may hold values from -256 to 256
- ln_gains: float32 [2, 2048], replicated, may hold values from 0.5 to 1.5
- w_query: bfloat16 [2048, 2048], P(None, 'vocab'), may hold values from -0.13258252 to 0.13258252
- w_key: bfloat16 [2048, 2048], P(None, 'vocab'), may hold values from -0.13258252 to 0.13258252
- w_value: bfloat16 [2048, 2048], P(None, 'vocab'), may hold values from -0.125 to 0.125
- w_out: bfloat16 [2048, 2048], P('vocab'), may hold values from -5 to 5
- embedding: bfloat16 [229376, 2048], P(('vocab', 'seq', 'grp')), may hold values from -2 to 2
- labels: int32 [1024], replicated, may hold values from 0 to 229375
- src_length: int32 [1], replicated, may hold values from 1024 to 2048
- tgt_length: int32 [1], replicated, may hold values from 512 to 1024
Outputs:
- token_loss: float32 [1024], replicated
- grad_table: bfloat16 [229376, 2048], P(('vocab', 'seq', 'grp'))
The draws below stay inside these ranges and needn't reach their ends.
All inputs are finite; a program needn't handle non-finite values.
Results may differ from the reference program's by a relative error of at most 0.0082.
Values may be sent and summed in bfloat16 or wider, within the bound.
A program may use at most 64 MiB of HBM per device.

```python
import math
import jax
import jax.numpy as jnp
from jax import lax

D = 2048
HEADS = 16
HEAD_DIM = 128
V_DEV = 896
TGT = 1024
SRC = 2048
VOCAB = 229376


def shared_rows(key):
    key_gauss = jax.random.fold_in(key, 0)
    key_rows = jax.random.fold_in(key, 2)
    key_columns = jax.random.fold_in(key, 3)
    gauss = jax.random.normal(key_gauss, (TGT, D), jnp.float32)
    row_scale = jnp.exp(jax.random.uniform(key_rows, (TGT, 1), jnp.float32, math.log(0.3), math.log(3.0)))
    column_scale = jnp.exp(jax.random.uniform(key_columns, (1, D), jnp.float32, 0.0, math.log(10.0))) / 4.6
    return (gauss, row_scale, column_scale)


def shared_weight(key):
    key_weight = jax.random.fold_in(key, 6)
    return jax.random.normal(key_weight, (D, D), jnp.float32)


def draw_decoder_states(key, part):
    gauss, row_scale, column_scale = shared_rows(key)
    base_rows = gauss * column_scale
    return jnp.clip(base_rows * row_scale, -64.0, 64.0).astype(jnp.bfloat16)


def draw_encoder_states(key, part):
    key = jax.random.fold_in(key, 2)
    key_noise = jax.random.fold_in(key, 0)
    states = jax.random.normal(key_noise, (SRC, D), jnp.float32)
    return jnp.clip(states, -256.0, 256.0).astype(jnp.bfloat16)


def draw_w_query(key, part):
    common_weight = shared_weight(key)
    limit = 6.0 / math.sqrt(D)
    return jnp.clip(common_weight / math.sqrt(D), -limit, limit).astype(jnp.bfloat16)


def draw_w_key(key, part):
    key = jax.random.fold_in(key, 4)
    own_weight = jax.random.normal(key, (D, D), jnp.float32)
    limit = 6.0 / math.sqrt(D)
    mixed = own_weight
    return jnp.clip(mixed / math.sqrt(D), -limit, limit).astype(jnp.bfloat16)


def draw_embedding(key, part):
    key = jax.random.fold_in(key, 5)
    key_table = jax.random.fold_in(key, 0)
    table = jax.random.normal(key_table, (VOCAB, D), jnp.float32) * (3.0 / math.sqrt(D))
    return jnp.clip(table, -2.0, 2.0).astype(jnp.bfloat16)


def plant(values, key, smallest, largest):
    shape = values.shape
    place = [jax.random.randint(jax.random.fold_in(key, axis), (), 0, shape[axis]) for axis in range(len(shape))]
    values = values.at[tuple(place)].set(smallest)
    longest = shape.index(max(shape))
    place[longest] = (place[longest] + 1) % shape[longest]
    return values.at[tuple(place)].set(largest)


def level_of(key, shape, shards, least, largest):
    def one(dim, shards_of):
        heights = jax.random.uniform(jax.random.fold_in(jax.random.fold_in(key, 6), dim), (shards_of,), jnp.float32, least / len(shards), largest / len(shards))
        return jnp.repeat(jnp.exp(heights), shape[dim] // shards_of).reshape((-1,) + (1,) * (len(shape) - dim - 1))

    factor_of = one(*shards[0])
    for cut in shards[1:]:
        factor_of = factor_of * one(*cut)
    return factor_of


def scatter_about(stream_key, dims, width, most, cuts=(), dtype=jnp.bfloat16):
    factor_of = level_of(stream_key, dims, cuts, -0.22, 0.18) if cuts else 1.0
    values = jax.random.normal(stream_key, dims, jnp.float32) * width * factor_of
    return jnp.minimum(jnp.maximum(values, -most), most).astype(dtype)


def setup_inputs(seed: int = 0) -> dict:
    key_list = jax.random.split(jax.random.key(seed), 12)
    return {
        "decoder_states": draw_decoder_states(jax.random.fold_in(key_list[11], 71), 0),
        "encoder_states": draw_encoder_states(jax.random.fold_in(key_list[11], 71), 0),
        "ln_gains": jnp.clip(1.0 + 0.1 * jax.random.normal(key_list[2], (2, D), jnp.float32), 0.5, 1.5),
        "w_query": draw_w_query(jax.random.fold_in(key_list[11], 71), 0),
        "w_key": draw_w_key(jax.random.fold_in(key_list[11], 71), 0),
        "w_value": scatter_about(key_list[5], (D, D), D ** -0.5, 0.125, ((1, 16),)),
        "w_out": scatter_about(key_list[6], (D, D), (16 / D ** 0.5), 5.0, ((0, 16),)),
        "embedding": draw_embedding(jax.random.fold_in(key_list[11], 71), 0),
        "labels": plant(jax.random.randint(key_list[8], (TGT,), 0, VOCAB), jax.random.fold_in(key_list[8], 1), 0, VOCAB - 1).astype(jnp.int32),
        "src_length": jax.random.randint(key_list[9], (1,), SRC // 2, SRC + 1).astype(jnp.int32),
        "tgt_length": jax.random.randint(key_list[10], (1,), TGT // 2, TGT + 1).astype(jnp.int32),
    }


EPSILON = 1e-05

def layer_norm(matrix, gain_row):
    row_mean = lax.optimization_barrier(jnp.mean(matrix, axis=-1, keepdims=True))
    centred = matrix - row_mean
    variance = lax.optimization_barrier(jnp.mean(centred * centred, axis=-1, keepdims=True))
    return centred * lax.rsqrt(variance + EPSILON) * gain_row

def reference(decoder_states, encoder_states, ln_gains, w_query, w_key, w_value, w_out, embedding, labels, src_length, tgt_length):
    states = decoder_states.astype(jnp.float32)
    normed = layer_norm(states, ln_gains[0]).astype(jnp.bfloat16)
    query_scale = 1.0 / math.sqrt(HEAD_DIM)
    query = (jnp.dot(normed, w_query, preferred_element_type=jnp.float32) * query_scale).astype(jnp.bfloat16)
    key_rows = jnp.dot(encoder_states, w_key, preferred_element_type=jnp.float32).astype(jnp.bfloat16)
    value_rows = jnp.dot(encoder_states, w_value, preferred_element_type=jnp.float32).astype(jnp.bfloat16)
    query_heads = query.astype(jnp.float32).reshape(TGT, HEADS, HEAD_DIM)
    key_heads = key_rows.astype(jnp.float32).reshape(SRC, HEADS, HEAD_DIM)
    value_heads = value_rows.astype(jnp.float32).reshape(SRC, HEADS, HEAD_DIM)
    key_valid = jnp.arange(SRC) < src_length[0]
    scores = jnp.einsum('qhd,khd->hqk', query_heads, key_heads)
    scores = jnp.where(key_valid[None, None, :], scores, -1e+30)
    score_top = lax.optimization_barrier(jnp.max(scores, axis=2, keepdims=True))
    exp_scores = jnp.where(key_valid[None, None, :], jnp.exp(scores - score_top), 0.0)
    weights = (exp_scores / lax.optimization_barrier(jnp.sum(exp_scores, axis=2, keepdims=True))).astype(jnp.bfloat16)
    context = jnp.einsum('hqk,khd->qhd', weights.astype(jnp.float32), value_heads)
    context = context.reshape(TGT, D).astype(jnp.bfloat16)
    hidden = states + jnp.dot(context, w_out, preferred_element_type=jnp.float32)
    final_rows = layer_norm(hidden, ln_gains[1]).astype(jnp.bfloat16)
    row_live = jnp.arange(TGT) < tgt_length[0]
    block_rows = V_DEV * 8
    block_count = VOCAB // block_rows
    tables = embedding.reshape(block_count, block_rows, D)
    starts = (jnp.arange(block_count) * block_rows).astype(jnp.int32)
    offsets = jnp.arange(block_rows).astype(jnp.int32)

    def block_logits(table, start):
        logits = jnp.dot(final_rows, table.T, preferred_element_type=jnp.float32)
        label_hit = labels[:, None] == (start + offsets)[None, :]
        return (logits, label_hit)

    def stats_step(carried, inputs):
        top_row, row_total, picked = carried
        logits, label_hit = block_logits(inputs[0], inputs[1])
        new_top = jnp.maximum(top_row, lax.optimization_barrier(jnp.max(logits, axis=1)))
        row_total = row_total * jnp.exp(top_row - new_top) + lax.optimization_barrier(jnp.sum(jnp.exp(logits - new_top[:, None]), axis=1))
        picked = picked + lax.optimization_barrier(jnp.sum(jnp.where(label_hit, logits, 0.0), axis=1))
        return ((new_top, row_total, picked), None)
    initial = (jnp.full((TGT,), -1e+30, jnp.float32), jnp.zeros((TGT,), jnp.float32), jnp.zeros((TGT,), jnp.float32))
    (row_max, row_total, picked), unused = lax.scan(stats_step, initial, (tables, starts))
    token_loss = jnp.where(row_live, row_max + jnp.log(row_total) - picked, 0.0)

    def grad_block(inputs):
        logits, label_hit = block_logits(inputs[0], inputs[1])
        prob_rows = jnp.exp(logits - row_max[:, None]) / row_total[:, None]
        grad_logits = jnp.where(row_live[:, None], prob_rows - label_hit.astype(jnp.float32), 0.0).astype(jnp.bfloat16)
        return jnp.dot(grad_logits.T, final_rows, preferred_element_type=jnp.float32).astype(jnp.bfloat16)
    grad_table = lax.map(grad_block, (tables, starts)).reshape(VOCAB, D)
    return (token_loss, grad_table)
```

```python
import functools
import math

import jax
import jax.numpy as jnp
from jax import lax
from jax.experimental import pallas as pl
from jax.experimental.pallas import tpu as pltpu
from jax.sharding import PartitionSpec as P

HEAD_DIM = 128
EPSILON = 1e-05
MESH = pl.DeviceIdType.MESH
NC = 2
NY = 4
NT = (((1,), (1,)), ((), ()))
F32, BF16 = jnp.float32, jnp.bfloat16


def front_kernel(
    cfg,
    dec_in,
    enc_in,
    gains,
    labels,
    src_len,
    tgt_len,
    wq_in,
    wk_in,
    wv_in,
    wo_in,
    emb_in,
    loss_out,
    lse_out,
    hit_out,
    logit_out,
    rows_out,
    dec,
    enc,
    wq,
    wkv,
    wo,
    emb,
    kv,
    ctx_own,
    ctx_got,
    part,
    summed,
    norm_stat,
    rows,
    logit,
    local_stat,
    stat_x,
    stat_y,
    stat_z,
    load_sem,
    store_sem,
    kv_send,
    kv_recv,
    ctx_sem,
    sum_send,
    sum_recv,
    norm_send,
    norm_recv,
    first_send,
    first_recv,
    second_send,
    second_recv,
    ring_send,
    ring_recv,
    third_send,
    third_recv,
    core_send,
    core_recv,
    stat_send,
    stat_recv,
):
    nv, nz, ng, ny, nxl = cfg
    d = dec.shape[1]
    tz = dec.shape[0]
    ez = enc.shape[0]
    hd = wq.shape[1]
    tg = tz // ng
    ty = tg // ny
    width = d // (nxl * NC)
    wa, wb = width // 2, width // 4
    table_rows = emb.shape[0]
    nx = ng * nxl
    half = nz // 2

    v = lax.axis_index("vocab")
    z = lax.axis_index("seq")
    g = lax.axis_index("grp")
    c = v % NC
    y = (v // NC) % ny
    xl = v // (NC * ny)
    x = g * nxl + xl

    def vocab_of(xl_, y_, c_):
        return (xl_ * ny + y_) * NC + c_

    def at_x(x_, c_=None):
        return {"vocab": vocab_of(x_ % nxl, y, c if c_ is None else c_), "seq": z, "grp": x_ // nxl}

    def at_y(y_):
        return {"vocab": vocab_of(xl, y_, c), "seq": z, "grp": g}

    def at_z(z_):
        return {"vocab": v, "seq": z_, "grp": g}

    def at_v(v_):
        return {"vocab": v_, "seq": z, "grp": g}

    barrier = pltpu.get_barrier_semaphore()
    friends = [at_v((v + o) % nv) for o in range(1, nv)]
    friends += [at_z((z + o) % nz) for o in range(1, nz)]
    friends += [
        {"vocab": vocab_of(xl_, y, c_), "seq": z, "grp": (g + o) % ng}
        for o in range(1, ng)
        for xl_ in range(nxl)
        for c_ in range(NC)
    ]
    for friend in friends:
        pl.semaphore_signal(barrier, inc=1, device_id=friend, device_id_type=MESH)

    loads = [
        pltpu.make_async_copy(src, dst, load_sem.at[i])
        for i, (src, dst) in enumerate(
            (
                (enc_in, enc),
                (wk_in, wkv.at[:, 0:hd]),
                (wv_in, wkv.at[:, hd : 2 * hd]),
                (dec_in, dec),
                (wq_in, wq),
                (wo_in, wo),
                (emb_in, emb),
            )
        )
    ]
    for load in loads:
        load.start()

    sent = []

    def send(ref, dst, send_sem, recv_sem, device):
        copy = pltpu.make_async_remote_copy(
            src_ref=ref,
            dst_ref=dst,
            send_sem=send_sem,
            recv_sem=recv_sem,
            device_id=device,
            device_id_type=MESH,
        )
        copy.start()
        sent.append(copy)

    def arrived(ref, recv_sem):
        pltpu.make_async_remote_copy(
            src_ref=ref,
            dst_ref=ref,
            send_sem=load_sem.at[0],
            recv_sem=recv_sem,
            device_id=at_z((z + 1) % nz),
            device_id_type=MESH,
        ).wait_recv()

    def ring_post(view, t, send_sems, recv_sems):
        for way, step in ((0, 1), (1, nz - 1)):
            block = (z + t * (nz - step)) % nz
            for part_ in (0, 1) if t + 1 < half else (way,):
                ref = view(block, part_)
                send(ref, ref, send_sems.at[way, t, part_], recv_sems.at[way, t, part_], at_z((z + step) % nz))

    def ring_wait(view, t, recv_sems):
        for way, step in ((0, 1), (1, nz - 1)):
            block = (z + t * (nz - step)) % nz
            for part_ in (0, 1) if t < half else (way,):
                arrived(view(block, part_), recv_sems.at[way, t - 1, part_])

    def ring_blocks(t):
        return [(z + nz - t) % nz, (z + t) % nz] if t < half else [(z + half) % nz]

    for i in (0, 1, 2):
        loads[i].wait()
    own_kv = jnp.dot(enc[...], wkv[...], preferred_element_type=F32).astype(BF16)
    kv[z, 0] = own_kv[:, 0:hd]
    kv[z, 1] = own_kv[:, hd : 2 * hd]
    pl.semaphore_wait(barrier, len(friends))

    def kv_view(block, part_):
        return kv.at[block, part_]

    ring_post(kv_view, 0, kv_send, kv_recv)

    loads[3].wait()
    states = dec[...].astype(F32)
    centred = states - jnp.mean(states, axis=1, keepdims=True)
    variance = jnp.mean(centred * centred, axis=1, keepdims=True)
    normed = (centred * lax.rsqrt(variance + EPSILON) * gains[0:1, :]).astype(BF16)
    loads[4].wait()
    query = (jnp.dot(normed, wq[...], preferred_element_type=F32) * (1.0 / math.sqrt(hd))).astype(BF16)

    source_count = src_len[0]

    def scores_of(block):
        s = lax.dot_general(query, kv[block, 0], NT, preferred_element_type=F32)
        place = (block * ng + g) * ez + lax.broadcasted_iota(jnp.int32, s.shape, 1)
        valid = place < source_count
        return block, valid, jnp.where(valid, s, -1e30)

    scored = [scores_of(z)]
    for t in range(1, half + 1):
        ring_wait(kv_view, t, kv_recv)
        if t < half:
            ring_post(kv_view, t, kv_send, kv_recv)
        scored += [scores_of(block) for block in ring_blocks(t)]
    top = functools.reduce(jnp.maximum, [s for _, _, s in scored])
    top = jnp.max(top, axis=1, keepdims=True)
    total = jnp.zeros((tz, ez), F32)
    acc = jnp.zeros((tz, hd), F32)
    for block, valid, s in scored:
        e = jnp.where(valid, jnp.exp(s - top), 0.0)
        total = total + e
        acc = acc + jnp.dot(e.astype(BF16), kv[block, 1], preferred_element_type=F32)
    total = jnp.sum(total, axis=1, keepdims=True)
    low = lax.broadcasted_iota(jnp.int32, (tz, 128), 1) < 64
    ctx_own[:, 0:hd] = acc
    ctx_own[:, hd : hd + 128] = jnp.where(low, top, total)
    send(
        ctx_own.at[pl.ds(pl.multiple_of((1 - g) * tg, tg), tg)],
        ctx_got,
        ctx_sem.at[0],
        ctx_sem.at[1],
        {"vocab": v, "seq": z, "grp": 1 - g},
    )
    arrived(ctx_got, ctx_sem.at[1])
    mine = ctx_own[pl.ds(pl.multiple_of(g * tg, tg), tg), :]
    other = ctx_got[...]
    top0, top1 = mine[:, hd : hd + 1], other[:, hd : hd + 1]
    both = jnp.maximum(top0, top1)
    f0, f1 = jnp.exp(top0 - both), jnp.exp(top1 - both)
    total = mine[:, hd + 64 : hd + 65] * f0 + other[:, hd + 64 : hd + 65] * f1
    context = ((mine[:, 0:hd] * f0 + other[:, 0:hd] * f1) / total).astype(BF16)

    def columns_of(xl_, c_):
        base = c_ * (d // NC)
        return (
            (base + xl_ * wa, wa),
            (base + nxl * wa + xl_ * wb, wb),
            (base + nxl * (wa + wb) + xl_ * wb, wb),
        )

    loads[5].wait()
    projected = jnp.dot(context, wo[...], preferred_element_type=F32)
    for xl_ in range(nxl):
        for y_ in range(ny):
            for c_ in range(NC):
                at = 0
                for start, size in columns_of(xl_, c_):
                    part[vocab_of(xl_, y_, c_), :, at : at + size] = projected[
                        y_ * ty : (y_ + 1) * ty, start : start + size
                    ]
                    at += size
    for o in range(1, nv):
        to = (v + o) % nv
        send(part.at[to], summed.at[v], sum_send.at[o], sum_recv.at[v], at_v(to))
    own_cols = [(pl.multiple_of(start, 128), size) for start, size in columns_of(xl, c)]
    own_row = pl.multiple_of(g * tg + y * ty, ty)
    hidden = part[v] + jnp.concatenate(
        [dec[pl.ds(own_row, ty), pl.ds(start, size)].astype(F32) for start, size in own_cols], axis=1
    )
    for o in range(1, nv):
        frm = (v + o) % nv
        arrived(summed.at[frm], sum_recv.at[frm])
        hidden = hidden + summed[frm]

    piece = xl * NC + c
    pieces = nxl * NC
    own_mean = jnp.mean(hidden, axis=1, keepdims=True)
    own_square = jnp.sum((hidden - own_mean) * (hidden - own_mean), axis=1, keepdims=True)
    low = lax.broadcasted_iota(jnp.int32, (ty, 128), 1) < 64
    norm_stat[piece] = jnp.where(low, own_mean, own_square)
    for o in range(1, pieces):
        to = (piece + o) % pieces
        send(
            norm_stat.at[piece],
            norm_stat.at[piece],
            norm_send.at[o],
            norm_recv.at[piece],
            at_v(vocab_of(to // NC, y, to % NC)),
        )
    for o in range(1, pieces):
        frm = (piece + o) % pieces
        arrived(norm_stat.at[frm], norm_recv.at[frm])
    means = [norm_stat[i, :, 0:1] for i in range(pieces)]
    squares = [norm_stat[i, :, 64:65] for i in range(pieces)]
    mean = sum(means) * (1.0 / pieces)
    square = sum(squares) + width * sum((m - mean) * (m - mean) for m in means)
    scale = lax.rsqrt(square * (1.0 / d) + EPSILON)
    gain = jnp.concatenate([gains[1:2, pl.ds(start, size)] for start, size in own_cols], axis=1)
    final = ((hidden - mean) * scale * gain).astype(BF16)
    at = 0
    for start, size in own_cols:
        rows[z, g, y, :, pl.ds(start, size)] = final[:, at : at + size]
        at += size

    def cols_all(c_):
        base = pl.multiple_of(c_ * (d // NC), 128)
        return (
            pl.ds(base, nxl * wa),
            pl.ds(pl.multiple_of(base + nxl * wa, 128), nxl * wb),
            pl.ds(pl.multiple_of(base + nxl * (wa + wb), 128), nxl * wb),
        )

    def cols_piece(xl_):
        return [pl.ds(pl.multiple_of(start, 128), size) for start, size in columns_of(xl_, c)]

    own_a, own_b, own_c = cols_piece(xl)
    all_a, all_b, all_c = cols_all(c)

    def exchange(n, me, ref_of, send_sems, recv_sems, device_of):
        for o in range(1, n):
            ref = ref_of(me)
            send(ref, ref, send_sems.at[o], recv_sems.at[me], device_of((me + o) % n))

    def collect(n, me, ref_of, recv_sems, then=None):
        for o in range(1, n):
            frm = (me + o) % n
            arrived(ref_of(frm), recv_sems.at[frm])
            if then is not None:
                then(frm)

    def a1(x_):
        return rows.at[z, x_ // nxl, y, :, cols_piece(x_ % nxl)[0]]

    def b1(z_):
        return rows.at[z_, g, y, :, own_b]

    def c1(z_):
        return rows.at[z_, g, y, :, own_c]

    def a2(y_):
        return rows.at[z, :, y_, :, all_a]

    def b2(x_):
        return rows.at[:, x_ // nxl, y, :, cols_piece(x_ % nxl)[1]]

    def c2(y_):
        return rows.at[:, g, y_, :, own_c]

    def b3(y_):
        return rows.at[:, :, y_, :, all_b]

    def c3(x_):
        return rows.at[:, x_ // nxl, :, :, cols_piece(x_ % nxl)[2]]

    def a3(block, part_):
        base = pl.multiple_of(c * (d // NC) + part_ * (nxl * wa // 2), 128)
        return rows.at[block, :, :, :, pl.ds(base, nxl * wa // 2)]

    exchange(nx, x, a1, first_send.at[0], first_recv.at[0], at_x)
    exchange(nz, z, b1, first_send.at[1], first_recv.at[1], at_z)
    exchange(nz, z, c1, first_send.at[2], first_recv.at[2], at_z)
    collect(nx, x, a1, first_recv.at[0])
    exchange(ny, y, a2, second_send.at[0], second_recv.at[0], at_y)
    collect(nz, z, b1, first_recv.at[1])
    exchange(nx, x, b2, second_send.at[1], second_recv.at[1], at_x)
    collect(nz, z, c1, first_recv.at[2])
    exchange(ny, y, c2, second_send.at[2], second_recv.at[2], at_y)

    sibling = at_x(x, 1 - c)

    def to_core(kind, i, ref):
        send(ref, ref, core_send.at[kind, i], core_recv.at[kind, i], sibling)

    def a_block(c_):
        return lambda z_: rows.at[z_, :, :, :, cols_all(c_)[0]]

    def b_block(c_):
        return lambda y_: rows.at[:, :, y_, :, cols_all(c_)[1]]

    def c_block(c_):
        def view(x_):
            base = pl.multiple_of(c_ * (d // NC) + nxl * (wa + wb) + (x_ % nxl) * wb, 128)
            return rows.at[:, x_ // nxl, :, :, pl.ds(base, wb)]

        return view

    def share(kind, view):
        return lambda i: to_core(kind, i, view(c)(i))

    share_a, share_b, share_c = share(0, a_block), share(1, b_block), share(2, c_block)

    collect(ny, y, a2, second_recv.at[0])
    ring_post(a3, 0, ring_send, ring_recv)
    share_a(z)
    collect(nx, x, b2, second_recv.at[1])
    exchange(ny, y, b3, third_send.at[0], third_recv.at[0], at_y)
    share_b(y)
    collect(ny, y, c2, second_recv.at[2])
    exchange(nx, x, c3, third_send.at[1], third_recv.at[1], at_x)
    share_c(x)
    for t in range(1, half + 1):
        ring_wait(a3, t, ring_recv)
        if t < half:
            ring_post(a3, t, ring_send, ring_recv)
        for block in ring_blocks(t):
            share_a(block)
        if t == half - 1:
            collect(ny, y, b3, third_recv.at[0], share_b)
            collect(nx, x, c3, third_recv.at[1], share_c)
    for kind, count, view in ((0, nz, a_block), (1, ny, b_block), (2, nx, c_block)):
        for i in range(count):
            arrived(view(1 - c)(i), core_recv.at[kind, i])

    rows_store = pltpu.make_async_copy(rows, rows_out, store_sem.at[0])
    rows_store.start()

    loads[6].wait()
    table_base = ((v * nz + z) * ng + g) * table_rows
    step_blocks = max(1, 256 // tz)
    step_rows = step_blocks * tz

    def logit_step(i, carry):
        chunk = rows[pl.ds(i * step_blocks, step_blocks)].reshape(step_rows, d)
        lanes = pl.ds(pl.multiple_of(i * step_rows, 128), step_rows)
        values = lax.dot_general(emb[...], chunk, NT, preferred_element_type=F32)
        logit[:, lanes] = values
        top_ = jnp.max(values, axis=0, keepdims=True)
        total_ = jnp.sum(jnp.exp(values - top_), axis=0, keepdims=True)
        token = table_base + lax.broadcasted_iota(jnp.int32, values.shape, 0)
        local_stat[i, 0:1, :] = top_ + jnp.log(total_)
        local_stat[i, 1:2, :] = jnp.sum(jnp.where(token == labels[:, lanes], values, 0.0), axis=0, keepdims=True)
        return carry

    steps = nz // step_blocks
    lax.fori_loop(0, steps, logit_step, 0)
    logit_store = pltpu.make_async_copy(logit, logit_out, store_sem.at[1])
    logit_store.start()

    stat_rows = nz * tz // 128
    per_step = step_rows // 128
    nxc = nx * NC
    xc = x * NC + c
    for r in range(stat_rows):
        for k in range(2):
            stat_x[xc, k * stat_rows + r : k * stat_rows + r + 1, :] = local_stat[
                r // per_step, k : k + 1, (r % per_step) * 128 : (r % per_step + 1) * 128
            ]

    def merge(ref, n):
        lses = [ref[i, 0:stat_rows] for i in range(n)]
        top_ = functools.reduce(jnp.maximum, lses)
        total_ = sum(jnp.exp(s - top_) for s in lses)
        return top_ + jnp.log(total_), sum(ref[i, stat_rows : 2 * stat_rows] for i in range(n))

    def stat_round(ref, n, me, k, device_of):
        exchange(n, me, lambda i: ref.at[i], stat_send.at[k], stat_recv.at[k], device_of)
        collect(n, me, lambda i: ref.at[i], stat_recv.at[k])
        return merge(ref, n)

    lse, picked = stat_round(stat_x, nxc, xc, 0, lambda i: at_x(i // NC, i % NC))
    stat_y[y, 0:stat_rows] = lse
    stat_y[y, stat_rows : 2 * stat_rows] = picked
    lse, picked = stat_round(stat_y, ny, y, 1, at_y)
    stat_z[z, 0:stat_rows] = lse
    stat_z[z, stat_rows : 2 * stat_rows] = picked
    lse, picked = stat_round(stat_z, nz, z, 2, at_z)

    place = lax.broadcasted_iota(jnp.int32, lse.shape, 0) * 128 + lax.broadcasted_iota(jnp.int32, lse.shape, 1)
    live = place < tgt_len[0]
    loss_out[...] = jnp.where(live, lse - picked, 0.0)
    lse = jnp.where(live, lse, 1e30)
    for r in range(stat_rows):
        lse_out[0:1, r * 128 : (r + 1) * 128] = lse[r : r + 1, :]
    place = lax.broadcasted_iota(jnp.int32, labels.shape, 1)
    hit_out[...] = jnp.where(place < tgt_len[0], labels[...] - table_base, -1)

    for copy in sent:
        copy.wait_send()
    rows_store.wait()
    logit_store.wait()


def grad_kernel(lse, hit, logit, rows, out):
    base = pl.program_id(0) * out.shape[0]
    token = base + lax.broadcasted_iota(jnp.int32, logit.shape, 0)
    grad = jnp.exp(logit[...] - lse[...]) - jnp.where(token == hit[...], 1.0, 0.0)
    out[...] = jnp.dot(grad.astype(BF16), rows[...], preferred_element_type=F32).astype(BF16)


def body(
    cfg,
    decoder_states,
    encoder_states,
    ln_gains,
    w_query,
    w_key,
    w_value,
    w_out,
    embedding,
    labels,
    src_length,
    tgt_length,
):
    nv, nz, ng, ny, nxl = cfg
    tz, d = decoder_states.shape
    ez = encoder_states.shape[0]
    hd = w_query.shape[1]
    table_rows = embedding.shape[0]
    target = labels.shape[0]
    tg = tz // ng
    ty = tg // ny
    width = d // (nxl * NC)
    nx = ng * nxl
    half = nz // 2
    pieces = nxl * NC
    step_blocks = max(1, 256 // tz)
    stat_rows = target // 128
    most = max(nz, nx, ny)
    hbm = pl.BlockSpec(memory_space=pl.ANY)
    vmem = pl.BlockSpec(memory_space=pltpu.VMEM)
    smem = pl.BlockSpec(memory_space=pltpu.SMEM)
    dma = pltpu.SemaphoreType.DMA
    loss, lse, hit, logit, rows = pl.pallas_call(
        functools.partial(front_kernel, cfg),
        out_shape=(
            jax.ShapeDtypeStruct((stat_rows, 128), F32),
            jax.ShapeDtypeStruct((1, target), F32),
            jax.ShapeDtypeStruct((1, target), jnp.int32),
            jax.ShapeDtypeStruct((table_rows, target), F32),
            jax.ShapeDtypeStruct((nz, ng, ny, ty, d), BF16),
        ),
        in_specs=[hbm, hbm, vmem, vmem, smem, smem, hbm, hbm, hbm, hbm, hbm],
        out_specs=(vmem, vmem, vmem, hbm, hbm),
        scratch_shapes=[
            pltpu.VMEM((tz, d), BF16),
            pltpu.VMEM((ez, d), BF16),
            pltpu.VMEM((d, hd), BF16),
            pltpu.VMEM((d, 2 * hd), BF16),
            pltpu.VMEM((hd, d), BF16),
            pltpu.VMEM((table_rows, d), BF16),
            pltpu.VMEM((nz, 2, ez, hd), BF16),
            pltpu.VMEM((tz, hd + 128), F32),
            pltpu.VMEM((tg, hd + 128), F32),
            pltpu.VMEM((nv, ty, width), F32),
            pltpu.VMEM((nv, ty, width), F32),
            pltpu.VMEM((pieces, ty, 128), F32),
            pltpu.VMEM((nz, ng, ny, ty, d), BF16),
            pltpu.VMEM((table_rows, target), F32),
            pltpu.VMEM((nz // step_blocks, 8, step_blocks * tz), F32),
            pltpu.VMEM((nx * NC, 2 * stat_rows, 128), F32),
            pltpu.VMEM((ny, 2 * stat_rows, 128), F32),
            pltpu.VMEM((nz, 2 * stat_rows, 128), F32),
            dma((7,)),
            dma((2,)),
            dma((2, half, 2)),
            dma((2, half, 2)),
            dma((2,)),
            dma((nv,)),
            dma((nv,)),
            dma((pieces,)),
            dma((pieces,)),
            dma((3, most)),
            dma((3, most)),
            dma((3, most)),
            dma((3, most)),
            dma((2, half, 2)),
            dma((2, half, 2)),
            dma((2, most)),
            dma((2, most)),
            dma((3, most)),
            dma((3, most)),
            dma((3, max(most, nx * NC))),
            dma((3, max(most, nx * NC))),
        ],
        compiler_params=pltpu.CompilerParams(
            collective_id=0, has_side_effects=True, vmem_limit_bytes=48 * 1024 * 1024
        ),
    )(
        decoder_states,
        encoder_states,
        ln_gains,
        labels.reshape(1, target),
        src_length,
        tgt_length,
        w_query,
        w_key,
        w_value,
        w_out,
        embedding,
    )
    block = 128
    grad_table = pl.pallas_call(
        grad_kernel,
        out_shape=jax.ShapeDtypeStruct((table_rows, d), BF16),
        grid=(table_rows // block,),
        in_specs=[
            pl.BlockSpec((1, target), lambda i: (0, 0)),
            pl.BlockSpec((1, target), lambda i: (0, 0)),
            pl.BlockSpec((block, target), lambda i: (i, 0)),
            pl.BlockSpec((target, d), lambda i: (0, 0)),
        ],
        out_specs=pl.BlockSpec((block, d), lambda i: (i, 0)),
        compiler_params=pltpu.CompilerParams(vmem_limit_bytes=32 * 1024 * 1024),
    )(lse, hit, logit, rows.reshape(target, d))
    return (loss.reshape(target), grad_table)


def solution(mesh):
    nv, nz, ng = mesh.shape["vocab"], mesh.shape["seq"], mesh.shape["grp"]
    cfg = (nv, nz, ng, NY, nv // (NY * NC))
    in_specs = (
        P("seq", None),
        P(("seq", "grp"), None),
        P(),
        P(None, "vocab"),
        P(None, "vocab"),
        P(None, "vocab"),
        P("vocab", None),
        P(("vocab", "seq", "grp"), None),
        P(),
        P(),
        P(),
    )
    out_specs = (P(), P(("vocab", "seq", "grp"), None))
    return jax.shard_map(
        functools.partial(body, cfg), mesh=mesh, in_specs=in_specs, out_specs=out_specs, check_vma=False
    )
```

```python
import functools
import math

import jax
import jax.numpy as jnp
from jax import lax
from jax.experimental import pallas as pl
from jax.experimental.pallas import tpu as pltpu
from jax.sharding import PartitionSpec as P

HEAD_DIM = 128
EPSILON = 1e-05
MESH = pl.DeviceIdType.MESH
NC = 2
NY = 4
NT = (((1,), (1,)), ((), ()))
F32, BF16 = jnp.float32, jnp.bfloat16


def front_kernel(
    cfg,
    src_len,
    tgt_len,
    dec_in,
    enc_in,
    gains_in,
    labels_in,
    wq_in,
    wk_in,
    wv_in,
    wo_in,
    emb_in,
    loss_out,
    grad,
    rows,
    gains,
    labels,
    dec,
    enc,
    wq,
    wkv,
    wo,
    emb,
    kv,
    ctx_own,
    ctx_got,
    part,
    summed,
    norm_stat,
    logit,
    local_stat,
    stat_x,
    stat_y,
    stat_z,
    load_sem,
    kv_send,
    kv_recv,
    ctx_sem,
    sum_send,
    sum_recv,
    norm_send,
    norm_recv,
    first_send,
    first_recv,
    second_send,
    second_recv,
    ring_send,
    ring_recv,
    third_send,
    third_recv,
    core_send,
    core_recv,
    stat_send,
    stat_recv,
):
    nv, nz, ng, ny, nxl = cfg
    d = dec.shape[1]
    tz = dec.shape[0]
    ez = enc.shape[0]
    hd = wq.shape[1]
    tg = tz // ng
    ty = tg // ny
    width = d // (nxl * NC)
    wa, wb, wc = width // 4, width // 4, width // 2
    table_rows = emb.shape[0]
    nx = ng * nxl
    half = nz // 2

    v = lax.axis_index("vocab")
    z = lax.axis_index("seq")
    g = lax.axis_index("grp")
    c = v % NC
    y = (v // NC) % ny
    xl = v // (NC * ny)
    x = g * nxl + xl

    def vocab_of(xl_, y_, c_):
        return (xl_ * ny + y_) * NC + c_

    def at_x(x_, c_=None):
        return {"vocab": vocab_of(x_ % nxl, y, c if c_ is None else c_), "seq": z, "grp": x_ // nxl}

    def at_y(y_):
        return {"vocab": vocab_of(xl, y_, c), "seq": z, "grp": g}

    def at_z(z_):
        return {"vocab": v, "seq": z_, "grp": g}

    def at_v(v_):
        return {"vocab": v_, "seq": z, "grp": g}

    barrier = pltpu.get_barrier_semaphore()
    friends = [at_v((v + o) % nv) for o in range(1, nv)]
    friends += [at_z((z + o) % nz) for o in range(1, nz)]
    friends += [
        {"vocab": vocab_of(xl_, y, c_), "seq": z, "grp": (g + o) % ng}
        for o in range(1, ng)
        for xl_ in range(nxl)
        for c_ in range(NC)
    ]
    for friend in friends:
        pl.semaphore_signal(barrier, inc=1, device_id=friend, device_id_type=MESH)

    loads = [
        pltpu.make_async_copy(src, dst, load_sem.at[i])
        for i, (src, dst) in enumerate(
            (
                (enc_in, enc),
                (wk_in, wkv.at[:, 0:hd]),
                (wv_in, wkv.at[:, hd : 2 * hd]),
                (dec_in, dec),
                (wq_in, wq),
                (wo_in, wo),
                (emb_in, emb),
                (gains_in, gains),
                (labels_in, labels),
            )
        )
    ]
    for load in loads:
        load.start()

    sent = []

    def send(ref, dst, send_sem, recv_sem, device):
        copy = pltpu.make_async_remote_copy(
            src_ref=ref,
            dst_ref=dst,
            send_sem=send_sem,
            recv_sem=recv_sem,
            device_id=device,
            device_id_type=MESH,
        )
        copy.start()
        sent.append(copy)

    def arrived(ref, recv_sem):
        pltpu.make_async_remote_copy(
            src_ref=ref,
            dst_ref=ref,
            send_sem=load_sem.at[0],
            recv_sem=recv_sem,
            device_id=at_z((z + 1) % nz),
            device_id_type=MESH,
        ).wait_recv()

    def ring_post(view, t, send_sems, recv_sems):
        for way, step in ((0, 1), (1, nz - 1)):
            block = (z + t * (nz - step)) % nz
            for part_ in (0, 1) if t + 1 < half else (way,):
                ref = view(block, part_)
                send(ref, ref, send_sems.at[way, t, part_], recv_sems.at[way, t, part_], at_z((z + step) % nz))

    def ring_wait(view, t, recv_sems):
        for way, step in ((0, 1), (1, nz - 1)):
            block = (z + t * (nz - step)) % nz
            for part_ in (0, 1) if t < half else (way,):
                arrived(view(block, part_), recv_sems.at[way, t - 1, part_])

    def ring_blocks(t):
        return [(z + nz - t) % nz, (z + t) % nz] if t < half else [(z + half) % nz]

    for i in (0, 1, 2):
        loads[i].wait()
    own_kv = jnp.dot(enc[...], wkv[...], preferred_element_type=F32).astype(BF16)
    kv[z, 0] = own_kv[:, 0:hd]
    kv[z, 1] = own_kv[:, hd : 2 * hd]
    pl.semaphore_wait(barrier, len(friends))

    def kv_view(block, part_):
        return kv.at[block, part_]

    ring_post(kv_view, 0, kv_send, kv_recv)

    loads[3].wait()
    loads[7].wait()
    states = dec[...].astype(F32)
    centred = states - jnp.mean(states, axis=1, keepdims=True)
    variance = jnp.mean(centred * centred, axis=1, keepdims=True)
    normed = (centred * lax.rsqrt(variance + EPSILON) * gains[0:1, :]).astype(BF16)
    loads[4].wait()
    query = (jnp.dot(normed, wq[...], preferred_element_type=F32) * (1.0 / math.sqrt(hd))).astype(BF16)

    source_count = src_len[0]

    def scores_of(block):
        s = lax.dot_general(query, kv[block, 0], NT, preferred_element_type=F32)
        place = (block * ng + g) * ez + lax.broadcasted_iota(jnp.int32, s.shape, 1)
        valid = place < source_count
        return block, valid, jnp.where(valid, s, -1e30)

    scored = [scores_of(z)]
    for t in range(1, half + 1):
        ring_wait(kv_view, t, kv_recv)
        if t < half:
            ring_post(kv_view, t, kv_send, kv_recv)
        scored += [scores_of(block) for block in ring_blocks(t)]
    top = functools.reduce(jnp.maximum, [s for _, _, s in scored])
    top = jnp.max(top, axis=1, keepdims=True)
    total = jnp.zeros((tz, ez), F32)
    acc = jnp.zeros((tz, hd), F32)
    for block, valid, s in scored:
        e = jnp.where(valid, jnp.exp(s - top), 0.0)
        total = total + e
        acc = acc + jnp.dot(e.astype(BF16), kv[block, 1], preferred_element_type=F32)
    total = jnp.sum(total, axis=1, keepdims=True)
    low = lax.broadcasted_iota(jnp.int32, (tz, 128), 1) < 64
    ctx_own[:, 0:hd] = acc
    ctx_own[:, hd : hd + 128] = jnp.where(low, top, total)
    send(
        ctx_own.at[pl.ds(pl.multiple_of((1 - g) * tg, tg), tg)],
        ctx_got,
        ctx_sem.at[0],
        ctx_sem.at[1],
        {"vocab": v, "seq": z, "grp": 1 - g},
    )
    arrived(ctx_got, ctx_sem.at[1])
    mine = ctx_own[pl.ds(pl.multiple_of(g * tg, tg), tg), :]
    other = ctx_got[...]
    top0, top1 = mine[:, hd : hd + 1], other[:, hd : hd + 1]
    both = jnp.maximum(top0, top1)
    f0, f1 = jnp.exp(top0 - both), jnp.exp(top1 - both)
    total = mine[:, hd + 64 : hd + 65] * f0 + other[:, hd + 64 : hd + 65] * f1
    context = ((mine[:, 0:hd] * f0 + other[:, 0:hd] * f1) / total).astype(BF16)

    def columns_of(xl_, c_):
        base = c_ * (d // NC)
        return (
            (base + xl_ * wa, wa),
            (base + nxl * wa + xl_ * wb, wb),
            (base + nxl * (wa + wb) + xl_ * wc, wc),
        )

    loads[5].wait()
    projected = jnp.dot(context, wo[...], preferred_element_type=F32)
    for xl_ in range(nxl):
        for y_ in range(ny):
            for c_ in range(NC):
                at = 0
                for start, size in columns_of(xl_, c_):
                    part[vocab_of(xl_, y_, c_), :, at : at + size] = projected[
                        y_ * ty : (y_ + 1) * ty, start : start + size
                    ]
                    at += size
    for o in range(1, nv):
        to = (v + o) % nv
        send(part.at[to], summed.at[v], sum_send.at[o], sum_recv.at[v], at_v(to))
    own_cols = [(pl.multiple_of(start, 128), size) for start, size in columns_of(xl, c)]
    own_row = pl.multiple_of(g * tg + y * ty, ty)
    hidden = part[v] + jnp.concatenate(
        [dec[pl.ds(own_row, ty), pl.ds(start, size)].astype(F32) for start, size in own_cols], axis=1
    )
    for o in range(1, nv):
        frm = (v + o) % nv
        arrived(summed.at[frm], sum_recv.at[frm])
        hidden = hidden + summed[frm]

    piece = xl * NC + c
    pieces = nxl * NC
    own_mean = jnp.mean(hidden, axis=1, keepdims=True)
    own_square = jnp.sum((hidden - own_mean) * (hidden - own_mean), axis=1, keepdims=True)
    low = lax.broadcasted_iota(jnp.int32, (ty, 128), 1) < 64
    norm_stat[piece] = jnp.where(low, own_mean, own_square)
    for o in range(1, pieces):
        to = (piece + o) % pieces
        send(
            norm_stat.at[piece],
            norm_stat.at[piece],
            norm_send.at[o],
            norm_recv.at[piece],
            at_v(vocab_of(to // NC, y, to % NC)),
        )
    for o in range(1, pieces):
        frm = (piece + o) % pieces
        arrived(norm_stat.at[frm], norm_recv.at[frm])
    means = [norm_stat[i, :, 0:1] for i in range(pieces)]
    squares = [norm_stat[i, :, 64:65] for i in range(pieces)]
    mean = sum(means) * (1.0 / pieces)
    square = sum(squares) + width * sum((m - mean) * (m - mean) for m in means)
    scale = lax.rsqrt(square * (1.0 / d) + EPSILON)
    gain = jnp.concatenate([gains[1:2, pl.ds(start, size)] for start, size in own_cols], axis=1)
    final = ((hidden - mean) * scale * gain).astype(BF16)
    at = 0
    for start, size in own_cols:
        rows[z, g, y, :, pl.ds(start, size)] = final[:, at : at + size]
        at += size

    def cols_all(c_):
        base = pl.multiple_of(c_ * (d // NC), 128)
        return (
            pl.ds(base, nxl * wa),
            pl.ds(pl.multiple_of(base + nxl * wa, 128), nxl * wb),
            pl.ds(pl.multiple_of(base + nxl * (wa + wb), 128), nxl * wc),
        )

    def cols_piece(xl_):
        return [pl.ds(pl.multiple_of(start, 128), size) for start, size in columns_of(xl_, c)]

    own_a, own_b, own_c = cols_piece(xl)
    all_a, all_b, all_c = cols_all(c)

    def exchange(n, me, ref_of, send_sems, recv_sems, device_of):
        for o in range(1, n):
            ref = ref_of(me)
            send(ref, ref, send_sems.at[o], recv_sems.at[me], device_of((me + o) % n))

    def collect(n, me, ref_of, recv_sems, then=None):
        for o in range(1, n):
            frm = (me + o) % n
            arrived(ref_of(frm), recv_sems.at[frm])
            if then is not None:
                then(frm)

    def a1(x_):
        return rows.at[z, x_ // nxl, y, :, cols_piece(x_ % nxl)[0]]

    def b1(z_):
        return rows.at[z_, g, y, :, own_b]

    def c1(z_):
        return rows.at[z_, g, y, :, own_c]

    def a2(y_):
        return rows.at[z, :, y_, :, all_a]

    def b2(x_):
        return rows.at[:, x_ // nxl, y, :, cols_piece(x_ % nxl)[1]]

    def c2(y_):
        return rows.at[:, g, y_, :, own_c]

    def b3(y_):
        return rows.at[:, :, y_, :, all_b]

    def c3(x_):
        return rows.at[:, x_ // nxl, :, :, cols_piece(x_ % nxl)[2]]

    def a3(z_):
        return rows.at[z_, :, :, :, all_a]

    exchange(nx, x, a1, first_send.at[0], first_recv.at[0], at_x)
    exchange(nz, z, b1, first_send.at[1], first_recv.at[1], at_z)
    exchange(nz, z, c1, first_send.at[2], first_recv.at[2], at_z)
    collect(nx, x, a1, first_recv.at[0])
    exchange(ny, y, a2, second_send.at[0], second_recv.at[0], at_y)
    collect(nz, z, b1, first_recv.at[1])
    exchange(nx, x, b2, second_send.at[1], second_recv.at[1], at_x)
    collect(nz, z, c1, first_recv.at[2])
    exchange(ny, y, c2, second_send.at[2], second_recv.at[2], at_y)

    sibling = at_x(x, 1 - c)

    def to_core(kind, i, ref):
        send(ref, ref, core_send.at[kind, i], core_recv.at[kind, i], sibling)

    def a_block(c_):
        return lambda z_: rows.at[z_, :, :, :, cols_all(c_)[0]]

    def b_block(c_):
        return lambda y_: rows.at[:, :, y_, :, cols_all(c_)[1]]

    def c_block(c_):
        def view(x_):
            base = pl.multiple_of(c_ * (d // NC) + nxl * (wa + wb) + (x_ % nxl) * wc, 128)
            return rows.at[:, x_ // nxl, :, :, pl.ds(base, wc)]

        return view

    def share(kind, view):
        return lambda i: to_core(kind, i, view(c)(i))

    share_a, share_b, share_c = share(0, a_block), share(1, b_block), share(2, c_block)

    collect(ny, y, a2, second_recv.at[0])
    exchange(nz, z, a3, ring_send, ring_recv, at_z)
    share_a(z)
    collect(nx, x, b2, second_recv.at[1])
    exchange(ny, y, b3, third_send.at[0], third_recv.at[0], at_y)
    share_b(y)
    collect(ny, y, c2, second_recv.at[2])
    exchange(nx, x, c3, third_send.at[1], third_recv.at[1], at_x)
    share_c(x)
    collect(ny, y, b3, third_recv.at[0], share_b)
    collect(nz, z, a3, ring_recv, share_a)
    collect(nx, x, c3, third_recv.at[1], share_c)
    for kind, count, view in ((0, nz, a_block), (1, ny, b_block), (2, nx, c_block)):
        for i in range(count):
            arrived(view(1 - c)(i), core_recv.at[kind, i])

    loads[6].wait()
    loads[8].wait()
    table_base = ((v * nz + z) * ng + g) * table_rows
    step_blocks = max(1, 256 // tz)
    step_rows = step_blocks * tz

    def logit_step(i, carry):
        chunk = rows[pl.ds(i * step_blocks, step_blocks)].reshape(step_rows, d)
        lanes = pl.ds(pl.multiple_of(i * step_rows, 128), step_rows)
        values = lax.dot_general(emb[...], chunk, NT, preferred_element_type=F32)
        logit[:, lanes] = values
        top_ = jnp.max(values, axis=0, keepdims=True)
        total_ = jnp.sum(jnp.exp(values - top_), axis=0, keepdims=True)
        token = table_base + lax.broadcasted_iota(jnp.int32, values.shape, 0)
        local_stat[i, 0:1, :] = top_ + jnp.log(total_)
        local_stat[i, 1:2, :] = jnp.sum(jnp.where(token == labels[:, lanes], values, 0.0), axis=0, keepdims=True)
        return carry

    steps = nz // step_blocks
    lax.fori_loop(0, steps, logit_step, 0)

    stat_rows = nz * tz // 128
    per_step = step_rows // 128
    nxc = nx * NC
    xc = x * NC + c
    for r in range(stat_rows):
        for k in range(2):
            stat_x[xc, k * stat_rows + r : k * stat_rows + r + 1, :] = local_stat[
                r // per_step, k : k + 1, (r % per_step) * 128 : (r % per_step + 1) * 128
            ]

    def merge(ref, n):
        lses = [ref[i, 0:stat_rows] for i in range(n)]
        top_ = functools.reduce(jnp.maximum, lses)
        total_ = sum(jnp.exp(s - top_) for s in lses)
        return top_ + jnp.log(total_), sum(ref[i, stat_rows : 2 * stat_rows] for i in range(n))

    def stat_round(ref, n, me, k, device_of):
        exchange(n, me, lambda i: ref.at[i], stat_send.at[k], stat_recv.at[k], device_of)
        collect(n, me, lambda i: ref.at[i], stat_recv.at[k])
        return merge(ref, n)

    lse, picked = stat_round(stat_x, nxc, xc, 0, lambda i: at_x(i // NC, i % NC))
    stat_y[y, 0:stat_rows] = lse
    stat_y[y, stat_rows : 2 * stat_rows] = picked
    lse, picked = stat_round(stat_y, ny, y, 1, at_y)
    stat_z[z, 0:stat_rows] = lse
    stat_z[z, stat_rows : 2 * stat_rows] = picked
    lse, picked = stat_round(stat_z, nz, z, 2, at_z)

    place = lax.broadcasted_iota(jnp.int32, lse.shape, 0) * 128 + lax.broadcasted_iota(jnp.int32, lse.shape, 1)
    live = place < tgt_len[0]
    loss_out[...] = jnp.where(live, lse - picked, 0.0)
    lse = jnp.where(live, lse, 1e30)
    lse = jnp.concatenate([lse[r : r + 1, :] for r in range(stat_rows)], axis=1)
    place = lax.broadcasted_iota(jnp.int32, labels.shape, 1)
    hit = jnp.where(place < tgt_len[0], labels[...] - table_base, -1)

    def grad_step(i, carry):
        some = pl.ds(i * 128, 128)
        token = i * 128 + lax.broadcasted_iota(jnp.int32, (128, nz * tz), 0)
        grad[some, :] = (jnp.exp(logit[some, :] - lse) - jnp.where(token == hit, 1.0, 0.0)).astype(BF16)
        return carry

    lax.fori_loop(0, table_rows // 128, grad_step, 0)

    for copy in sent:
        copy.wait_send()


def grad_kernel(grad, rows, out):
    cols = pl.ds(pl.multiple_of(pl.program_id(0) * out.shape[1], 128), out.shape[1])
    chunk = rows[:, :, :, :, cols].reshape(grad.shape[1], out.shape[1])
    out[...] = jnp.dot(grad[...], chunk, preferred_element_type=F32).astype(BF16)


def body(
    cfg,
    decoder_states,
    encoder_states,
    ln_gains,
    w_query,
    w_key,
    w_value,
    w_out,
    embedding,
    labels,
    src_length,
    tgt_length,
):
    nv, nz, ng, ny, nxl = cfg
    tz, d = decoder_states.shape
    ez = encoder_states.shape[0]
    hd = w_query.shape[1]
    table_rows = embedding.shape[0]
    target = labels.shape[0]
    tg = tz // ng
    ty = tg // ny
    width = d // (nxl * NC)
    nx = ng * nxl
    half = nz // 2
    pieces = nxl * NC
    step_blocks = max(1, 256 // tz)
    stat_rows = target // 128
    most = max(nz, nx, ny)
    hbm = pl.BlockSpec(memory_space=pl.ANY)
    vmem = pl.BlockSpec(memory_space=pltpu.VMEM)
    smem = pl.BlockSpec(memory_space=pltpu.SMEM)
    dma = pltpu.SemaphoreType.DMA
    far = [
        pltpu.with_memory_space_constraint(array, pltpu.HBM)
        for array in (
            decoder_states,
            encoder_states,
            ln_gains,
            labels.reshape(1, target),
            w_query,
            w_key,
            w_value,
            w_out,
            embedding,
        )
    ]
    loss, grad, rows = pl.pallas_call(
        functools.partial(front_kernel, cfg),
        out_shape=(
            jax.ShapeDtypeStruct((stat_rows, 128), F32),
            pltpu.VMEM((table_rows, target), BF16),
            pltpu.VMEM((nz, ng, ny, ty, d), BF16),
        ),
        in_specs=[smem, smem] + [hbm] * len(far),
        out_specs=(vmem, vmem, vmem),
        scratch_shapes=[
            pltpu.VMEM(ln_gains.shape, F32),
            pltpu.VMEM((1, target), jnp.int32),
            pltpu.VMEM((tz, d), BF16),
            pltpu.VMEM((ez, d), BF16),
            pltpu.VMEM((d, hd), BF16),
            pltpu.VMEM((d, 2 * hd), BF16),
            pltpu.VMEM((hd, d), BF16),
            pltpu.VMEM((table_rows, d), BF16),
            pltpu.VMEM((nz, 2, ez, hd), BF16),
            pltpu.VMEM((tz, hd + 128), F32),
            pltpu.VMEM((tg, hd + 128), F32),
            pltpu.VMEM((nv, ty, width), F32),
            pltpu.VMEM((nv, ty, width), F32),
            pltpu.VMEM((pieces, ty, 128), F32),
            pltpu.VMEM((table_rows, target), F32),
            pltpu.VMEM((nz // step_blocks, 8, step_blocks * tz), F32),
            pltpu.VMEM((nx * NC, 2 * stat_rows, 128), F32),
            pltpu.VMEM((ny, 2 * stat_rows, 128), F32),
            pltpu.VMEM((nz, 2 * stat_rows, 128), F32),
            dma((9,)),
            dma((2, half, 2)),
            dma((2, half, 2)),
            dma((2,)),
            dma((nv,)),
            dma((nv,)),
            dma((pieces,)),
            dma((pieces,)),
            dma((3, most)),
            dma((3, most)),
            dma((3, most)),
            dma((3, most)),
            dma((nz,)),
            dma((nz,)),
            dma((2, most)),
            dma((2, most)),
            dma((3, most)),
            dma((3, most)),
            dma((3, max(most, nx * NC))),
            dma((3, max(most, nx * NC))),
        ],
        compiler_params=pltpu.CompilerParams(
            collective_id=0, has_side_effects=True, vmem_limit_bytes=40 * 1024 * 1024
        ),
    )(src_length, tgt_length, *far)
    block = 512
    grad_table = pl.pallas_call(
        grad_kernel,
        out_shape=jax.ShapeDtypeStruct((table_rows, d), BF16),
        grid=(d // block,),
        in_specs=[vmem, vmem],
        out_specs=pl.BlockSpec((table_rows, block), lambda i: (0, i)),
        compiler_params=pltpu.CompilerParams(vmem_limit_bytes=24 * 1024 * 1024),
    )(*(pltpu.with_memory_space_constraint(array, pltpu.VMEM) for array in (grad, rows)))
    return (loss.reshape(target), grad_table)


def solution(mesh):
    nv, nz, ng = mesh.shape["vocab"], mesh.shape["seq"], mesh.shape["grp"]
    cfg = (nv, nz, ng, NY, nv // (NY * NC))
    in_specs = (
        P("seq", None),
        P(("seq", "grp"), None),
        P(),
        P(None, "vocab"),
        P(None, "vocab"),
        P(None, "vocab"),
        P("vocab", None),
        P(("vocab", "seq", "grp"), None),
        P(),
        P(),
        P(),
    )
    out_specs = (P(), P(("vocab", "seq", "grp"), None))
    return jax.shard_map(
        functools.partial(body, cfg), mesh=mesh, in_specs=in_specs, out_specs=out_specs, check_vma=False
    )
```

```python
import functools
import math

import jax
import jax.numpy as jnp
from jax import lax
from jax.experimental import pallas as pl
from jax.experimental.pallas import tpu as pltpu
from jax.sharding import PartitionSpec as P

HEAD_DIM = 128
EPSILON = 1e-05
MESH = pl.DeviceIdType.MESH
NC = 2
NY = 4
NT = (((1,), (1,)), ((), ()))
F32, BF16 = jnp.float32, jnp.bfloat16


def front_kernel(
    cfg,
    src_len,
    tgt_len,
    dec_in,
    enc_in,
    gains_in,
    labels_in,
    wq_in,
    wk_in,
    wv_in,
    wo_in,
    emb_in,
    loss_out,
    grad_out,
    rows_out,
    gains,
    labels,
    dec,
    enc,
    wq,
    wkv,
    wo,
    emb,
    kv,
    ctx_own,
    ctx_got,
    part,
    summed,
    norm_stat,
    rows,
    logit,
    grad,
    local_stat,
    stat_x,
    stat_y,
    stat_z,
    load_sem,
    store_sem,
    kv_recv,
    a_recv,
    b_recv,
    c_recv,
    send_sem,
    recv_sem,
):
    nv, nz, ng, ny, nxl = cfg
    d = dec.shape[1]
    tz = dec.shape[0]
    ez = enc.shape[0]
    hd = wq.shape[1]
    tg = tz // ng
    ty = tg // ny
    width = d // (nxl * NC)
    wa, wb, wc = width // 4, width // 4, width // 2
    table_rows = emb.shape[0]
    nx = ng * nxl
    half = nz // 2

    v = lax.axis_index("vocab")
    z = lax.axis_index("seq")
    g = lax.axis_index("grp")
    c = v % NC
    y = (v // NC) % ny
    xl = v // (NC * ny)
    x = g * nxl + xl

    def vocab_of(xl_, y_, c_):
        return (xl_ * ny + y_) * NC + c_

    def at_x(x_, c_=None):
        return {"vocab": vocab_of(x_ % nxl, y, c if c_ is None else c_), "seq": z, "grp": x_ // nxl}

    def at_y(y_):
        return {"vocab": vocab_of(xl, y_, c), "seq": z, "grp": g}

    def at_z(z_):
        return {"vocab": v, "seq": z_, "grp": g}

    def at_v(v_):
        return {"vocab": v_, "seq": z, "grp": g}

    barrier = pltpu.get_barrier_semaphore()
    friends = [at_v((v + o) % nv) for o in range(1, nv)]
    friends += [at_z((z + o) % nz) for o in range(1, nz)]
    friends += [
        {"vocab": vocab_of(xl_, y, c_), "seq": z, "grp": (g + o) % ng}
        for o in range(1, ng)
        for xl_ in range(nxl)
        for c_ in range(NC)
    ]
    for friend in friends:
        pl.semaphore_signal(barrier, inc=1, device_id=friend, device_id_type=MESH)

    loads = [
        pltpu.make_async_copy(src, dst, load_sem.at[i])
        for i, (src, dst) in enumerate(
            (
                (enc_in, enc),
                (wk_in, wkv.at[:, 0:hd]),
                (wv_in, wkv.at[:, hd : 2 * hd]),
                (dec_in, dec),
                (gains_in, gains),
                (wq_in, wq),
                (wo_in, wo),
                (labels_in, labels),
                (emb_in, emb),
            )
        )
    ]
    for load in loads[:6]:
        load.start()

    def remote(src, dst, out_sem, in_sem, device):
        return pltpu.make_async_remote_copy(
            src_ref=src, dst_ref=dst, send_sem=out_sem, recv_sem=in_sem, device_id=device, device_id_type=MESH
        )

    def arrived(ref, in_sem):
        remote(ref, ref, send_sem.at[0], in_sem, at_z((z + 1) % nz)).wait_recv()

    def left(ref, out_sem):
        remote(ref, ref, out_sem, recv_sem.at[0], at_z((z + 1) % nz)).wait_send()

    for load in loads[:3]:
        load.wait()
    for load in loads[6:]:
        load.start()
    own_kv = jnp.dot(enc[...], wkv[...], preferred_element_type=F32).astype(BF16)
    kv[z, 0] = own_kv[:, 0:hd]
    kv[z, 1] = own_kv[:, hd : 2 * hd]

    loads[3].wait()
    loads[4].wait()
    states = dec[...].astype(F32)
    centred = states - jnp.mean(states, axis=1, keepdims=True)
    variance = jnp.mean(centred * centred, axis=1, keepdims=True)
    normed = (centred * lax.rsqrt(variance + EPSILON) * gains[0:1, :]).astype(BF16)
    loads[5].wait()
    query = (jnp.dot(normed, wq[...], preferred_element_type=F32) * (1.0 / math.sqrt(hd))).astype(BF16)

    pl.semaphore_wait(barrier, len(friends))

    def kv_post(way, t, part_):
        step = (1, nz - 1)[way]
        ref = kv.at[(z + t * (nz - step)) % nz, part_]
        remote(ref, ref, send_sem.at[0], kv_recv.at[way, t, part_], at_z((z + step) % nz)).start()

    for part_ in (0, 1):
        for way in (0, 1):
            if half > 1 or part_ == way:
                kv_post(way, 0, part_)

    source_count = src_len[0]

    def scores_of(block):
        s = lax.dot_general(query, kv[block, 0], NT, preferred_element_type=F32)
        place = (block * ng + g) * ez + lax.broadcasted_iota(jnp.int32, s.shape, 1)
        valid = place < source_count
        return block, valid, jnp.where(valid, s, -1e30)

    scored = [scores_of(z)]
    for t in range(1, half + 1):
        for part_ in (0, 1):
            for way in (0, 1):
                if t < half or part_ == way:
                    arrived(kv.at[(z + t * (nz - (1, nz - 1)[way])) % nz, part_], kv_recv.at[way, t - 1, part_])
                if t + 1 < half or (t + 1 == half and part_ == way):
                    kv_post(way, t, part_)
        scored += [scores_of((z + o) % nz) for o in ((nz - t, t) if t < half else (half,))]
    top = functools.reduce(jnp.maximum, [s for _, _, s in scored])
    top = jnp.max(top, axis=1, keepdims=True)
    total = jnp.zeros((tz, ez), F32)
    acc = jnp.zeros((tz, hd), F32)
    for block, valid, s in scored:
        e = jnp.where(valid, jnp.exp(s - top), 0.0)
        total = total + e
        acc = acc + jnp.dot(e.astype(BF16), kv[block, 1], preferred_element_type=F32)
    total = jnp.sum(total, axis=1, keepdims=True)
    low = lax.broadcasted_iota(jnp.int32, (tz, 128), 1) < 64
    ctx_own[:, 0:hd] = acc
    ctx_own[:, hd : hd + 128] = jnp.where(low, top, total)
    remote(
        ctx_own.at[pl.ds(pl.multiple_of((1 - g) * tg, tg), tg)],
        ctx_got,
        send_sem.at[1],
        recv_sem.at[1],
        {"vocab": v, "seq": z, "grp": 1 - g},
    ).start()
    arrived(ctx_got, recv_sem.at[1])
    mine = ctx_own[pl.ds(pl.multiple_of(g * tg, tg), tg), :]
    other = ctx_got[...]
    top0, top1 = mine[:, hd : hd + 1], other[:, hd : hd + 1]
    both = jnp.maximum(top0, top1)
    f0, f1 = jnp.exp(top0 - both), jnp.exp(top1 - both)
    total = mine[:, hd + 64 : hd + 65] * f0 + other[:, hd + 64 : hd + 65] * f1
    context = ((mine[:, 0:hd] * f0 + other[:, 0:hd] * f1) / total).astype(BF16)

    def columns_of(xl_, c_):
        base = c_ * (d // NC)
        return (
            (base + xl_ * wa, wa),
            (base + nxl * wa + xl_ * wb, wb),
            (base + nxl * (wa + wb) + xl_ * wc, wc),
        )

    loads[6].wait()
    projected = jnp.dot(context, wo[...], preferred_element_type=F32)
    for xl_ in range(nxl):
        for y_ in range(ny):
            for c_ in range(NC):
                at = 0
                for start, size in columns_of(xl_, c_):
                    part[vocab_of(xl_, y_, c_), :, at : at + size] = projected[
                        y_ * ty : (y_ + 1) * ty, start : start + size
                    ]
                    at += size
    for o in range(1, nv):
        to = (v + o) % nv
        remote(part.at[to], summed.at[v], send_sem.at[2], recv_sem.at[2], at_v(to)).start()
    own_cols = [(pl.multiple_of(start, 128), size) for start, size in columns_of(xl, c)]
    own_row = pl.multiple_of(g * tg + y * ty, ty)
    hidden = part[v] + jnp.concatenate(
        [dec[pl.ds(own_row, ty), pl.ds(start, size)].astype(F32) for start, size in own_cols], axis=1
    )
    arrived(summed.at[0 : nv - 1], recv_sem.at[2])
    for o in range(1, nv):
        hidden = hidden + summed[(v + o) % nv]

    piece = xl * NC + c
    pieces = nxl * NC
    own_mean = jnp.mean(hidden, axis=1, keepdims=True)
    own_square = jnp.sum((hidden - own_mean) * (hidden - own_mean), axis=1, keepdims=True)
    low = lax.broadcasted_iota(jnp.int32, (ty, 128), 1) < 64
    norm_stat[piece] = jnp.where(low, own_mean, own_square)
    for o in range(1, pieces):
        to = (piece + o) % pieces
        remote(
            norm_stat.at[piece],
            norm_stat.at[piece],
            send_sem.at[3],
            recv_sem.at[3],
            at_v(vocab_of(to // NC, y, to % NC)),
        ).start()
    arrived(norm_stat.at[0 : pieces - 1], recv_sem.at[3])
    means = [norm_stat[i, :, 0:1] for i in range(pieces)]
    squares = [norm_stat[i, :, 64:65] for i in range(pieces)]
    mean = sum(means) * (1.0 / pieces)
    square = sum(squares) + width * sum((m - mean) * (m - mean) for m in means)
    scale = lax.rsqrt(square * (1.0 / d) + EPSILON)
    gain = jnp.concatenate([gains[1:2, pl.ds(start, size)] for start, size in own_cols], axis=1)
    final = ((hidden - mean) * scale * gain).astype(BF16)
    at = 0
    for start, size in own_cols:
        rows[z, g, y, :, pl.ds(start, size)] = final[:, at : at + size]
        at += size

    def cols_all(c_):
        base = pl.multiple_of(c_ * (d // NC), 128)
        return (
            pl.ds(base, nxl * wa),
            pl.ds(pl.multiple_of(base + nxl * wa, 128), nxl * wb),
            pl.ds(pl.multiple_of(base + nxl * (wa + wb), 128), nxl * wc),
        )

    def cols_piece(xl_):
        return [pl.ds(pl.multiple_of(start, 128), size) for start, size in columns_of(xl_, c)]

    own_a, own_b, own_c = cols_piece(xl)
    all_a, all_b, all_c = cols_all(c)

    def exchange(n, me, ref_of, out_sem, in_sem, device_of):
        ref = ref_of(me)
        for o in range(1, n):
            remote(ref, ref, out_sem, in_sem, device_of((me + o) % n)).start()

    def a1(x_):
        return rows.at[z, x_ // nxl, y, :, cols_piece(x_ % nxl)[0]]

    def b1(z_):
        return rows.at[z_, g, y, :, own_b]

    def c1(z_):
        return rows.at[z_, g, y, :, own_c]

    def a2(y_):
        return rows.at[z, :, y_, :, all_a]

    def b2(x_):
        return rows.at[:, x_ // nxl, y, :, cols_piece(x_ % nxl)[1]]

    def c2(y_):
        return rows.at[:, g, y_, :, own_c]

    def b3(y_):
        return rows.at[:, :, y_, :, all_b]

    def c3(x_):
        return rows.at[:, x_ // nxl, :, :, cols_piece(x_ % nxl)[2]]

    def a3(z_):
        return rows.at[z_, :, :, :, all_a]

    all_a1 = rows.at[0, 0, 0 : nx - 1, :, 0:wa]
    all_b1 = rows.at[0 : nz - 1, 0, 0, :, 0:wb]
    all_c1 = rows.at[0 : nz - 1, 0, 0, :, 0:wc]
    all_a2 = rows.at[0, :, 0 : ny - 1, :, 0 : nxl * wa]
    all_b2 = rows.at[:, 0, 0 : nx - 1, :, 0:wb]
    all_c2 = rows.at[:, 0, 0 : ny - 1, :, 0:wc]
    all_a3 = rows.at[0 : nz - 1, :, :, :, 0 : nxl * wa]
    all_b3 = rows.at[:, :, 0 : ny - 1, :, 0 : nxl * wb]
    all_c3 = rows.at[:, 0, :, :, 0 : (nx - 1) * wc]

    exchange(nx, x, a1, send_sem.at[4], recv_sem.at[4], at_x)
    exchange(nz, z, c1, send_sem.at[6], recv_sem.at[6], at_z)
    exchange(nz, z, b1, send_sem.at[5], recv_sem.at[5], at_z)
    arrived(all_a1, recv_sem.at[4])
    exchange(ny, y, a2, send_sem.at[7], recv_sem.at[7], at_y)
    arrived(all_c1, recv_sem.at[6])
    exchange(ny, y, c2, send_sem.at[9], recv_sem.at[9], at_y)
    arrived(all_b1, recv_sem.at[5])
    exchange(nx, x, b2, send_sem.at[8], recv_sem.at[8], at_x)

    sibling = at_x(x, 1 - c)

    def a_block(z_):
        return rows.at[z_, :, :, :, all_a]

    def b_block(y_):
        return rows.at[:, :, y_, :, all_b]

    def c_block(x_):
        base = pl.multiple_of(c * (d // NC) + nxl * (wa + wb) + (x_ % nxl) * wc, 128)
        return rows.at[:, x_ // nxl, :, :, pl.ds(base, wc)]

    def share(kind, ref):
        remote(ref, ref, send_sem.at[13 + kind], recv_sem.at[10 + kind], sibling).start()

    arrived(all_a2, recv_sem.at[7])
    ref = a3(z)
    for o in range(1, nz):
        remote(ref, ref, send_sem.at[10], a_recv.at[z], at_z((z + o) % nz)).start()
    share(0, a_block(z))
    arrived(all_c2, recv_sem.at[9])
    ref = c3(x)
    for o in range(1, nx):
        remote(ref, ref, send_sem.at[12], c_recv.at[x], at_x((x + o) % nx)).start()
    share(2, c_block(x))
    arrived(all_b2, recv_sem.at[8])
    ref = b3(y)
    for o in range(1, ny):
        remote(ref, ref, send_sem.at[11], b_recv.at[y], at_y((y + o) % ny)).start()
    share(1, b_block(y))
    for o in range(1, ny):
        frm = (y + o) % ny
        arrived(b3(frm), b_recv.at[frm])
        share(1, b_block(frm))
    for o in range(1, nz):
        frm = (z + o) % nz
        arrived(a3(frm), a_recv.at[frm])
        share(0, a_block(frm))
    their_a, their_b, their_c = cols_all(1 - c)
    arrived(rows.at[:, :, :, :, their_a], recv_sem.at[10])
    arrived(rows.at[:, :, :, :, their_b], recv_sem.at[11])
    loads[7].wait()
    loads[8].wait()
    table_base = ((v * nz + z) * ng + g) * table_rows
    step_blocks = max(1, 256 // tz)
    step_rows = step_blocks * tz
    early = nxl * (wa + wb)

    def logits_of(i, starts, size):
        total_ = None
        for start in starts:
            chunk = rows[pl.ds(i * step_blocks, step_blocks), :, :, :, start : start + size].reshape(step_rows, size)
            values = lax.dot_general(emb[:, start : start + size], chunk, NT, preferred_element_type=F32)
            total_ = values if total_ is None else total_ + values
        return total_

    def lanes_of(i):
        return pl.ds(pl.multiple_of(i * step_rows, 128), step_rows)

    def early_step(i, carry):
        logit[:, lanes_of(i)] = logits_of(i, range(0, d, d // NC), early)
        return carry

    steps = nz // step_blocks
    for o in range(1, nx):
        frm = (x + o) % nx
        arrived(c3(frm), c_recv.at[frm])
        share(2, c_block(frm))
    lax.fori_loop(0, steps, early_step, 0)
    arrived(rows.at[:, :, :, :, their_c], recv_sem.at[12])
    rows_store = pltpu.make_async_copy(rows, rows_out, store_sem.at[0])
    rows_store.start()

    def logit_step(i, carry):
        lanes = lanes_of(i)
        values = logit[:, lanes] + logits_of(i, range(early, d, d // NC), d // NC - early)
        logit[:, lanes] = values
        top_ = jnp.max(values, axis=0, keepdims=True)
        total_ = jnp.sum(jnp.exp(values - top_), axis=0, keepdims=True)
        token = table_base + lax.broadcasted_iota(jnp.int32, values.shape, 0)
        local_stat[i, 0:1, :] = top_ + jnp.log(total_)
        local_stat[i, 1:2, :] = jnp.sum(jnp.where(token == labels[:, lanes], values, 0.0), axis=0, keepdims=True)
        return carry

    lax.fori_loop(0, steps, logit_step, 0)
    stat_rows = nz * tz // 128
    per_step = step_rows // 128
    nxc = nx * NC
    xc = x * NC + c
    for r in range(stat_rows):
        for k in range(2):
            stat_x[xc, k * stat_rows + r : k * stat_rows + r + 1, :] = local_stat[
                r // per_step, k : k + 1, (r % per_step) * 128 : (r % per_step + 1) * 128
            ]

    def merge(ref, n):
        lses = [ref[i, 0:stat_rows] for i in range(n)]
        top_ = functools.reduce(jnp.maximum, lses)
        total_ = sum(jnp.exp(s - top_) for s in lses)
        return top_ + jnp.log(total_), sum(ref[i, stat_rows : 2 * stat_rows] for i in range(n))

    def stat_round(ref, n, me, k, device_of):
        exchange(n, me, lambda i: ref.at[i], send_sem.at[16 + k], recv_sem.at[13 + k], device_of)
        arrived(ref.at[0 : n - 1], recv_sem.at[13 + k])
        return merge(ref, n)

    lse, picked = stat_round(stat_x, nxc, xc, 0, lambda i: at_x(i // NC, i % NC))
    stat_y[y, 0:stat_rows] = lse
    stat_y[y, stat_rows : 2 * stat_rows] = picked
    lse, picked = stat_round(stat_y, ny, y, 1, at_y)
    stat_z[z, 0:stat_rows] = lse
    stat_z[z, stat_rows : 2 * stat_rows] = picked
    lse, picked = stat_round(stat_z, nz, z, 2, at_z)

    place = lax.broadcasted_iota(jnp.int32, lse.shape, 0) * 128 + lax.broadcasted_iota(jnp.int32, lse.shape, 1)
    live = place < tgt_len[0]
    loss_out[...] = jnp.where(live, lse - picked, 0.0)
    lse = jnp.where(live, lse, 1e30)
    lse = jnp.concatenate([lse[r : r + 1, :] for r in range(stat_rows)], axis=1)
    place = lax.broadcasted_iota(jnp.int32, labels.shape, 1)
    hit = jnp.where(place < tgt_len[0], labels[...] - table_base, -1)

    def grad_step(i, carry):
        some = pl.ds(i * 128, 128)
        token = i * 128 + lax.broadcasted_iota(jnp.int32, (128, nz * tz), 0)
        grad[some, :] = (jnp.exp(logit[some, :] - lse) - jnp.where(token == hit, 1.0, 0.0)).astype(BF16)
        return carry

    lax.fori_loop(0, table_rows // 128, grad_step, 0)

    grad_store = pltpu.make_async_copy(grad, grad_out, store_sem.at[1])
    grad_store.start()
    for i, ref in enumerate(
        (
            kv.at[0 : nz - 1],
            ctx_got,
            part.at[0 : nv - 1],
            norm_stat.at[0 : pieces - 1],
            all_a1,
            all_b1,
            all_c1,
            all_a2,
            all_b2,
            all_c2,
            all_a3,
            all_b3,
            all_c3,
            rows.at[:, :, :, :, all_a],
            rows.at[:, :, :, :, all_b],
            rows.at[:, :, :, :, all_c],
            stat_x.at[0 : nxc - 1],
            stat_y.at[0 : ny - 1],
            stat_z.at[0 : nz - 1],
        )
    ):
        left(ref, send_sem.at[i])
    rows_store.wait()
    grad_store.wait()


def grad_kernel(grad, rows, out):
    cols = pl.ds(pl.multiple_of(pl.program_id(0) * out.shape[1], 128), out.shape[1])
    chunk = rows[:, :, :, :, cols].reshape(grad.shape[1], out.shape[1])
    out[...] = jnp.dot(grad[...], chunk, preferred_element_type=F32).astype(BF16)


def body(
    cfg,
    decoder_states,
    encoder_states,
    ln_gains,
    w_query,
    w_key,
    w_value,
    w_out,
    embedding,
    labels,
    src_length,
    tgt_length,
):
    nv, nz, ng, ny, nxl = cfg
    tz, d = decoder_states.shape
    ez = encoder_states.shape[0]
    hd = w_query.shape[1]
    table_rows = embedding.shape[0]
    target = labels.shape[0]
    tg = tz // ng
    ty = tg // ny
    width = d // (nxl * NC)
    nx = ng * nxl
    half = nz // 2
    pieces = nxl * NC
    step_blocks = max(1, 256 // tz)
    stat_rows = target // 128
    hbm = pl.BlockSpec(memory_space=pl.ANY)
    vmem = pl.BlockSpec(memory_space=pltpu.VMEM)
    smem = pl.BlockSpec(memory_space=pltpu.SMEM)
    dma = pltpu.SemaphoreType.DMA
    far = [
        pltpu.with_memory_space_constraint(array, pltpu.HBM)
        for array in (
            decoder_states,
            encoder_states,
            ln_gains,
            labels.reshape(1, target),
            w_query,
            w_key,
            w_value,
            w_out,
            embedding,
        )
    ]
    loss, grad, rows = pl.pallas_call(
        functools.partial(front_kernel, cfg),
        out_shape=(
            jax.ShapeDtypeStruct((stat_rows, 128), F32),
            pltpu.VMEM((table_rows, target), BF16),
            pltpu.VMEM((nz, ng, ny, ty, d), BF16),
        ),
        in_specs=[smem, smem] + [hbm] * len(far),
        out_specs=(vmem, hbm, hbm),
        scratch_shapes=[
            pltpu.VMEM(ln_gains.shape, F32),
            pltpu.VMEM((1, target), jnp.int32),
            pltpu.VMEM((tz, d), BF16),
            pltpu.VMEM((ez, d), BF16),
            pltpu.VMEM((d, hd), BF16),
            pltpu.VMEM((d, 2 * hd), BF16),
            pltpu.VMEM((hd, d), BF16),
            pltpu.VMEM((table_rows, d), BF16),
            pltpu.VMEM((nz, 2, ez, hd), BF16),
            pltpu.VMEM((tz, hd + 128), F32),
            pltpu.VMEM((tg, hd + 128), F32),
            pltpu.VMEM((nv, ty, width), F32),
            pltpu.VMEM((nv, ty, width), F32),
            pltpu.VMEM((pieces, ty, 128), F32),
            pltpu.VMEM((nz, ng, ny, ty, d), BF16),
            pltpu.VMEM((table_rows, target), F32),
            pltpu.VMEM((table_rows, target), BF16),
            pltpu.VMEM((nz // step_blocks, 8, step_blocks * tz), F32),
            pltpu.VMEM((nx * NC, 2 * stat_rows, 128), F32),
            pltpu.VMEM((ny, 2 * stat_rows, 128), F32),
            pltpu.VMEM((nz, 2 * stat_rows, 128), F32),
            dma((9,)),
            dma((2,)),
            dma((2, half, 2)),
            dma((nz,)),
            dma((ny,)),
            dma((nx,)),
            dma((19,)),
            dma((16,)),
        ],
        compiler_params=pltpu.CompilerParams(
            collective_id=0, has_side_effects=True, vmem_limit_bytes=40 * 1024 * 1024
        ),
    )(src_length, tgt_length, *far)
    block = 512
    grad_table = pl.pallas_call(
        grad_kernel,
        out_shape=jax.ShapeDtypeStruct((table_rows, d), BF16),
        grid=(d // block,),
        in_specs=[vmem, vmem],
        out_specs=pl.BlockSpec((table_rows, block), lambda i: (0, i)),
        compiler_params=pltpu.CompilerParams(vmem_limit_bytes=24 * 1024 * 1024),
    )(*(pltpu.with_memory_space_constraint(array, pltpu.VMEM) for array in (grad, rows)))
    return (loss.reshape(target), grad_table)


def solution(mesh):
    nv, nz, ng = mesh.shape["vocab"], mesh.shape["seq"], mesh.shape["grp"]
    cfg = (nv, nz, ng, NY, nv // (NY * NC))
    in_specs = (
        P("seq", None),
        P(("seq", "grp"), None),
        P(),
        P(None, "vocab"),
        P(None, "vocab"),
        P(None, "vocab"),
        P("vocab", None),
        P(("vocab", "seq", "grp"), None),
        P(),
        P(),
        P(),
    )
    out_specs = (P(), P(("vocab", "seq", "grp"), None))
    return jax.shard_map(
        functools.partial(body, cfg), mesh=mesh, in_specs=in_specs, out_specs=out_specs, check_vma=False
    )
```

```python
import functools
import math

import jax
import jax.numpy as jnp
from jax import lax
from jax.experimental import pallas as pl
from jax.experimental.pallas import tpu as pltpu
from jax.sharding import PartitionSpec as P

HEAD_DIM = 128
EPSILON = 1e-05
MESH = pl.DeviceIdType.MESH
NC = 2
NY = 4
NT = (((1,), (1,)), ((), ()))
F32, BF16 = jnp.float32, jnp.bfloat16


def front_kernel(
    cfg,
    src_len,
    tgt_len,
    dec_in,
    enc_in,
    gains_in,
    labels_in,
    wq_in,
    wk_in,
    wv_in,
    wo_in,
    emb_in,
    loss_out,
    grad_out,
    rows_out,
    gains,
    labels,
    dec,
    enc,
    wq,
    wkv,
    wo,
    emb,
    kv,
    ctx_own,
    ctx_got,
    part,
    summed,
    norm_stat,
    rows,
    logit,
    grad,
    local_stat,
    stat_x,
    stat_y,
    stat_z,
    load_sem,
    store_sem,
    kv_recv,
    a_recv,
    b_recv,
    c_recv,
    send_sem,
    recv_sem,
):
    nv, nz, ng, ny, nxl = cfg
    d = dec.shape[1]
    tz = dec.shape[0]
    ez = enc.shape[0]
    hd = wq.shape[1]
    tg = tz // ng
    ty = tg // ny
    width = d // (nxl * NC)
    wa, wb, wc = width // 4, width // 4, width // 2
    table_rows = emb.shape[0]
    nx = ng * nxl
    half = nz // 2

    v = lax.axis_index("vocab")
    z = lax.axis_index("seq")
    g = lax.axis_index("grp")
    c = v % NC
    y = (v // NC) % ny
    xl = v // (NC * ny)
    x = g * nxl + xl

    def vocab_of(xl_, y_, c_):
        return (xl_ * ny + y_) * NC + c_

    def at_x(x_, c_=None):
        return {"vocab": vocab_of(x_ % nxl, y, c if c_ is None else c_), "seq": z, "grp": x_ // nxl}

    def at_y(y_):
        return {"vocab": vocab_of(xl, y_, c), "seq": z, "grp": g}

    def at_z(z_):
        return {"vocab": v, "seq": z_, "grp": g}

    def at_v(v_):
        return {"vocab": v_, "seq": z, "grp": g}

    barrier = pltpu.get_barrier_semaphore()
    friends = [at_v((v + o) % nv) for o in range(1, nv)]
    friends += [at_z((z + o) % nz) for o in range(1, nz)]
    friends += [{"vocab": v_, "seq": z, "grp": (g + o) % ng} for o in range(1, ng) for v_ in range(nv)]
    for friend in friends:
        pl.semaphore_signal(barrier, inc=1, device_id=friend, device_id_type=MESH)

    loads = [
        pltpu.make_async_copy(src, dst, load_sem.at[i])
        for i, (src, dst) in enumerate(
            (
                (enc_in, enc),
                (wk_in, wkv.at[:, 0:hd]),
                (wv_in, wkv.at[:, hd : 2 * hd]),
                (dec_in, dec),
                (gains_in, gains),
                (wq_in, wq),
                (wo_in, wo),
                (labels_in, labels),
                (emb_in, emb),
            )
        )
    ]
    for load in loads[:6]:
        load.start()

    def remote(src, dst, out_sem, in_sem, device):
        return pltpu.make_async_remote_copy(
            src_ref=src, dst_ref=dst, send_sem=out_sem, recv_sem=in_sem, device_id=device, device_id_type=MESH
        )

    def arrived(ref, in_sem):
        remote(ref, ref, send_sem.at[0], in_sem, at_z((z + 1) % nz)).wait_recv()

    def left(ref, out_sem):
        remote(ref, ref, out_sem, recv_sem.at[0], at_z((z + 1) % nz)).wait_send()

    for load in loads[:3]:
        load.wait()
    for load in loads[6:]:
        load.start()
    own_kv = jnp.dot(enc[...], wkv[...], preferred_element_type=F32).astype(BF16)
    kv[z, 0] = own_kv[:, 0:hd]
    kv[z, 1] = own_kv[:, hd : 2 * hd]

    pl.semaphore_wait(barrier, len(friends))

    def kv_post(way, t, part_):
        step = (1, nz - 1)[way]
        ref = kv.at[(z + t * (nz - step)) % nz, part_]
        remote(ref, ref, send_sem.at[0], kv_recv.at[way, t, part_], at_z((z + step) % nz)).start()

    for part_ in (0, 1):
        for way in (0, 1):
            if half > 1 or part_ == way:
                kv_post(way, 0, part_)

    loads[3].wait()
    loads[4].wait()
    states = dec[...].astype(F32)
    centred = states - jnp.mean(states, axis=1, keepdims=True)
    variance = jnp.mean(centred * centred, axis=1, keepdims=True)
    normed = (centred * lax.rsqrt(variance + EPSILON) * gains[0:1, :]).astype(BF16)
    loads[5].wait()
    query = (jnp.dot(normed, wq[...], preferred_element_type=F32) * (1.0 / math.sqrt(hd))).astype(BF16)

    source_count = src_len[0]

    def scores_of(block):
        s = lax.dot_general(query, kv[block, 0], NT, preferred_element_type=F32)
        place = (block * ng + g) * ez + lax.broadcasted_iota(jnp.int32, s.shape, 1)
        valid = place < source_count
        return block, valid, jnp.where(valid, s, -1e30)

    scored = [scores_of(z)]
    for t in range(1, half + 1):
        for part_ in (0, 1):
            for way in (0, 1):
                if t < half or part_ == way:
                    arrived(kv.at[(z + t * (nz - (1, nz - 1)[way])) % nz, part_], kv_recv.at[way, t - 1, part_])
                if t + 1 < half or (t + 1 == half and part_ == way):
                    kv_post(way, t, part_)
        scored += [scores_of((z + o) % nz) for o in ((nz - t, t) if t < half else (half,))]
    top = functools.reduce(jnp.maximum, [s for _, _, s in scored])
    top = jnp.max(top, axis=1, keepdims=True)
    total = jnp.zeros((tz, ez), F32)
    acc = jnp.zeros((tz, hd), F32)
    for block, valid, s in scored:
        e = jnp.where(valid, jnp.exp(s - top), 0.0)
        total = total + e
        acc = acc + jnp.dot(e.astype(BF16), kv[block, 1], preferred_element_type=F32)
    total = jnp.sum(total, axis=1, keepdims=True)
    low = lax.broadcasted_iota(jnp.int32, (tz, 128), 1) < 64
    ctx_own[:, 0:hd] = acc
    ctx_own[:, hd : hd + 128] = jnp.where(low, top, total)
    remote(
        ctx_own.at[pl.ds(pl.multiple_of((1 - g) * tg, tg), tg)],
        ctx_got,
        send_sem.at[1],
        recv_sem.at[1],
        {"vocab": v, "seq": z, "grp": 1 - g},
    ).start()
    arrived(ctx_got, recv_sem.at[1])
    mine = ctx_own[pl.ds(pl.multiple_of(g * tg, tg), tg), :]
    other = ctx_got[...]
    top0, top1 = mine[:, hd : hd + 1], other[:, hd : hd + 1]
    both = jnp.maximum(top0, top1)
    f0, f1 = jnp.exp(top0 - both), jnp.exp(top1 - both)
    total = mine[:, hd + 64 : hd + 65] * f0 + other[:, hd + 64 : hd + 65] * f1
    context = ((mine[:, 0:hd] * f0 + other[:, 0:hd] * f1) / total).astype(BF16)

    def columns_of(xl_, c_):
        base = c_ * (d // NC)
        return (
            (base + xl_ * wa, wa),
            (base + nxl * wa + xl_ * wb, wb),
            (base + nxl * (wa + wb) + xl_ * wc, wc),
        )

    loads[6].wait()
    projected = jnp.dot(context, wo[...], preferred_element_type=F32).astype(BF16)
    for xl_ in range(nxl):
        for y_ in range(ny):
            for c_ in range(NC):
                at = 0
                for start, size in columns_of(xl_, c_):
                    part[vocab_of(xl_, y_, c_), :, at : at + size] = projected[
                        y_ * ty : (y_ + 1) * ty, start : start + size
                    ]
                    at += size
    for o in range(1, nv):
        to = (v + o) % nv
        remote(part.at[to], summed.at[v], send_sem.at[2], recv_sem.at[2], at_v(to)).start()
    own_cols = [(pl.multiple_of(start, 128), size) for start, size in columns_of(xl, c)]
    own_row = pl.multiple_of(g * tg + y * ty, ty)
    hidden = part[v].astype(F32) + jnp.concatenate(
        [dec[pl.ds(own_row, ty), pl.ds(start, size)].astype(F32) for start, size in own_cols], axis=1
    )
    arrived(summed.at[0 : nv - 1], recv_sem.at[2])
    for o in range(1, nv):
        hidden = hidden + summed[(v + o) % nv].astype(F32)

    piece = xl * NC + c
    pieces = nxl * NC
    own_mean = jnp.mean(hidden, axis=1, keepdims=True)
    own_square = jnp.sum((hidden - own_mean) * (hidden - own_mean), axis=1, keepdims=True)
    low = lax.broadcasted_iota(jnp.int32, (ty, 128), 1) < 64
    norm_stat[piece] = jnp.where(low, own_mean, own_square)
    for o in range(1, pieces):
        to = (piece + o) % pieces
        remote(
            norm_stat.at[piece],
            norm_stat.at[piece],
            send_sem.at[3],
            recv_sem.at[3],
            at_v(vocab_of(to // NC, y, to % NC)),
        ).start()
    arrived(norm_stat.at[0 : pieces - 1], recv_sem.at[3])
    means = [norm_stat[i, :, 0:1] for i in range(pieces)]
    squares = [norm_stat[i, :, 64:65] for i in range(pieces)]
    mean = sum(means) * (1.0 / pieces)
    square = sum(squares) + width * sum((m - mean) * (m - mean) for m in means)
    scale = lax.rsqrt(square * (1.0 / d) + EPSILON)
    gain = jnp.concatenate([gains[1:2, pl.ds(start, size)] for start, size in own_cols], axis=1)
    final = ((hidden - mean) * scale * gain).astype(BF16)
    at = 0
    for start, size in own_cols:
        rows[z, g, y, :, pl.ds(start, size)] = final[:, at : at + size]
        at += size

    def cols_all(c_):
        base = pl.multiple_of(c_ * (d // NC), 128)
        return (
            pl.ds(base, nxl * wa),
            pl.ds(pl.multiple_of(base + nxl * wa, 128), nxl * wb),
            pl.ds(pl.multiple_of(base + nxl * (wa + wb), 128), nxl * wc),
        )

    def cols_piece(xl_):
        return [pl.ds(pl.multiple_of(start, 128), size) for start, size in columns_of(xl_, c)]

    _, own_b, own_c = cols_piece(xl)
    all_a, all_b, all_c = cols_all(c)

    def exchange(n, me, ref_of, out_sem, in_sem, device_of):
        ref = ref_of(me)
        for o in range(1, n):
            remote(ref, ref, out_sem, in_sem, device_of((me + o) % n)).start()

    swap = c

    def pick(here, there):
        return here + swap * (there - here)

    def place_b(i):
        return pick(x, i), pick(i, y)

    def place_c(i):
        return pick(i, x), pick(y, i)

    def at_xy(xy):
        return {"vocab": vocab_of(xy[0] % nxl, xy[1], c), "seq": z, "grp": xy[0] // nxl}

    def a1(xy):
        return rows.at[z, xy[0] // nxl, xy[1], :, cols_piece(xy[0] % nxl)[0]]

    def b1(z_):
        return rows.at[z_, g, y, :, own_b]

    def c1(z_):
        return rows.at[z_, g, y, :, own_c]

    def b2(xy):
        return rows.at[:, xy[0] // nxl, xy[1], :, cols_piece(xy[0] % nxl)[1]]

    def c2(xy):
        return rows.at[:, xy[0] // nxl, xy[1], :, cols_piece(xy[0] % nxl)[2]]

    def along_x(kind, x_):
        return rows.at[:, x_ // nxl, :, :, cols_piece(x_ % nxl)[kind]]

    def along_y(kind, y_):
        return rows.at[:, :, y_, :, cols_all(c)[kind]]

    all_a1 = rows.at[0, 0, 0, :, 0 : (nx * ny - 1) * wa]
    all_b1 = rows.at[0 : nz - 1, 0, 0, :, 0:wb]
    all_c1 = rows.at[0 : nz - 1, 0, 0, :, 0:wc]
    all_b2 = rows.at[:, 0, 0 : nx - 1, :, 0:wb]
    all_c2 = rows.at[:, 0, 0 : ny - 1, :, 0:wc]
    all_a3 = rows.at[0 : nz - 1, :, :, :, 0 : nxl * wa]
    all_b3 = rows.at[:, :, 0 : ny - 1, :, 0 : nxl * wb]
    all_c3 = rows.at[:, 0, :, :, 0 : (nx - 1) * wc]

    me_b, me_c = pick(y, x), pick(x, y)
    ref = a1((x, y))
    for o in range(1, nx * ny):
        to = ((x + o) % nx, (y + o // nx) % ny)
        remote(ref, ref, send_sem.at[4], recv_sem.at[4], at_xy(to)).start()
    exchange(nz, z, c1, send_sem.at[6], recv_sem.at[6], at_z)
    exchange(nz, z, b1, send_sem.at[5], recv_sem.at[5], at_z)

    sibling = at_x(x, 1 - c)

    def share(kind, ref):
        remote(ref, ref, send_sem.at[12 + kind], recv_sem.at[7 + kind], sibling).start()

    def last(view, kind, n, me, in_sems, device_of):
        ref = view(kind, me)
        for o in range(1, n):
            remote(ref, ref, send_sem.at[9 + kind], in_sems.at[me], device_of((me + o) % n)).start()
        share(kind, ref)

    def last_in(view, kind, n, me, in_sems):
        for o in range(1, n):
            ref = view(kind, (me + o) % n)
            arrived(ref, in_sems.at[(me + o) % n])
            share(kind, ref)

    def at_x_(i):
        return at_x(i)

    def slab(kind, z_):
        return rows.at[z_, :, :, :, all_a]

    arrived(all_a1, recv_sem.at[4])
    last(slab, 0, nz, z, a_recv, at_z)
    arrived(all_c1, recv_sem.at[6])
    ref = c2((x, y))
    for o in range(1, nx):
        remote(ref, ref, send_sem.at[8], recv_sem.at[16], at_xy(place_b((me_b + o) % nx))).start()
    arrived(all_b1, recv_sem.at[5])
    ref = b2((x, y))
    for o in range(1, nx):
        remote(ref, ref, send_sem.at[7], recv_sem.at[15], at_xy(place_c((me_c + o) % nx))).start()
    arrived(all_c2, recv_sem.at[16])

    @pl.when(c == 0)
    def _():
        last(along_x, 2, nx, x, c_recv, at_x_)
        arrived(all_b2, recv_sem.at[15])
        last(along_y, 1, ny, y, b_recv, at_y)
        last_in(along_y, 1, ny, y, b_recv)

    @pl.when(c == 1)
    def _():
        last(along_y, 2, ny, y, c_recv, at_y)
        arrived(all_b2, recv_sem.at[15])
        last(along_x, 1, nx, x, b_recv, at_x_)
        last_in(along_x, 1, nx, x, b_recv)

    last_in(slab, 0, nz, z, a_recv)
    their_a, their_b, their_c = cols_all(1 - c)
    arrived(rows.at[:, :, :, :, their_a], recv_sem.at[7])
    arrived(rows.at[:, :, :, :, their_b], recv_sem.at[8])
    loads[7].wait()
    loads[8].wait()
    table_base = ((v * nz + z) * ng + g) * table_rows
    step_blocks = max(1, 256 // tz)
    step_rows = step_blocks * tz
    early = nxl * (wa + wb)

    def logits_of(i, starts, size):
        total_ = None
        for start in starts:
            chunk = rows[pl.ds(i * step_blocks, step_blocks), :, :, :, start : start + size].reshape(step_rows, size)
            values = lax.dot_general(emb[:, start : start + size], chunk, NT, preferred_element_type=F32)
            total_ = values if total_ is None else total_ + values
        return total_

    def lanes_of(i):
        return pl.ds(pl.multiple_of(i * step_rows, 128), step_rows)

    def early_step(i, carry):
        logit[:, lanes_of(i)] = logits_of(i, range(0, d, d // NC), early)
        return carry

    steps = nz // step_blocks

    @pl.when(c == 0)
    def _():
        last_in(along_x, 2, nx, x, c_recv)

    @pl.when(c == 1)
    def _():
        last_in(along_y, 2, ny, y, c_recv)

    lax.fori_loop(0, steps, early_step, 0)
    arrived(rows.at[:, :, :, :, their_c], recv_sem.at[9])
    rows_store = pltpu.make_async_copy(rows, rows_out, store_sem.at[0])
    rows_store.start()

    def logit_step(i, carry):
        lanes = lanes_of(i)
        values = logit[:, lanes] + logits_of(i, range(early, d, d // NC), d // NC - early)
        logit[:, lanes] = values
        top_ = jnp.max(values, axis=0, keepdims=True)
        total_ = jnp.sum(jnp.exp(values - top_), axis=0, keepdims=True)
        token = table_base + lax.broadcasted_iota(jnp.int32, values.shape, 0)
        local_stat[i, 0:1, :] = top_ + jnp.log(total_)
        local_stat[i, 1:2, :] = jnp.sum(jnp.where(token == labels[:, lanes], values, 0.0), axis=0, keepdims=True)
        return carry

    lax.fori_loop(0, steps, logit_step, 0)
    stat_rows = nz * tz // 128
    per_step = step_rows // 128
    nxc = nx * NC
    xc = x * NC + c
    for r in range(stat_rows):
        for k in range(2):
            stat_x[xc, k * stat_rows + r : k * stat_rows + r + 1, :] = local_stat[
                r // per_step, k : k + 1, (r % per_step) * 128 : (r % per_step + 1) * 128
            ]

    def merge(ref, n):
        lses = [ref[i, 0:stat_rows] for i in range(n)]
        top_ = functools.reduce(jnp.maximum, lses)
        total_ = sum(jnp.exp(s - top_) for s in lses)
        return top_ + jnp.log(total_), sum(ref[i, stat_rows : 2 * stat_rows] for i in range(n))

    def stat_round(ref, n, me, k, device_of):
        exchange(n, me, lambda i: ref.at[i], send_sem.at[15 + k], recv_sem.at[10 + k], device_of)
        arrived(ref.at[0 : n - 1], recv_sem.at[10 + k])
        return merge(ref, n)

    lse, picked = stat_round(stat_x, nxc, xc, 0, lambda i: at_x(i // NC, i % NC))
    stat_y[y, 0:stat_rows] = lse
    stat_y[y, stat_rows : 2 * stat_rows] = picked
    lse, picked = stat_round(stat_y, ny, y, 1, at_y)
    stat_z[z, 0:stat_rows] = lse
    stat_z[z, stat_rows : 2 * stat_rows] = picked
    lse, picked = stat_round(stat_z, nz, z, 2, at_z)

    place = lax.broadcasted_iota(jnp.int32, lse.shape, 0) * 128 + lax.broadcasted_iota(jnp.int32, lse.shape, 1)
    live = place < tgt_len[0]
    loss_out[...] = jnp.where(live, lse - picked, 0.0)
    lse = jnp.where(live, lse, 1e30)
    lse = jnp.concatenate([lse[r : r + 1, :] for r in range(stat_rows)], axis=1)
    place = lax.broadcasted_iota(jnp.int32, labels.shape, 1)
    hit = jnp.where(place < tgt_len[0], labels[...] - table_base, -1)

    def grad_step(i, carry):
        some = pl.ds(i * 128, 128)
        token = i * 128 + lax.broadcasted_iota(jnp.int32, (128, nz * tz), 0)
        grad[some, :] = (jnp.exp(logit[some, :] - lse) - jnp.where(token == hit, 1.0, 0.0)).astype(BF16)
        return carry

    lax.fori_loop(0, table_rows // 128, grad_step, 0)

    grad_store = pltpu.make_async_copy(grad, grad_out, store_sem.at[1])
    grad_store.start()
    for i, ref in enumerate(
        (
            kv.at[0 : nz - 1],
            ctx_got,
            part.at[0 : nv - 1],
            norm_stat.at[0 : pieces - 1],
            all_a1,
            all_b1,
            all_c1,
            all_b2,
            all_c2,
            all_a3,
            all_b3,
            all_c3,
            rows.at[:, :, :, :, all_a],
            rows.at[:, :, :, :, all_b],
            rows.at[:, :, :, :, all_c],
            stat_x.at[0 : nxc - 1],
            stat_y.at[0 : ny - 1],
            stat_z.at[0 : nz - 1],
        )
    ):
        left(ref, send_sem.at[i])
    rows_store.wait()
    grad_store.wait()


def grad_kernel(grad, rows, loss, out, loss_out):
    loss_out[...] = loss[...]
    cols = pl.ds(pl.multiple_of(pl.program_id(0) * out.shape[1], 128), out.shape[1])
    chunk = rows[:, :, :, :, cols].reshape(grad.shape[1], out.shape[1])
    out[...] = jnp.dot(grad[...], chunk, preferred_element_type=F32).astype(BF16)


def body(
    cfg,
    decoder_states,
    encoder_states,
    ln_gains,
    w_query,
    w_key,
    w_value,
    w_out,
    embedding,
    labels,
    src_length,
    tgt_length,
):
    nv, nz, ng, ny, nxl = cfg
    tz, d = decoder_states.shape
    ez = encoder_states.shape[0]
    hd = w_query.shape[1]
    table_rows = embedding.shape[0]
    target = labels.shape[0]
    tg = tz // ng
    ty = tg // ny
    width = d // (nxl * NC)
    nx = ng * nxl
    half = nz // 2
    pieces = nxl * NC
    step_blocks = max(1, 256 // tz)
    stat_rows = target // 128
    hbm = pl.BlockSpec(memory_space=pl.ANY)
    vmem = pl.BlockSpec(memory_space=pltpu.VMEM)
    smem = pl.BlockSpec(memory_space=pltpu.SMEM)
    dma = pltpu.SemaphoreType.DMA
    far = [
        pltpu.with_memory_space_constraint(array, pltpu.HBM)
        for array in (
            decoder_states,
            encoder_states,
            ln_gains,
            labels.reshape(1, target),
            w_query,
            w_key,
            w_value,
            w_out,
            embedding,
        )
    ]
    loss, grad, rows = pl.pallas_call(
        functools.partial(front_kernel, cfg),
        out_shape=(
            jax.ShapeDtypeStruct((stat_rows, 128), F32),
            pltpu.VMEM((table_rows, target), BF16),
            pltpu.VMEM((nz, ng, ny, ty, d), BF16),
        ),
        in_specs=[smem, smem] + [hbm] * len(far),
        out_specs=(vmem, hbm, hbm),
        scratch_shapes=[
            pltpu.VMEM(ln_gains.shape, F32),
            pltpu.VMEM((1, target), jnp.int32),
            pltpu.VMEM((tz, d), BF16),
            pltpu.VMEM((ez, d), BF16),
            pltpu.VMEM((d, hd), BF16),
            pltpu.VMEM((d, 2 * hd), BF16),
            pltpu.VMEM((hd, d), BF16),
            pltpu.VMEM((table_rows, d), BF16),
            pltpu.VMEM((nz, 2, ez, hd), BF16),
            pltpu.VMEM((tz, hd + 128), F32),
            pltpu.VMEM((tg, hd + 128), F32),
            pltpu.VMEM((nv, ty, width), BF16),
            pltpu.VMEM((nv, ty, width), BF16),
            pltpu.VMEM((pieces, ty, 128), F32),
            pltpu.VMEM((nz, ng, ny, ty, d), BF16),
            pltpu.VMEM((table_rows, target), F32),
            pltpu.VMEM((table_rows, target), BF16),
            pltpu.VMEM((nz // step_blocks, 8, step_blocks * tz), F32),
            pltpu.VMEM((nx * NC, 2 * stat_rows, 128), F32),
            pltpu.VMEM((ny, 2 * stat_rows, 128), F32),
            pltpu.VMEM((nz, 2 * stat_rows, 128), F32),
            dma((9,)),
            dma((2,)),
            dma((2, half, 2)),
            dma((nz,)),
            dma((ny,)),
            dma((nx,)),
            dma((18,)),
            dma((17,)),
        ],
        compiler_params=pltpu.CompilerParams(
            collective_id=0, has_side_effects=True, vmem_limit_bytes=40 * 1024 * 1024
        ),
    )(src_length, tgt_length, *far)
    block = 512
    grad_table, loss = pl.pallas_call(
        grad_kernel,
        out_shape=(jax.ShapeDtypeStruct((table_rows, d), BF16), jax.ShapeDtypeStruct(loss.shape, F32)),
        grid=(d // block,),
        in_specs=[vmem, vmem, vmem],
        out_specs=(pl.BlockSpec((table_rows, block), lambda i: (0, i)), pl.BlockSpec(loss.shape, lambda i: (0, 0))),
        compiler_params=pltpu.CompilerParams(vmem_limit_bytes=24 * 1024 * 1024),
    )(*(pltpu.with_memory_space_constraint(array, pltpu.VMEM) for array in (grad, rows)), loss)
    return (loss.reshape(target), grad_table)


def solution(mesh):
    nv, nz, ng = mesh.shape["vocab"], mesh.shape["seq"], mesh.shape["grp"]
    cfg = (nv, nz, ng, NY, nv // (NY * NC))
    in_specs = (
        P("seq", None),
        P(("seq", "grp"), None),
        P(),
        P(None, "vocab"),
        P(None, "vocab"),
        P(None, "vocab"),
        P("vocab", None),
        P(("vocab", "seq", "grp"), None),
        P(),
        P(),
        P(),
    )
    out_specs = (P(), P(("vocab", "seq", "grp"), None))
    return jax.shard_map(
        functools.partial(body, cfg), mesh=mesh, in_specs=in_specs, out_specs=out_specs, check_vma=False
    )
```

```python
import functools
import math

import jax
import jax.numpy as jnp
from jax import lax
from jax.experimental import pallas as pl
from jax.experimental.pallas import tpu as pltpu
from jax.sharding import PartitionSpec as P

HEAD_DIM = 128
EPSILON = 1e-05
MESH = pl.DeviceIdType.MESH
NC = 2
NY = 4
NT = (((1,), (1,)), ((), ()))
F32, BF16 = jnp.float32, jnp.bfloat16


def front_kernel(
    cfg,
    src_len,
    tgt_len,
    dec_in,
    enc_in,
    gains_in,
    labels_in,
    wq_in,
    wk_in,
    wv_in,
    wo_in,
    emb_in,
    loss_out,
    grad_out,
    rows_out,
    gains,
    labels,
    dec,
    enc,
    wq,
    wkv,
    wo,
    emb,
    kv,
    ctx_own,
    ctx_got,
    part,
    summed,
    norm_stat,
    rows,
    logit,
    grad,
    local_stat,
    stat_x,
    stat_y,
    stat_z,
    load_sem,
    store_sem,
    kv_recv,
    a_recv,
    b_recv,
    c_recv,
    send_sem,
    recv_sem,
):
    nv, nz, ng, ny, nxl = cfg
    d = dec.shape[1]
    tz = dec.shape[0]
    ez = enc.shape[0]
    hd = wq.shape[1]
    tg = tz // ng
    ty = tg // ny
    width = d // (nxl * NC)
    wa, wb, wc = width // 4, width // 4, width // 2
    table_rows = emb.shape[0]
    nx = ng * nxl
    half = nz // 2

    v = lax.axis_index("vocab")
    z = lax.axis_index("seq")
    g = lax.axis_index("grp")
    c = v % NC
    y = (v // NC) % ny
    xl = v // (NC * ny)
    x = g * nxl + xl

    def vocab_of(xl_, y_, c_):
        return (xl_ * ny + y_) * NC + c_

    def at_x(x_, c_=None):
        return {"vocab": vocab_of(x_ % nxl, y, c if c_ is None else c_), "seq": z, "grp": x_ // nxl}

    def at_y(y_):
        return {"vocab": vocab_of(xl, y_, c), "seq": z, "grp": g}

    def at_z(z_):
        return {"vocab": v, "seq": z_, "grp": g}

    def at_v(v_):
        return {"vocab": v_, "seq": z, "grp": g}

    barrier = pltpu.get_barrier_semaphore()
    friends = [at_v((v + o) % nv) for o in range(1, nv)]
    friends += [at_z((z + o) % nz) for o in range(1, nz)]
    friends += [{"vocab": v_, "seq": z, "grp": (g + o) % ng} for o in range(1, ng) for v_ in range(nv)]

    loads = [
        pltpu.make_async_copy(src, dst, load_sem.at[i])
        for i, (src, dst) in enumerate(
            (
                (enc_in, enc),
                (wk_in, wkv.at[:, 0:hd]),
                (wv_in, wkv.at[:, hd : 2 * hd]),
                (dec_in, dec),
                (gains_in, gains),
                (wq_in, wq),
                (wo_in, wo),
                (labels_in, labels),
                (emb_in, emb),
            )
        )
    ]
    for load in loads[:6]:
        load.start()
    for friend in friends:
        pl.semaphore_signal(barrier, inc=1, device_id=friend, device_id_type=MESH)

    def remote(src, dst, out_sem, in_sem, device):
        return pltpu.make_async_remote_copy(
            src_ref=src, dst_ref=dst, send_sem=out_sem, recv_sem=in_sem, device_id=device, device_id_type=MESH
        )

    def arrived(ref, in_sem):
        remote(ref, ref, send_sem.at[0], in_sem, at_z((z + 1) % nz)).wait_recv()

    def left(ref, out_sem):
        remote(ref, ref, out_sem, recv_sem.at[0], at_z((z + 1) % nz)).wait_send()

    for load in loads[:3]:
        load.wait()
    for load in loads[6:]:
        load.start()
    own_kv = jnp.dot(enc[...], wkv[...], preferred_element_type=F32).astype(BF16)
    kv[z, 0] = own_kv[:, 0:hd]
    kv[z, 1] = own_kv[:, hd : 2 * hd]

    pl.semaphore_wait(barrier, len(friends))

    def kv_post(way, t, part_):
        step = (1, nz - 1)[way]
        ref = kv.at[(z + t * (nz - step)) % nz, part_]
        remote(ref, ref, send_sem.at[0], kv_recv.at[way, t, part_], at_z((z + step) % nz)).start()

    for part_ in (0, 1):
        for way in (0, 1):
            if half > 1:
                kv_post(way, 0, part_)
    for part_ in (0, 1):
        ref = kv.at[z, part_]
        remote(ref, ref, send_sem.at[0], kv_recv.at[0, half - 1, part_], at_z((z + half) % nz)).start()

    loads[3].wait()
    loads[4].wait()
    states = dec[...].astype(F32)
    centred = states - jnp.mean(states, axis=1, keepdims=True)
    variance = jnp.mean(centred * centred, axis=1, keepdims=True)
    normed = (centred * lax.rsqrt(variance + EPSILON) * gains[0:1, :]).astype(BF16)
    loads[5].wait()
    query = (jnp.dot(normed, wq[...], preferred_element_type=F32) * (1.0 / math.sqrt(hd))).astype(BF16)

    source_count = src_len[0]

    def scores_of(block):
        s = lax.dot_general(query, kv[block, 0], NT, preferred_element_type=F32)
        place = (block * ng + g) * ez + lax.broadcasted_iota(jnp.int32, s.shape, 1)
        valid = place < source_count
        return block, valid, jnp.where(valid, s, -1e30)

    scored = [scores_of(z)]
    for t in range(1, half + 1):
        for part_ in (0, 1):
            for way in (0, 1):
                if t < half or way == 0:
                    arrived(kv.at[(z + t * (nz - (1, nz - 1)[way])) % nz, part_], kv_recv.at[way, t - 1, part_])
                if t + 1 < half:
                    kv_post(way, t, part_)
        scored += [scores_of((z + o) % nz) for o in ((nz - t, t) if t < half else (half,))]
    top = functools.reduce(jnp.maximum, [s for _, _, s in scored])
    top = jnp.max(top, axis=1, keepdims=True)
    total = jnp.zeros((tz, ez), F32)
    acc = jnp.zeros((tz, hd), F32)
    for block, valid, s in scored:
        e = jnp.where(valid, jnp.exp(s - top), 0.0)
        total = total + e
        acc = acc + jnp.dot(e.astype(BF16), kv[block, 1], preferred_element_type=F32)
    total = jnp.sum(total, axis=1, keepdims=True)
    low = lax.broadcasted_iota(jnp.int32, (tz, 128), 1) < 64
    ctx_own[:, 0:hd] = acc
    ctx_own[:, hd : hd + 128] = jnp.where(low, top, total)
    remote(
        ctx_own.at[pl.ds(pl.multiple_of((1 - g) * tg, tg), tg)],
        ctx_got,
        send_sem.at[1],
        recv_sem.at[1],
        {"vocab": v, "seq": z, "grp": 1 - g},
    ).start()
    arrived(ctx_got, recv_sem.at[1])
    mine = ctx_own[pl.ds(pl.multiple_of(g * tg, tg), tg), :]
    other = ctx_got[...]
    top0, top1 = mine[:, hd : hd + 1], other[:, hd : hd + 1]
    both = jnp.maximum(top0, top1)
    f0, f1 = jnp.exp(top0 - both), jnp.exp(top1 - both)
    total = mine[:, hd + 64 : hd + 65] * f0 + other[:, hd + 64 : hd + 65] * f1
    context = ((mine[:, 0:hd] * f0 + other[:, 0:hd] * f1) / total).astype(BF16)

    def columns_of(xl_, c_):
        base = c_ * (d // NC)
        return (
            (base + xl_ * wa, wa),
            (base + nxl * wa + xl_ * wb, wb),
            (base + nxl * (wa + wb) + xl_ * wc, wc),
        )

    loads[6].wait()
    piece = xl * NC + c
    pieces = nxl * NC
    for op in range(pieces):
        to_piece = (piece + op) % pieces
        weights = jnp.concatenate(
            [
                wo[:, pl.ds(pl.multiple_of(start, 128), size)]
                for start, size in columns_of(to_piece // NC, to_piece % NC)
            ],
            axis=1,
        )
        projected = jnp.dot(context, weights, preferred_element_type=F32).astype(BF16)
        for y_ in range(ny):
            part[vocab_of(to_piece // NC, y_, to_piece % NC)] = projected[y_ * ty : (y_ + 1) * ty]
        for oy in range(ny):
            if op + oy > 0:
                to = vocab_of(to_piece // NC, (y + oy) % ny, to_piece % NC)
                remote(part.at[to], summed.at[v], send_sem.at[2], recv_sem.at[2], at_v(to)).start()
    own_cols = [(pl.multiple_of(start, 128), size) for start, size in columns_of(xl, c)]
    own_row = pl.multiple_of(g * tg + y * ty, ty)
    hidden = part[v].astype(F32) + jnp.concatenate(
        [dec[pl.ds(own_row, ty), pl.ds(start, size)].astype(F32) for start, size in own_cols], axis=1
    )
    arrived(summed.at[0 : nv - 1], recv_sem.at[2])
    for o in range(1, nv):
        hidden = hidden + summed[(v + o) % nv].astype(F32)

    own_mean = jnp.mean(hidden, axis=1, keepdims=True)
    own_square = jnp.sum((hidden - own_mean) * (hidden - own_mean), axis=1, keepdims=True)
    low = lax.broadcasted_iota(jnp.int32, (ty, 128), 1) < 64
    norm_stat[piece] = jnp.where(low, own_mean, own_square)
    for o in range(1, pieces):
        to = (piece + o) % pieces
        remote(
            norm_stat.at[piece],
            norm_stat.at[piece],
            send_sem.at[3],
            recv_sem.at[3],
            at_v(vocab_of(to // NC, y, to % NC)),
        ).start()
    arrived(norm_stat.at[0 : pieces - 1], recv_sem.at[3])
    means = [norm_stat[i, :, 0:1] for i in range(pieces)]
    squares = [norm_stat[i, :, 64:65] for i in range(pieces)]
    mean = sum(means) * (1.0 / pieces)
    square = sum(squares) + width * sum((m - mean) * (m - mean) for m in means)
    scale = lax.rsqrt(square * (1.0 / d) + EPSILON)
    gain = jnp.concatenate([gains[1:2, pl.ds(start, size)] for start, size in own_cols], axis=1)
    final = ((hidden - mean) * scale * gain).astype(BF16)
    at = 0
    for start, size in own_cols:
        rows[z, g, y, :, pl.ds(start, size)] = final[:, at : at + size]
        at += size

    def cols_all(c_):
        base = pl.multiple_of(c_ * (d // NC), 128)
        return (
            pl.ds(base, nxl * wa),
            pl.ds(pl.multiple_of(base + nxl * wa, 128), nxl * wb),
            pl.ds(pl.multiple_of(base + nxl * (wa + wb), 128), nxl * wc),
        )

    def cols_piece(xl_):
        return [pl.ds(pl.multiple_of(start, 128), size) for start, size in columns_of(xl_, c)]

    _, own_b, own_c = cols_piece(xl)
    all_a, all_b, all_c = cols_all(c)

    def exchange(n, me, ref_of, out_sem, in_sem, device_of):
        ref = ref_of(me)
        for o in range(1, n):
            remote(ref, ref, out_sem, in_sem, device_of((me + o) % n)).start()

    swap = c

    def pick(here, there):
        return here + swap * (there - here)

    def place_b(i):
        return pick(x, i), pick(i, y)

    def place_c(i):
        return pick(i, x), pick(y, i)

    def at_xy(xy):
        return {"vocab": vocab_of(xy[0] % nxl, xy[1], c), "seq": z, "grp": xy[0] // nxl}

    def a1(xy):
        return rows.at[z, xy[0] // nxl, xy[1], :, cols_piece(xy[0] % nxl)[0]]

    def b1(z_):
        return rows.at[z_, g, y, :, own_b]

    def c1(z_):
        return rows.at[z_, g, y, :, own_c]

    def b2(xy):
        return rows.at[:, xy[0] // nxl, xy[1], :, cols_piece(xy[0] % nxl)[1]]

    def c2(xy):
        return rows.at[:, xy[0] // nxl, xy[1], :, cols_piece(xy[0] % nxl)[2]]

    def along_x(kind, x_):
        return rows.at[:, x_ // nxl, :, :, cols_piece(x_ % nxl)[kind]]

    def along_y(kind, y_):
        return rows.at[:, :, y_, :, cols_all(c)[kind]]

    all_a1 = rows.at[0, 0, 0, :, 0 : (nx * ny - 1) * wa]
    all_b1 = rows.at[0 : nz - 1, 0, 0, :, 0:wb]
    all_c1 = rows.at[0 : nz - 1, 0, 0, :, 0:wc]
    all_b2 = rows.at[:, 0, 0 : nx - 1, :, 0:wb]
    all_c2 = rows.at[:, 0, 0 : ny - 1, :, 0:wc]
    all_a3 = rows.at[0 : nz - 1, :, :, :, 0 : nxl * wa]
    all_b3 = rows.at[:, :, 0 : ny - 1, :, 0 : nxl * wb]
    all_c3 = rows.at[:, 0, :, :, 0 : (nx - 1) * wc]

    me_b, me_c = pick(y, x), pick(x, y)
    exchange(nz, z, c1, send_sem.at[6], recv_sem.at[6], at_z)
    exchange(nz, z, b1, send_sem.at[5], recv_sem.at[5], at_z)

    ref = a1((x, y))
    for o in range(1, nx * ny):
        to = ((x + o) % nx, (y + o // nx) % ny)
        remote(ref, ref, send_sem.at[4], recv_sem.at[4], at_xy(to)).start()
    sibling = at_x(x, 1 - c)

    def share(kind, ref):
        remote(ref, ref, send_sem.at[12 + kind], recv_sem.at[7 + kind], sibling).start()

    def last(view, kind, n, me, in_sems, device_of):
        ref = view(kind, me)
        for o in range(1, n):
            remote(ref, ref, send_sem.at[9 + kind], in_sems.at[me], device_of((me + o) % n)).start()
        share(kind, ref)

    def last_in(view, kind, n, me, in_sems):
        for o in range(1, n):
            ref = view(kind, (me + o) % n)
            arrived(ref, in_sems.at[(me + o) % n])
            share(kind, ref)

    def at_x_(i):
        return at_x(i)

    def slab(kind, z_):
        return rows.at[z_, :, :, :, all_a]

    arrived(all_a1, recv_sem.at[4])
    last(slab, 0, nz, z, a_recv, at_z)
    arrived(all_c1, recv_sem.at[6])
    ref = c2((x, y))
    for o in range(1, nx):
        remote(ref, ref, send_sem.at[8], recv_sem.at[16], at_xy(place_b((me_b + o) % nx))).start()
    arrived(all_b1, recv_sem.at[5])
    ref = b2((x, y))
    for o in range(1, nx):
        remote(ref, ref, send_sem.at[7], recv_sem.at[15], at_xy(place_c((me_c + o) % nx))).start()
    arrived(all_c2, recv_sem.at[16])

    @pl.when(c == 0)
    def _():
        last(along_x, 2, nx, x, c_recv, at_x_)
        arrived(all_b2, recv_sem.at[15])
        last(along_y, 1, ny, y, b_recv, at_y)
        last_in(along_y, 1, ny, y, b_recv)

    @pl.when(c == 1)
    def _():
        last(along_y, 2, ny, y, c_recv, at_y)
        arrived(all_b2, recv_sem.at[15])
        last(along_x, 1, nx, x, b_recv, at_x_)
        last_in(along_x, 1, nx, x, b_recv)

    last_in(slab, 0, nz, z, a_recv)
    their_a, their_b, their_c = cols_all(1 - c)
    arrived(rows.at[:, :, :, :, their_a], recv_sem.at[7])
    arrived(rows.at[:, :, :, :, their_b], recv_sem.at[8])
    loads[7].wait()
    loads[8].wait()
    table_base = ((v * nz + z) * ng + g) * table_rows
    step_blocks = max(1, 256 // tz)
    step_rows = step_blocks * tz
    early = nxl * (wa + wb)

    def logits_of(i, starts, size):
        total_ = None
        for start in starts:
            chunk = rows[pl.ds(i * step_blocks, step_blocks), :, :, :, start : start + size].reshape(step_rows, size)
            values = lax.dot_general(emb[:, start : start + size], chunk, NT, preferred_element_type=F32)
            total_ = values if total_ is None else total_ + values
        return total_

    def lanes_of(i):
        return pl.ds(pl.multiple_of(i * step_rows, 128), step_rows)

    def early_step(i, carry):
        logit[:, lanes_of(i)] = logits_of(i, range(0, d, d // NC), early)
        return carry

    steps = nz // step_blocks

    @pl.when(c == 0)
    def _():
        last_in(along_x, 2, nx, x, c_recv)

    @pl.when(c == 1)
    def _():
        last_in(along_y, 2, ny, y, c_recv)

    lax.fori_loop(0, steps, early_step, 0)
    arrived(rows.at[:, :, :, :, their_c], recv_sem.at[9])
    rows_store = pltpu.make_async_copy(rows, rows_out, store_sem.at[0])
    rows_store.start()

    def logit_step(i, carry):
        lanes = lanes_of(i)
        values = logit[:, lanes] + logits_of(i, range(early, d, d // NC), d // NC - early)
        logit[:, lanes] = values
        top_ = jnp.max(values, axis=0, keepdims=True)
        total_ = jnp.sum(jnp.exp(values - top_), axis=0, keepdims=True)
        token = table_base + lax.broadcasted_iota(jnp.int32, values.shape, 0)
        local_stat[i, 0:1, :] = top_ + jnp.log(total_)
        local_stat[i, 1:2, :] = jnp.sum(jnp.where(token == labels[:, lanes], values, 0.0), axis=0, keepdims=True)
        return carry

    lax.fori_loop(0, steps, logit_step, 0)
    stat_rows = nz * tz // 128
    per_step = step_rows // 128
    nxc = nx * NC
    xc = x * NC + c
    for r in range(stat_rows):
        for k in range(2):
            stat_x[xc, k * stat_rows + r : k * stat_rows + r + 1, :] = local_stat[
                r // per_step, k : k + 1, (r % per_step) * 128 : (r % per_step + 1) * 128
            ]

    def merge(ref, n):
        lses = [ref[i, 0:stat_rows] for i in range(n)]
        top_ = functools.reduce(jnp.maximum, lses)
        total_ = sum(jnp.exp(s - top_) for s in lses)
        return top_ + jnp.log(total_), sum(ref[i, stat_rows : 2 * stat_rows] for i in range(n))

    def stat_round(ref, n, me, k, device_of, meanwhile=None):
        exchange(n, me, lambda i: ref.at[i], send_sem.at[15 + k], recv_sem.at[10 + k], device_of)
        if meanwhile is not None:
            meanwhile()
        arrived(ref.at[0 : n - 1], recv_sem.at[10 + k])
        return merge(ref, n)

    lse, picked = stat_round(stat_x, nxc, xc, 0, lambda i: at_x(i // NC, i % NC))
    stat_y[y, 0:stat_rows] = lse
    stat_y[y, stat_rows : 2 * stat_rows] = picked
    lse, picked = stat_round(stat_y, ny, y, 1, at_y)
    stat_z[z, 0:stat_rows] = lse
    stat_z[z, stat_rows : 2 * stat_rows] = picked

    def settle():
        for i, ref in enumerate(
            (
                kv.at[0 : nz - 1],
                ctx_got,
                part.at[0 : nv - 1],
                norm_stat.at[0 : pieces - 1],
                all_a1,
                all_b1,
                all_c1,
                all_b2,
                all_c2,
                all_a3,
                all_b3,
                all_c3,
                rows.at[:, :, :, :, all_a],
                rows.at[:, :, :, :, all_b],
                rows.at[:, :, :, :, all_c],
                stat_x.at[0 : nxc - 1],
                stat_y.at[0 : ny - 1],
            )
        ):
            left(ref, send_sem.at[i])
        rows_store.wait()

    lse, picked = stat_round(stat_z, nz, z, 2, at_z, settle)

    place = lax.broadcasted_iota(jnp.int32, lse.shape, 0) * 128 + lax.broadcasted_iota(jnp.int32, lse.shape, 1)
    live = place < tgt_len[0]
    loss_out[...] = jnp.where(live, lse - picked, 0.0)
    lse = jnp.where(live, lse, 1e30)
    lse = jnp.concatenate([lse[r : r + 1, :] for r in range(stat_rows)], axis=1)
    place = lax.broadcasted_iota(jnp.int32, labels.shape, 1)
    hit = jnp.where(place < tgt_len[0], labels[...] - table_base, -1)

    def grad_step(i, carry):
        some = pl.ds(i * 128, 128)
        token = i * 128 + lax.broadcasted_iota(jnp.int32, (128, nz * tz), 0)
        grad[some, :] = (jnp.exp(logit[some, :] - lse) - jnp.where(token == hit, 1.0, 0.0)).astype(BF16)
        pltpu.make_async_copy(grad.at[some], grad_out.at[some], store_sem.at[1]).start()
        return carry

    lax.fori_loop(0, table_rows // 128, grad_step, 0)

    left(stat_z.at[0 : nz - 1], send_sem.at[17])
    pltpu.make_async_copy(grad, grad_out, store_sem.at[1]).wait()


def grad_kernel(tgt_len, grad, rows, loss, out, loss_out):
    loss_out[...] = loss[...]
    nz, block = rows.shape[0], out.shape[1]
    tz = grad.shape[1] // nz
    cols = pl.ds(pl.multiple_of(pl.program_id(0) * block, 128), block)
    step = max(1, 256 // tz)
    live = (tgt_len[0] + step * tz - 1) // (step * tz)
    for n in range(1, nz // step + 1):

        @pl.when(jnp.clip(live, 1, nz // step) == n)
        def _():
            count = n * step * tz
            chunk = rows[0 : n * step, :, :, :, cols].reshape(count, block)
            out[...] = jnp.dot(grad[:, 0:count], chunk, preferred_element_type=F32).astype(BF16)


def body(
    cfg,
    decoder_states,
    encoder_states,
    ln_gains,
    w_query,
    w_key,
    w_value,
    w_out,
    embedding,
    labels,
    src_length,
    tgt_length,
):
    nv, nz, ng, ny, nxl = cfg
    tz, d = decoder_states.shape
    ez = encoder_states.shape[0]
    hd = w_query.shape[1]
    table_rows = embedding.shape[0]
    target = labels.shape[0]
    tg = tz // ng
    ty = tg // ny
    width = d // (nxl * NC)
    nx = ng * nxl
    half = nz // 2
    pieces = nxl * NC
    step_blocks = max(1, 256 // tz)
    stat_rows = target // 128
    hbm = pl.BlockSpec(memory_space=pl.ANY)
    vmem = pl.BlockSpec(memory_space=pltpu.VMEM)
    smem = pl.BlockSpec(memory_space=pltpu.SMEM)
    dma = pltpu.SemaphoreType.DMA
    far = [
        pltpu.with_memory_space_constraint(array, pltpu.HBM)
        for array in (
            decoder_states,
            encoder_states,
            ln_gains,
            labels.reshape(1, target),
            w_query,
            w_key,
            w_value,
            w_out,
            embedding,
        )
    ]
    loss, grad, rows = pl.pallas_call(
        functools.partial(front_kernel, cfg),
        out_shape=(
            jax.ShapeDtypeStruct((stat_rows, 128), F32),
            pltpu.VMEM((table_rows, target), BF16),
            pltpu.VMEM((nz, ng, ny, ty, d), BF16),
        ),
        in_specs=[smem, smem] + [hbm] * len(far),
        out_specs=(vmem, hbm, hbm),
        scratch_shapes=[
            pltpu.VMEM(ln_gains.shape, F32),
            pltpu.VMEM((1, target), jnp.int32),
            pltpu.VMEM((tz, d), BF16),
            pltpu.VMEM((ez, d), BF16),
            pltpu.VMEM((d, hd), BF16),
            pltpu.VMEM((d, 2 * hd), BF16),
            pltpu.VMEM((hd, d), BF16),
            pltpu.VMEM((table_rows, d), BF16),
            pltpu.VMEM((nz, 2, ez, hd), BF16),
            pltpu.VMEM((tz, hd + 128), F32),
            pltpu.VMEM((tg, hd + 128), F32),
            pltpu.VMEM((nv, ty, width), BF16),
            pltpu.VMEM((nv, ty, width), BF16),
            pltpu.VMEM((pieces, ty, 128), F32),
            pltpu.VMEM((nz, ng, ny, ty, d), BF16),
            pltpu.VMEM((table_rows, target), F32),
            pltpu.VMEM((table_rows, target), BF16),
            pltpu.VMEM((nz // step_blocks, 8, step_blocks * tz), F32),
            pltpu.VMEM((nx * NC, 2 * stat_rows, 128), F32),
            pltpu.VMEM((ny, 2 * stat_rows, 128), F32),
            pltpu.VMEM((nz, 2 * stat_rows, 128), F32),
            dma((9,)),
            dma((2,)),
            dma((2, half, 2)),
            dma((nz,)),
            dma((ny,)),
            dma((nx,)),
            dma((18,)),
            dma((17,)),
        ],
        compiler_params=pltpu.CompilerParams(
            collective_id=0, has_side_effects=True, vmem_limit_bytes=40 * 1024 * 1024
        ),
    )(src_length, tgt_length, *far)
    block = 512
    grad_table, loss = pl.pallas_call(
        grad_kernel,
        out_shape=(jax.ShapeDtypeStruct((table_rows, d), BF16), jax.ShapeDtypeStruct(loss.shape, F32)),
        grid=(d // block,),
        in_specs=[smem, vmem, vmem, vmem],
        out_specs=(pl.BlockSpec((table_rows, block), lambda i: (0, i)), pl.BlockSpec(loss.shape, lambda i: (0, 0))),
        compiler_params=pltpu.CompilerParams(vmem_limit_bytes=24 * 1024 * 1024),
    )(tgt_length, *(pltpu.with_memory_space_constraint(array, pltpu.VMEM) for array in (grad, rows)), loss)
    return (loss.reshape(target), grad_table)


def solution(mesh):
    nv, nz, ng = mesh.shape["vocab"], mesh.shape["seq"], mesh.shape["grp"]
    cfg = (nv, nz, ng, NY, nv // (NY * NC))
    in_specs = (
        P("seq", None),
        P(("seq", "grp"), None),
        P(),
        P(None, "vocab"),
        P(None, "vocab"),
        P(None, "vocab"),
        P("vocab", None),
        P(("vocab", "seq", "grp"), None),
        P(),
        P(),
        P(),
    )
    out_specs = (P(), P(("vocab", "seq", "grp"), None))
    return jax.shard_map(
        functools.partial(body, cfg), mesh=mesh, in_specs=in_specs, out_specs=out_specs, check_vma=False
    )
```

```python
import functools
import math

import jax
import jax.numpy as jnp
from jax import lax
from jax.experimental import pallas as pl
from jax.experimental.pallas import tpu as pltpu
from jax.sharding import PartitionSpec as P

HEAD_DIM = 128
EPSILON = 1e-05
MESH = pl.DeviceIdType.MESH
NC = 2
NY = 4
NT = (((1,), (1,)), ((), ()))
F32, BF16 = jnp.float32, jnp.bfloat16


def front_kernel(
    cfg,
    src_len,
    tgt_len,
    dec_in,
    enc_in,
    gains_in,
    labels_in,
    wq_in,
    wk_in,
    wv_in,
    wo_in,
    emb_in,
    loss_out,
    grad_out,
    rows_out,
    gains,
    labels,
    dec,
    enc,
    wq,
    wkv,
    wo,
    emb,
    kv,
    ctx_own,
    ctx_got,
    part,
    summed,
    norm_stat,
    rows,
    logit,
    grad,
    local_stat,
    stat_x,
    stat_y,
    stat_z,
    load_sem,
    store_sem,
    kv_recv,
    a_recv,
    b_recv,
    c_recv,
    send_sem,
    recv_sem,
):
    nv, nz, ng, ny, nxl = cfg
    d = dec.shape[1]
    tz = dec.shape[0]
    ez = enc.shape[0]
    hd = wq.shape[1]
    tg = tz // ng
    ty = tg // ny
    width = d // (nxl * NC)
    wa, wb, wc = width // 4, width // 4, width // 2
    table_rows = emb.shape[0]
    nx = ng * nxl
    half = nz // 2

    v = lax.axis_index("vocab")
    z = lax.axis_index("seq")
    g = lax.axis_index("grp")
    c = v % NC
    y = (v // NC) % ny
    xl = v // (NC * ny)
    x = g * nxl + xl

    def vocab_of(xl_, y_, c_):
        return (xl_ * ny + y_) * NC + c_

    def at_x(x_, c_=None):
        return {"vocab": vocab_of(x_ % nxl, y, c if c_ is None else c_), "seq": z, "grp": x_ // nxl}

    def at_y(y_):
        return {"vocab": vocab_of(xl, y_, c), "seq": z, "grp": g}

    def at_z(z_):
        return {"vocab": v, "seq": z_, "grp": g}

    def at_v(v_):
        return {"vocab": v_, "seq": z, "grp": g}

    barrier = pltpu.get_barrier_semaphore()
    def far_first(n):
        return sorted(range(1, n), key=lambda o: -min(o, n - o))

    friends = [at_z((z + o) % nz) for o in far_first(nz)]
    friends += [{"vocab": v_, "seq": z, "grp": (g + o) % ng} for o in range(1, ng) for v_ in range(nv)]
    friends += [at_v((v + o) % nv) for o in range(1, nv)]

    loads = [
        pltpu.make_async_copy(src, dst, load_sem.at[i])
        for i, (src, dst) in enumerate(
            (
                (enc_in, enc),
                (wk_in, wkv.at[:, 0:hd]),
                (wv_in, wkv.at[:, hd : 2 * hd]),
                (dec_in, dec),
                (gains_in, gains),
                (wq_in, wq),
                (wo_in, wo),
                (labels_in, labels),
                (emb_in, emb),
            )
        )
    ]
    for load in loads[:6]:
        load.start()
    for friend in friends:
        pl.semaphore_signal(barrier, inc=1, device_id=friend, device_id_type=MESH)

    def remote(src, dst, out_sem, in_sem, device):
        return pltpu.make_async_remote_copy(
            src_ref=src, dst_ref=dst, send_sem=out_sem, recv_sem=in_sem, device_id=device, device_id_type=MESH
        )

    def arrived(ref, in_sem):
        remote(ref, ref, send_sem.at[0], in_sem, at_z((z + 1) % nz)).wait_recv()

    def left(ref, out_sem):
        remote(ref, ref, out_sem, recv_sem.at[0], at_z((z + 1) % nz)).wait_send()

    for load in loads[:3]:
        load.wait()
    for load in loads[6:]:
        load.start()
    own_kv = jnp.dot(enc[...], wkv[...], preferred_element_type=F32).astype(BF16)
    kv[z, 0] = own_kv[:, 0:hd]
    kv[z, 1] = own_kv[:, hd : 2 * hd]

    pl.semaphore_wait(barrier, len(friends))

    def kv_post(way, t, part_):
        step = (1, nz - 1)[way]
        ref = kv.at[(z + t * (nz - step)) % nz, part_]
        remote(ref, ref, send_sem.at[0], kv_recv.at[way, t, part_], at_z((z + step) % nz)).start()

    for part_ in (0, 1):
        for way in (0, 1):
            if half > 1:
                kv_post(way, 0, part_)
    for part_ in (0, 1):
        ref = kv.at[z, part_]
        remote(ref, ref, send_sem.at[0], kv_recv.at[0, half - 1, part_], at_z((z + half) % nz)).start()

    loads[3].wait()
    loads[4].wait()
    states = dec[...].astype(F32)
    centred = states - jnp.mean(states, axis=1, keepdims=True)
    variance = jnp.mean(centred * centred, axis=1, keepdims=True)
    normed = (centred * lax.rsqrt(variance + EPSILON) * gains[0:1, :]).astype(BF16)
    loads[5].wait()
    query = (jnp.dot(normed, wq[...], preferred_element_type=F32) * (1.0 / math.sqrt(hd))).astype(BF16)

    source_count = src_len[0]

    def scores_of(block):
        s = lax.dot_general(query, kv[block, 0], NT, preferred_element_type=F32)
        place = (block * ng + g) * ez + lax.broadcasted_iota(jnp.int32, s.shape, 1)
        valid = place < source_count
        return block, valid, jnp.where(valid, s, -1e30)

    scored = [scores_of(z)]
    for t in range(1, half + 1):
        for part_ in (0, 1):
            for way in (0, 1):
                if t < half or way == 0:
                    arrived(kv.at[(z + t * (nz - (1, nz - 1)[way])) % nz, part_], kv_recv.at[way, t - 1, part_])
                if t + 1 < half:
                    kv_post(way, t, part_)
        scored += [scores_of((z + o) % nz) for o in ((nz - t, t) if t < half else (half,))]
    top = functools.reduce(jnp.maximum, [s for _, _, s in scored])
    top = jnp.max(top, axis=1, keepdims=True)
    total = jnp.zeros((tz, ez), F32)
    acc = jnp.zeros((tz, hd), F32)
    for block, valid, s in scored:
        e = jnp.where(valid, jnp.exp(s - top), 0.0)
        total = total + e
        acc = acc + jnp.dot(e.astype(BF16), kv[block, 1], preferred_element_type=F32)
    total = jnp.sum(total, axis=1, keepdims=True)
    low = lax.broadcasted_iota(jnp.int32, (tz, 128), 1) < 64
    ctx_own[:, 0:hd] = acc
    ctx_own[:, hd : hd + 128] = jnp.where(low, top, total)
    remote(
        ctx_own.at[pl.ds(pl.multiple_of((1 - g) * tg, tg), tg)],
        ctx_got,
        send_sem.at[1],
        recv_sem.at[1],
        {"vocab": v, "seq": z, "grp": 1 - g},
    ).start()
    arrived(ctx_got, recv_sem.at[1])
    mine = ctx_own[pl.ds(pl.multiple_of(g * tg, tg), tg), :]
    other = ctx_got[...]
    top0, top1 = mine[:, hd : hd + 1], other[:, hd : hd + 1]
    both = jnp.maximum(top0, top1)
    f0, f1 = jnp.exp(top0 - both), jnp.exp(top1 - both)
    total = mine[:, hd + 64 : hd + 65] * f0 + other[:, hd + 64 : hd + 65] * f1
    context = ((mine[:, 0:hd] * f0 + other[:, 0:hd] * f1) / total).astype(BF16)

    def columns_of(xl_, c_):
        base = c_ * (d // NC)
        return (
            (base + xl_ * wa, wa),
            (base + nxl * wa + xl_ * wb, wb),
            (base + nxl * (wa + wb) + xl_ * wc, wc),
        )

    loads[6].wait()
    piece = xl * NC + c
    pieces = nxl * NC
    for op in [pieces // 2, *(o for o in range(pieces - 1, -1, -1) if o != pieces // 2)]:
        to_piece = (piece + op) % pieces
        weights = jnp.concatenate(
            [
                wo[:, pl.ds(pl.multiple_of(start, 128), size)]
                for start, size in columns_of(to_piece // NC, to_piece % NC)
            ],
            axis=1,
        )
        projected = jnp.dot(context, weights, preferred_element_type=F32).astype(BF16)
        for y_ in range(ny):
            part[vocab_of(to_piece // NC, y_, to_piece % NC)] = projected[y_ * ty : (y_ + 1) * ty]
        for oy in [*far_first(ny), 0]:
            if op + oy > 0:
                to = vocab_of(to_piece // NC, (y + oy) % ny, to_piece % NC)
                remote(part.at[to], summed.at[v], send_sem.at[2], recv_sem.at[2], at_v(to)).start()
    own_cols = [(pl.multiple_of(start, 128), size) for start, size in columns_of(xl, c)]
    own_row = pl.multiple_of(g * tg + y * ty, ty)
    hidden = part[v].astype(F32) + jnp.concatenate(
        [dec[pl.ds(own_row, ty), pl.ds(start, size)].astype(F32) for start, size in own_cols], axis=1
    )
    arrived(summed.at[0 : nv - 1], recv_sem.at[2])
    for o in range(1, nv):
        hidden = hidden + summed[(v + o) % nv].astype(F32)

    own_mean = jnp.mean(hidden, axis=1, keepdims=True)
    own_square = jnp.sum((hidden - own_mean) * (hidden - own_mean), axis=1, keepdims=True)
    low = lax.broadcasted_iota(jnp.int32, (ty, 128), 1) < 64
    norm_stat[piece] = jnp.where(low, own_mean, own_square)
    for o in range(1, pieces):
        to = (piece + o) % pieces
        remote(
            norm_stat.at[piece],
            norm_stat.at[piece],
            send_sem.at[3],
            recv_sem.at[3],
            at_v(vocab_of(to // NC, y, to % NC)),
        ).start()
    arrived(norm_stat.at[0 : pieces - 1], recv_sem.at[3])
    means = [norm_stat[i, :, 0:1] for i in range(pieces)]
    squares = [norm_stat[i, :, 64:65] for i in range(pieces)]
    mean = sum(means) * (1.0 / pieces)
    square = sum(squares) + width * sum((m - mean) * (m - mean) for m in means)
    scale = lax.rsqrt(square * (1.0 / d) + EPSILON)
    gain = jnp.concatenate([gains[1:2, pl.ds(start, size)] for start, size in own_cols], axis=1)
    final = ((hidden - mean) * scale * gain).astype(BF16)
    at = 0
    for start, size in own_cols:
        rows[z, g, y, :, pl.ds(start, size)] = final[:, at : at + size]
        at += size

    def cols_all(c_):
        base = pl.multiple_of(c_ * (d // NC), 128)
        return (
            pl.ds(base, nxl * wa),
            pl.ds(pl.multiple_of(base + nxl * wa, 128), nxl * wb),
            pl.ds(pl.multiple_of(base + nxl * (wa + wb), 128), nxl * wc),
        )

    def cols_piece(xl_):
        return [pl.ds(pl.multiple_of(start, 128), size) for start, size in columns_of(xl_, c)]

    _, own_b, own_c = cols_piece(xl)
    all_a, all_b, all_c = cols_all(c)

    def exchange(n, me, ref_of, out_sem, in_sem, device_of):
        ref = ref_of(me)
        for o in far_first(n):
            remote(ref, ref, out_sem, in_sem, device_of((me + o) % n)).start()

    swap = c

    def pick(here, there):
        return here + swap * (there - here)

    def place_b(i):
        return pick(x, i), pick(i, y)

    def place_c(i):
        return pick(i, x), pick(y, i)

    def at_xy(xy):
        return {"vocab": vocab_of(xy[0] % nxl, xy[1], c), "seq": z, "grp": xy[0] // nxl}

    def a1(xy):
        return rows.at[z, xy[0] // nxl, xy[1], :, cols_piece(xy[0] % nxl)[0]]

    def b1(z_):
        return rows.at[z_, g, y, :, own_b]

    def c1(z_):
        return rows.at[z_, g, y, :, own_c]

    def b2(xy):
        return rows.at[:, xy[0] // nxl, xy[1], :, cols_piece(xy[0] % nxl)[1]]

    def c2(xy):
        return rows.at[:, xy[0] // nxl, xy[1], :, cols_piece(xy[0] % nxl)[2]]

    def along_x(kind, x_):
        return rows.at[:, x_ // nxl, :, :, cols_piece(x_ % nxl)[kind]]

    def along_y(kind, y_):
        return rows.at[:, :, y_, :, cols_all(c)[kind]]

    all_a1 = rows.at[0, 0, 0, :, 0 : (nx * ny - 1) * wa]
    all_b1 = rows.at[0 : nz - 1, 0, 0, :, 0:wb]
    all_c1 = rows.at[0 : nz - 1, 0, 0, :, 0:wc]
    all_b2 = rows.at[:, 0, 0 : nx - 1, :, 0:wb]
    all_c2 = rows.at[:, 0, 0 : ny - 1, :, 0:wc]
    all_a3 = rows.at[0 : nz - 1, :, :, :, 0 : nxl * wa]
    all_b3 = rows.at[:, :, 0 : ny - 1, :, 0 : nxl * wb]
    all_c3 = rows.at[:, 0, :, :, 0 : (nx - 1) * wc]

    me_b, me_c = pick(y, x), pick(x, y)
    exchange(nz, z, c1, send_sem.at[6], recv_sem.at[6], at_z)
    exchange(nz, z, b1, send_sem.at[5], recv_sem.at[5], at_z)

    ref = a1((x, y))
    hops = [(min(o % nx, nx - o % nx) + min(o // nx, ny - o // nx), o) for o in range(1, nx * ny)]
    for _, o in sorted(hops, reverse=True):
        to = ((x + o) % nx, (y + o // nx) % ny)
        remote(ref, ref, send_sem.at[4], recv_sem.at[4], at_xy(to)).start()
    sibling = at_x(x, 1 - c)

    def share(kind, ref):
        remote(ref, ref, send_sem.at[12 + kind], recv_sem.at[7 + kind], sibling).start()

    def last(view, kind, n, me, in_sems, device_of):
        ref = view(kind, me)
        for o in far_first(n):
            remote(ref, ref, send_sem.at[9 + kind], in_sems.at[me], device_of((me + o) % n)).start()
        share(kind, ref)

    def last_in(view, kind, n, me, in_sems):
        for o in reversed(far_first(n)):
            ref = view(kind, (me + o) % n)
            arrived(ref, in_sems.at[(me + o) % n])
            share(kind, ref)

    def at_x_(i):
        return at_x(i)

    mid = nz // 2

    def half_x(i, part_):
        return rows.at[part_ * mid : (part_ + 1) * mid, i // nxl, :, :, cols_piece(i % nxl)[2]]

    def half_y(i, part_):
        return rows.at[part_ * mid : (part_ + 1) * mid, :, i, :, all_c]

    def relay_send(view, block, part_, sem, to, device_of):
        ref = view(block, part_)
        remote(ref, ref, send_sem.at[11], c_recv.at[sem], device_of(to)).start()

    def relay_get(view, block, part_, sem):
        ref = view(block, part_)
        arrived(ref, c_recv.at[sem])
        share(2, ref)

    def relay_start(view, me, device_of):
        for first in (0, 1):
            relay_send(view, me, first, first, (me + 1) % nx, device_of)
            relay_send(view, me, 1 - first, 3 - first, (me + nx - 1) % nx, device_of)
        for part_ in (0, 1):
            share(2, view(me, part_))

    def relay_pass(view, me, device_of):
        down, up = (me + nx - 1) % nx, (me + 1) % nx
        relay_get(view, down, 0, 0)
        relay_send(view, down, 0, 4, up, device_of)
        relay_get(view, up, 1, 3)
        relay_send(view, up, 1, 5, down, device_of)

    def relay_end(view, me):
        relay_get(view, (me + nx - 1) % nx, 1, 1)
        relay_get(view, (me + 1) % nx, 0, 2)
        relay_get(view, (me + 2) % nx, 0, 4)
        relay_get(view, (me + 2) % nx, 1, 5)

    def slab(kind, z_):
        return rows.at[z_, :, :, :, all_a]

    arrived(all_a1, recv_sem.at[4])
    last(slab, 0, nz, z, a_recv, at_z)
    arrived(all_c1, recv_sem.at[6])
    ref = c2((x, y))
    for o in far_first(nx):
        remote(ref, ref, send_sem.at[8], recv_sem.at[16], at_xy(place_b((me_b + o) % nx))).start()
    arrived(all_b1, recv_sem.at[5])
    ref = b2((x, y))
    for o in far_first(nx):
        remote(ref, ref, send_sem.at[7], recv_sem.at[15], at_xy(place_c((me_c + o) % nx))).start()
    arrived(all_c2, recv_sem.at[16])

    @pl.when(c == 0)
    def _():
        relay_start(half_x, x, at_x_)
        arrived(all_b2, recv_sem.at[15])
        last(along_y, 1, ny, y, b_recv, at_y)
        relay_pass(half_x, x, at_x_)
        last_in(along_y, 1, ny, y, b_recv)

    @pl.when(c == 1)
    def _():
        relay_start(half_y, y, at_y)
        arrived(all_b2, recv_sem.at[15])
        last(along_x, 1, nx, x, b_recv, at_x_)
        relay_pass(half_y, y, at_y)
        last_in(along_x, 1, nx, x, b_recv)

    last_in(slab, 0, nz, z, a_recv)
    their_a, their_b, their_c = cols_all(1 - c)
    arrived(rows.at[:, :, :, :, their_a], recv_sem.at[7])
    arrived(rows.at[:, :, :, :, their_b], recv_sem.at[8])
    loads[7].wait()
    loads[8].wait()
    table_base = ((v * nz + z) * ng + g) * table_rows
    step_blocks = max(1, 256 // tz)
    step_rows = step_blocks * tz
    early = nxl * (wa + wb)

    def logits_of(i, starts, size):
        total_ = None
        for start in starts:
            chunk = rows[pl.ds(i * step_blocks, step_blocks), :, :, :, start : start + size].reshape(step_rows, size)
            values = lax.dot_general(emb[:, start : start + size], chunk, NT, preferred_element_type=F32)
            total_ = values if total_ is None else total_ + values
        return total_

    def lanes_of(i):
        return pl.ds(pl.multiple_of(i * step_rows, 128), step_rows)

    def early_step(i, carry):
        logit[:, lanes_of(i)] = logits_of(i, range(0, d, d // NC), early)
        return carry

    steps = nz // step_blocks

    @pl.when(c == 0)
    def _():
        relay_end(half_x, x)

    @pl.when(c == 1)
    def _():
        relay_end(half_y, y)

    lax.fori_loop(0, steps, early_step, 0)
    arrived(rows.at[:, :, :, :, their_c], recv_sem.at[9])
    rows_store = pltpu.make_async_copy(rows, rows_out, store_sem.at[0])
    rows_store.start()

    for i in range(steps):
        lanes = pl.ds(i * step_rows, step_rows)
        values = logit[:, lanes] + logits_of(i, range(early, d, d // NC), d // NC - early)
        logit[:, lanes] = values
        top_ = jnp.max(values, axis=0, keepdims=True)
        total_ = jnp.sum(jnp.exp(values - top_), axis=0, keepdims=True)
        token = table_base + lax.broadcasted_iota(jnp.int32, values.shape, 0)
        local_stat[i, 0:1, :] = top_ + jnp.log(total_)
        local_stat[i, 1:2, :] = jnp.sum(jnp.where(token == labels[:, lanes], values, 0.0), axis=0, keepdims=True)

    stat_rows = nz * tz // 128
    per_step = step_rows // 128
    nxc = nx * NC
    xc = x * NC + c
    for r in range(stat_rows):
        for k in range(2):
            stat_x[xc, k * stat_rows + r : k * stat_rows + r + 1, :] = local_stat[
                r // per_step, k : k + 1, (r % per_step) * 128 : (r % per_step + 1) * 128
            ]

    def merge(ref, n):
        lses = [ref[i, 0:stat_rows] for i in range(n)]
        top_ = functools.reduce(jnp.maximum, lses)
        total_ = sum(jnp.exp(s - top_) for s in lses)
        return top_ + jnp.log(total_), sum(ref[i, stat_rows : 2 * stat_rows] for i in range(n))

    def stat_round(ref, n, me, k, device_of, meanwhile=None):
        exchange(n, me, lambda i: ref.at[i], send_sem.at[15 + k], recv_sem.at[10 + k], device_of)
        if meanwhile is not None:
            meanwhile()
        arrived(ref.at[0 : n - 1], recv_sem.at[10 + k])
        return merge(ref, n)

    lse, picked = stat_round(stat_x, nxc, xc, 0, lambda i: at_x(i // NC, i % NC))
    stat_y[y, 0:stat_rows] = lse
    stat_y[y, stat_rows : 2 * stat_rows] = picked
    lse, picked = stat_round(stat_y, ny, y, 1, at_y)
    stat_z[z, 0:stat_rows] = lse
    stat_z[z, stat_rows : 2 * stat_rows] = picked

    def settle():
        for i, ref in enumerate(
            (
                kv.at[0 : nz - 1],
                ctx_got,
                part.at[0 : nv - 1],
                norm_stat.at[0 : pieces - 1],
                all_a1,
                all_b1,
                all_c1,
                all_b2,
                all_c2,
                all_a3,
                all_b3,
                all_c3,
                rows.at[:, :, :, :, all_a],
                rows.at[:, :, :, :, all_b],
                rows.at[:, :, :, :, all_c],
                stat_x.at[0 : nxc - 1],
                stat_y.at[0 : ny - 1],
            )
        ):
            left(ref, send_sem.at[i])
        rows_store.wait()

    lse, picked = stat_round(stat_z, nz, z, 2, at_z, settle)

    place = lax.broadcasted_iota(jnp.int32, lse.shape, 0) * 128 + lax.broadcasted_iota(jnp.int32, lse.shape, 1)
    live = place < tgt_len[0]
    loss_out[...] = jnp.where(live, lse - picked, 0.0)
    lse = jnp.where(live, lse, 1e30)
    lse = jnp.concatenate([lse[r : r + 1, :] for r in range(stat_rows)], axis=1)
    place = lax.broadcasted_iota(jnp.int32, labels.shape, 1)
    hit = jnp.where(place < tgt_len[0], labels[...] - table_base, -1)

    def grad_step(i, carry):
        some = pl.ds(i * 128, 128)
        token = i * 128 + lax.broadcasted_iota(jnp.int32, (128, nz * tz), 0)
        grad[some, :] = (jnp.exp(logit[some, :] - lse) - jnp.where(token == hit, 1.0, 0.0)).astype(BF16)
        pltpu.make_async_copy(grad.at[some], grad_out.at[some], store_sem.at[1]).start()
        return carry

    lax.fori_loop(0, table_rows // 128, grad_step, 0)

    left(stat_z.at[0 : nz - 1], send_sem.at[17])
    pltpu.make_async_copy(grad, grad_out, store_sem.at[1]).wait()


def grad_kernel(tgt_len, grad, rows, loss, out, loss_out):
    loss_out[...] = loss[...]
    nz, block = rows.shape[0], out.shape[1]
    tz = grad.shape[1] // nz
    cols = pl.ds(pl.multiple_of(pl.program_id(0) * block, 128), block)
    step = max(1, 256 // tz)
    live = (tgt_len[0] + step * tz - 1) // (step * tz)
    for n in range(1, nz // step + 1):

        @pl.when(jnp.clip(live, 1, nz // step) == n)
        def _():
            count = n * step * tz
            chunk = rows[0 : n * step, :, :, :, cols].reshape(count, block)
            out[...] = jnp.dot(grad[:, 0:count], chunk, preferred_element_type=F32).astype(BF16)


def body(
    cfg,
    decoder_states,
    encoder_states,
    ln_gains,
    w_query,
    w_key,
    w_value,
    w_out,
    embedding,
    labels,
    src_length,
    tgt_length,
):
    nv, nz, ng, ny, nxl = cfg
    tz, d = decoder_states.shape
    ez = encoder_states.shape[0]
    hd = w_query.shape[1]
    table_rows = embedding.shape[0]
    target = labels.shape[0]
    tg = tz // ng
    ty = tg // ny
    width = d // (nxl * NC)
    nx = ng * nxl
    half = nz // 2
    pieces = nxl * NC
    step_blocks = max(1, 256 // tz)
    stat_rows = target // 128
    hbm = pl.BlockSpec(memory_space=pl.ANY)
    vmem = pl.BlockSpec(memory_space=pltpu.VMEM)
    smem = pl.BlockSpec(memory_space=pltpu.SMEM)
    dma = pltpu.SemaphoreType.DMA
    far = [
        pltpu.with_memory_space_constraint(array, pltpu.HBM)
        for array in (
            decoder_states,
            encoder_states,
            ln_gains,
            labels.reshape(1, target),
            w_query,
            w_key,
            w_value,
            w_out,
            embedding,
        )
    ]
    loss, grad, rows = pl.pallas_call(
        functools.partial(front_kernel, cfg),
        out_shape=(
            jax.ShapeDtypeStruct((stat_rows, 128), F32),
            pltpu.VMEM((table_rows, target), BF16),
            pltpu.VMEM((nz, ng, ny, ty, d), BF16),
        ),
        in_specs=[smem, smem] + [hbm] * len(far),
        out_specs=(vmem, hbm, hbm),
        scratch_shapes=[
            pltpu.VMEM(ln_gains.shape, F32),
            pltpu.VMEM((1, target), jnp.int32),
            pltpu.VMEM((tz, d), BF16),
            pltpu.VMEM((ez, d), BF16),
            pltpu.VMEM((d, hd), BF16),
            pltpu.VMEM((d, 2 * hd), BF16),
            pltpu.VMEM((hd, d), BF16),
            pltpu.VMEM((table_rows, d), BF16),
            pltpu.VMEM((nz, 2, ez, hd), BF16),
            pltpu.VMEM((tz, hd + 128), F32),
            pltpu.VMEM((tg, hd + 128), F32),
            pltpu.VMEM((nv, ty, width), BF16),
            pltpu.VMEM((nv, ty, width), BF16),
            pltpu.VMEM((pieces, ty, 128), F32),
            pltpu.VMEM((nz, ng, ny, ty, d), BF16),
            pltpu.VMEM((table_rows, target), F32),
            pltpu.VMEM((table_rows, target), BF16),
            pltpu.VMEM((nz // step_blocks, 8, step_blocks * tz), F32),
            pltpu.VMEM((nx * NC, 2 * stat_rows, 128), F32),
            pltpu.VMEM((ny, 2 * stat_rows, 128), F32),
            pltpu.VMEM((nz, 2 * stat_rows, 128), F32),
            dma((9,)),
            dma((2,)),
            dma((2, half, 2)),
            dma((nz,)),
            dma((ny,)),
            dma((6,)),
            dma((18,)),
            dma((17,)),
        ],
        compiler_params=pltpu.CompilerParams(
            collective_id=0, has_side_effects=True, vmem_limit_bytes=40 * 1024 * 1024
        ),
    )(src_length, tgt_length, *far)
    block = 512
    grad_table, loss = pl.pallas_call(
        grad_kernel,
        out_shape=(jax.ShapeDtypeStruct((table_rows, d), BF16), jax.ShapeDtypeStruct(loss.shape, F32)),
        grid=(d // block,),
        in_specs=[smem, vmem, vmem, vmem],
        out_specs=(pl.BlockSpec((table_rows, block), lambda i: (0, i)), pl.BlockSpec(loss.shape, lambda i: (0, 0))),
        compiler_params=pltpu.CompilerParams(vmem_limit_bytes=24 * 1024 * 1024),
    )(tgt_length, *(pltpu.with_memory_space_constraint(array, pltpu.VMEM) for array in (grad, rows)), loss)
    return (loss.reshape(target), grad_table)


def solution(mesh):
    nv, nz, ng = mesh.shape["vocab"], mesh.shape["seq"], mesh.shape["grp"]
    cfg = (nv, nz, ng, NY, nv // (NY * NC))
    in_specs = (
        P("seq", None),
        P(("seq", "grp"), None),
        P(),
        P(None, "vocab"),
        P(None, "vocab"),
        P(None, "vocab"),
        P("vocab", None),
        P(("vocab", "seq", "grp"), None),
        P(),
        P(),
        P(),
    )
    out_specs = (P(), P(("vocab", "seq", "grp"), None))
    return jax.shard_map(
        functools.partial(body, cfg), mesh=mesh, in_specs=in_specs, out_specs=out_specs, check_vma=False
    )
```

```python
import functools
import math

import jax
import jax.numpy as jnp
from jax import lax
from jax.experimental import pallas as pl
from jax.experimental.pallas import tpu as pltpu
from jax.sharding import PartitionSpec as P

HEAD_DIM = 128
EPSILON = 1e-05
MESH = pl.DeviceIdType.MESH
NC = 2
NY = 4
NT = (((1,), (1,)), ((), ()))
F32, BF16 = jnp.float32, jnp.bfloat16


def front_kernel(
    cfg,
    src_len,
    tgt_len,
    dec_in,
    enc_in,
    gains_in,
    labels_in,
    wq_in,
    wk_in,
    wv_in,
    wo_in,
    emb_in,
    loss_out,
    grad_out,
    rows_out,
    gains,
    labels,
    dec,
    enc,
    wq,
    wkv,
    wo,
    emb,
    kv,
    ctx_own,
    ctx_got,
    part,
    summed,
    norm_stat,
    rows,
    logit,
    grad,
    local_stat,
    stat_x,
    stat_y,
    stat_z,
    load_sem,
    store_sem,
    kv_recv,
    a_recv,
    b_recv,
    c_recv,
    send_sem,
    recv_sem,
):
    nv, nz, ng, ny, nxl = cfg
    d = dec.shape[1]
    tz = dec.shape[0]
    ez = enc.shape[0]
    hd = wq.shape[1]
    tg = tz // ng
    ty = tg // ny
    width = d // (nxl * NC)
    wa, wb, wc = width // 4, width // 4, width // 2
    table_rows = emb.shape[0]
    nx = ng * nxl
    half = nz // 2

    v = lax.axis_index("vocab")
    z = lax.axis_index("seq")
    g = lax.axis_index("grp")
    c = v % NC
    y = (v // NC) % ny
    xl = v // (NC * ny)
    x = g * nxl + xl

    def vocab_of(xl_, y_, c_):
        return (xl_ * ny + y_) * NC + c_

    def at_x(x_, c_=None):
        return {"vocab": vocab_of(x_ % nxl, y, c if c_ is None else c_), "seq": z, "grp": x_ // nxl}

    def at_y(y_):
        return {"vocab": vocab_of(xl, y_, c), "seq": z, "grp": g}

    def at_z(z_):
        return {"vocab": v, "seq": z_, "grp": g}

    def at_v(v_):
        return {"vocab": v_, "seq": z, "grp": g}

    barrier = pltpu.get_barrier_semaphore()
    def far_first(n):
        return sorted(range(1, n), key=lambda o: -min(o, n - o))

    friends = [at_z((z + o) % nz) for o in far_first(nz)]
    friends += [{"vocab": v_, "seq": z, "grp": (g + o) % ng} for o in range(1, ng) for v_ in range(nv)]
    friends += [at_v((v + o) % nv) for o in range(1, nv)]

    loads = [
        pltpu.make_async_copy(src, dst, load_sem.at[i])
        for i, (src, dst) in enumerate(
            (
                (enc_in, enc),
                (wk_in, wkv.at[:, 0:hd]),
                (wv_in, wkv.at[:, hd : 2 * hd]),
                (dec_in, dec),
                (gains_in, gains),
                (wq_in, wq),
                (wo_in, wo),
                (labels_in, labels),
                (emb_in, emb),
            )
        )
    ]
    for load in loads[:6]:
        load.start()
    for friend in friends:
        pl.semaphore_signal(barrier, inc=1, device_id=friend, device_id_type=MESH)

    def remote(src, dst, out_sem, in_sem, device):
        return pltpu.make_async_remote_copy(
            src_ref=src, dst_ref=dst, send_sem=out_sem, recv_sem=in_sem, device_id=device, device_id_type=MESH
        )

    def arrived(ref, in_sem):
        remote(ref, ref, send_sem.at[0], in_sem, at_z((z + 1) % nz)).wait_recv()

    def left(ref, out_sem):
        remote(ref, ref, out_sem, recv_sem.at[0], at_z((z + 1) % nz)).wait_send()

    for load in loads[:3]:
        load.wait()
    for load in loads[6:]:
        load.start()
    own_kv = jnp.dot(enc[...], wkv[...], preferred_element_type=F32).astype(BF16)
    kv[z, 0] = own_kv[:, 0:hd]
    kv[z, 1] = own_kv[:, hd : 2 * hd]

    pl.semaphore_wait(barrier, len(friends))

    def kv_post(way, t, part_):
        step = (1, nz - 1)[way]
        ref = kv.at[(z + t * (nz - step)) % nz, part_]
        remote(ref, ref, send_sem.at[0], kv_recv.at[way, t, part_], at_z((z + step) % nz)).start()

    for part_ in (0, 1):
        for way in (0, 1):
            if half > 1:
                kv_post(way, 0, part_)
    for part_ in (0, 1):
        ref = kv.at[z, part_]
        remote(ref, ref, send_sem.at[0], kv_recv.at[0, half - 1, part_], at_z((z + half) % nz)).start()

    loads[3].wait()
    loads[4].wait()
    states = dec[...].astype(F32)
    centred = states - jnp.mean(states, axis=1, keepdims=True)
    variance = jnp.mean(centred * centred, axis=1, keepdims=True)
    normed = (centred * lax.rsqrt(variance + EPSILON) * gains[0:1, :]).astype(BF16)
    loads[5].wait()
    query = (jnp.dot(normed, wq[...], preferred_element_type=F32) * (1.0 / math.sqrt(hd))).astype(BF16)

    source_count = src_len[0]

    def scores_of(block):
        s = lax.dot_general(query, kv[block, 0], NT, preferred_element_type=F32)
        place = (block * ng + g) * ez + lax.broadcasted_iota(jnp.int32, s.shape, 1)
        valid = place < source_count
        return block, valid, jnp.where(valid, s, -1e30)

    scored = [scores_of(z)]
    for t in range(1, half + 1):
        for part_ in (0, 1):
            for way in (0, 1):
                if t < half or way == 0:
                    arrived(kv.at[(z + t * (nz - (1, nz - 1)[way])) % nz, part_], kv_recv.at[way, t - 1, part_])
                if t + 1 < half:
                    kv_post(way, t, part_)
        scored += [scores_of((z + o) % nz) for o in ((nz - t, t) if t < half else (half,))]
    top = functools.reduce(jnp.maximum, [s for _, _, s in scored])
    top = jnp.max(top, axis=1, keepdims=True)
    total = jnp.zeros((tz, ez), F32)
    acc = jnp.zeros((tz, hd), F32)
    for block, valid, s in scored:
        e = jnp.where(valid, jnp.exp(s - top), 0.0)
        total = total + e
        acc = acc + jnp.dot(e.astype(BF16), kv[block, 1], preferred_element_type=F32)
    total = jnp.sum(total, axis=1, keepdims=True)
    low = lax.broadcasted_iota(jnp.int32, (tz, 128), 1) < 64
    ctx_own[:, 0:hd] = acc
    ctx_own[:, hd : hd + 128] = jnp.where(low, top, total)
    remote(
        ctx_own.at[pl.ds(pl.multiple_of((1 - g) * tg, tg), tg)],
        ctx_got,
        send_sem.at[1],
        recv_sem.at[1],
        {"vocab": v, "seq": z, "grp": 1 - g},
    ).start()
    arrived(ctx_got, recv_sem.at[1])
    mine = ctx_own[pl.ds(pl.multiple_of(g * tg, tg), tg), :]
    other = ctx_got[...]
    top0, top1 = mine[:, hd : hd + 1], other[:, hd : hd + 1]
    both = jnp.maximum(top0, top1)
    f0, f1 = jnp.exp(top0 - both), jnp.exp(top1 - both)
    total = mine[:, hd + 64 : hd + 65] * f0 + other[:, hd + 64 : hd + 65] * f1
    context = ((mine[:, 0:hd] * f0 + other[:, 0:hd] * f1) / total).astype(BF16)

    def columns_of(xl_, c_):
        base = c_ * (d // NC)
        return (
            (base + xl_ * wa, wa),
            (base + nxl * wa + xl_ * wb, wb),
            (base + nxl * (wa + wb) + xl_ * wc, wc),
        )

    loads[6].wait()
    piece = xl * NC + c
    pieces = nxl * NC
    for op in [pieces // 2, *(o for o in range(pieces - 1, -1, -1) if o != pieces // 2)]:
        to_piece = (piece + op) % pieces
        weights = jnp.concatenate(
            [
                wo[:, pl.ds(pl.multiple_of(start, 128), size)]
                for start, size in columns_of(to_piece // NC, to_piece % NC)
            ],
            axis=1,
        )
        projected = jnp.dot(context, weights, preferred_element_type=F32).astype(BF16)
        for y_ in range(ny):
            part[vocab_of(to_piece // NC, y_, to_piece % NC)] = projected[y_ * ty : (y_ + 1) * ty]
        for oy in [*far_first(ny), 0]:
            if op + oy > 0:
                to = vocab_of(to_piece // NC, (y + oy) % ny, to_piece % NC)
                remote(part.at[to], summed.at[v], send_sem.at[2], recv_sem.at[2], at_v(to)).start()
    own_cols = [(pl.multiple_of(start, 128), size) for start, size in columns_of(xl, c)]
    own_row = pl.multiple_of(g * tg + y * ty, ty)
    hidden = part[v].astype(F32) + jnp.concatenate(
        [dec[pl.ds(own_row, ty), pl.ds(start, size)].astype(F32) for start, size in own_cols], axis=1
    )
    arrived(summed.at[0 : nv - 1], recv_sem.at[2])
    for o in range(1, nv):
        hidden = hidden + summed[(v + o) % nv].astype(F32)

    own_mean = jnp.mean(hidden, axis=1, keepdims=True)
    own_square = jnp.sum((hidden - own_mean) * (hidden - own_mean), axis=1, keepdims=True)
    low = lax.broadcasted_iota(jnp.int32, (ty, 128), 1) < 64
    norm_stat[piece] = jnp.where(low, own_mean, own_square)
    for o in range(1, pieces):
        to = (piece + o) % pieces
        remote(
            norm_stat.at[piece],
            norm_stat.at[piece],
            send_sem.at[3],
            recv_sem.at[3],
            at_v(vocab_of(to // NC, y, to % NC)),
        ).start()
    arrived(norm_stat.at[0 : pieces - 1], recv_sem.at[3])
    means = [norm_stat[i, :, 0:1] for i in range(pieces)]
    squares = [norm_stat[i, :, 64:65] for i in range(pieces)]
    mean = sum(means) * (1.0 / pieces)
    square = sum(squares) + width * sum((m - mean) * (m - mean) for m in means)
    scale = lax.rsqrt(square * (1.0 / d) + EPSILON)
    gain = jnp.concatenate([gains[1:2, pl.ds(start, size)] for start, size in own_cols], axis=1)
    final = ((hidden - mean) * scale * gain).astype(BF16)
    at = 0
    for start, size in own_cols:
        rows[z, g, y, :, pl.ds(start, size)] = final[:, at : at + size]
        at += size

    def cols_all(c_):
        base = pl.multiple_of(c_ * (d // NC), 128)
        return (
            pl.ds(base, nxl * wa),
            pl.ds(pl.multiple_of(base + nxl * wa, 128), nxl * wb),
            pl.ds(pl.multiple_of(base + nxl * (wa + wb), 128), nxl * wc),
        )

    def cols_piece(xl_):
        return [pl.ds(pl.multiple_of(start, 128), size) for start, size in columns_of(xl_, c)]

    _, own_b, own_c = cols_piece(xl)
    all_a, all_b, all_c = cols_all(c)

    def exchange(n, me, ref_of, out_sem, in_sem, device_of):
        ref = ref_of(me)
        for o in far_first(n):
            remote(ref, ref, out_sem, in_sem, device_of((me + o) % n)).start()

    swap = c

    def pick(here, there):
        return here + swap * (there - here)

    def place_b(i):
        return pick(x, i), pick(i, y)

    def place_c(i):
        return pick(i, x), pick(y, i)

    def at_xy(xy):
        return {"vocab": vocab_of(xy[0] % nxl, xy[1], c), "seq": z, "grp": xy[0] // nxl}

    def a1(xy):
        return rows.at[z, xy[0] // nxl, xy[1], :, cols_piece(xy[0] % nxl)[0]]

    def b1(z_):
        return rows.at[z_, g, y, :, own_b]

    def c1(z_):
        return rows.at[z_, g, y, :, own_c]

    def b2(xy):
        return rows.at[:, xy[0] // nxl, xy[1], :, cols_piece(xy[0] % nxl)[1]]

    def c2(xy):
        return rows.at[:, xy[0] // nxl, xy[1], :, cols_piece(xy[0] % nxl)[2]]

    def along_x(kind, x_):
        return rows.at[:, x_ // nxl, :, :, cols_piece(x_ % nxl)[kind]]

    def along_y(kind, y_):
        return rows.at[:, :, y_, :, cols_all(c)[kind]]

    all_a1 = rows.at[0, 0, 0, :, 0 : (nx * ny - 1) * wa]
    all_b1 = rows.at[0 : nz - 1, 0, 0, :, 0:wb]
    all_c1 = rows.at[0 : nz - 1, 0, 0, :, 0:wc]
    all_b2 = rows.at[:, 0, 0 : nx - 1, :, 0:wb]
    all_c2 = rows.at[:, 0, 0 : ny - 1, :, 0:wc]
    all_a3 = rows.at[0 : nz - 1, :, :, :, 0 : nxl * wa]
    all_b3 = rows.at[:, :, 0 : ny - 1, :, 0 : nxl * wb]
    all_c3 = rows.at[:, 0, :, :, 0 : (nx - 1) * wc]

    me_b, me_c = pick(y, x), pick(x, y)
    exchange(nz, z, c1, send_sem.at[6], recv_sem.at[6], at_z)
    exchange(nz, z, b1, send_sem.at[5], recv_sem.at[5], at_z)

    ref = a1((x, y))
    hops = [(min(o % nx, nx - o % nx) + min(o // nx, ny - o // nx), o) for o in range(1, nx * ny)]
    for _, o in sorted(hops, reverse=True):
        to = ((x + o) % nx, (y + o // nx) % ny)
        remote(ref, ref, send_sem.at[4], recv_sem.at[4], at_xy(to)).start()
    sibling = at_x(x, 1 - c)

    def share(kind, ref):
        remote(ref, ref, send_sem.at[12 + kind], recv_sem.at[7 + kind], sibling).start()

    def last(view, kind, n, me, in_sems, device_of):
        ref = view(kind, me)
        for o in far_first(n):
            remote(ref, ref, send_sem.at[9 + kind], in_sems.at[me], device_of((me + o) % n)).start()
        share(kind, ref)

    def last_in(view, kind, n, me, in_sems):
        for o in reversed(far_first(n)):
            ref = view(kind, (me + o) % n)
            arrived(ref, in_sems.at[(me + o) % n])
            share(kind, ref)

    def at_x_(i):
        return at_x(i)

    mid = nz // 2

    def half_x(i, part_):
        return rows.at[part_ * mid : (part_ + 1) * mid, i // nxl, :, :, cols_piece(i % nxl)[2]]

    def half_y(i, part_):
        return rows.at[part_ * mid : (part_ + 1) * mid, :, i, :, all_c]

    def relay_send(view, block, part_, sem, to, device_of):
        ref = view(block, part_)
        remote(ref, ref, send_sem.at[11], c_recv.at[sem], device_of(to)).start()

    def relay_get(view, block, part_, sem):
        ref = view(block, part_)
        arrived(ref, c_recv.at[sem])
        share(2, ref)

    def relay_start(view, me, device_of):
        for first in (0, 1):
            relay_send(view, me, first, first, (me + 1) % nx, device_of)
            relay_send(view, me, 1 - first, 3 - first, (me + nx - 1) % nx, device_of)
        for part_ in (0, 1):
            share(2, view(me, part_))

    def relay_pass(view, me, device_of):
        down, up = (me + nx - 1) % nx, (me + 1) % nx
        relay_get(view, down, 0, 0)
        relay_send(view, down, 0, 4, up, device_of)
        relay_get(view, up, 1, 3)
        relay_send(view, up, 1, 5, down, device_of)

    def relay_end(view, me):
        relay_get(view, (me + nx - 1) % nx, 1, 1)
        relay_get(view, (me + 1) % nx, 0, 2)
        relay_get(view, (me + 2) % nx, 0, 4)
        relay_get(view, (me + 2) % nx, 1, 5)

    def slab(kind, z_):
        return rows.at[z_, :, :, :, all_a]

    arrived(all_a1, recv_sem.at[4])
    last(slab, 0, nz, z, a_recv, at_z)
    arrived(all_c1, recv_sem.at[6])
    ref = c2((x, y))
    for o in far_first(nx):
        remote(ref, ref, send_sem.at[8], recv_sem.at[16], at_xy(place_b((me_b + o) % nx))).start()
    arrived(all_b1, recv_sem.at[5])
    ref = b2((x, y))
    for o in far_first(nx):
        remote(ref, ref, send_sem.at[7], recv_sem.at[15], at_xy(place_c((me_c + o) % nx))).start()
    arrived(all_c2, recv_sem.at[16])

    @pl.when(c == 0)
    def _():
        relay_start(half_x, x, at_x_)
        arrived(all_b2, recv_sem.at[15])
        last(along_y, 1, ny, y, b_recv, at_y)
        relay_pass(half_x, x, at_x_)
        last_in(along_y, 1, ny, y, b_recv)

    @pl.when(c == 1)
    def _():
        relay_start(half_y, y, at_y)
        arrived(all_b2, recv_sem.at[15])
        last(along_x, 1, nx, x, b_recv, at_x_)
        relay_pass(half_y, y, at_y)
        last_in(along_x, 1, nx, x, b_recv)

    last_in(slab, 0, nz, z, a_recv)
    their_a, their_b, their_c = cols_all(1 - c)
    arrived(rows.at[:, :, :, :, their_a], recv_sem.at[7])
    arrived(rows.at[:, :, :, :, their_b], recv_sem.at[8])
    loads[7].wait()
    loads[8].wait()
    table_base = ((v * nz + z) * ng + g) * table_rows
    step_blocks = max(1, 256 // tz)
    step_rows = step_blocks * tz
    early = nxl * (wa + wb)

    def logits_of(i, starts, size):
        total_ = None
        for start in starts:
            chunk = rows[pl.ds(i * step_blocks, step_blocks), :, :, :, start : start + size].reshape(step_rows, size)
            values = lax.dot_general(emb[:, start : start + size], chunk, NT, preferred_element_type=F32)
            total_ = values if total_ is None else total_ + values
        return total_

    def lanes_of(i):
        return pl.ds(pl.multiple_of(i * step_rows, 128), step_rows)

    def early_step(i, carry):
        logit[:, lanes_of(i)] = logits_of(i, range(0, d, d // NC), early)
        return carry

    steps = nz // step_blocks

    @pl.when(c == 0)
    def _():
        relay_end(half_x, x)

    @pl.when(c == 1)
    def _():
        relay_end(half_y, y)

    lax.fori_loop(0, steps, early_step, 0)
    arrived(rows.at[:, :, :, :, their_c], recv_sem.at[9])
    rows_store = pltpu.make_async_copy(rows, rows_out, store_sem.at[0])
    rows_store.start()

    for i in range(steps):
        lanes = pl.ds(i * step_rows, step_rows)
        values = logit[:, lanes] + logits_of(i, range(early, d, d // NC), d // NC - early)
        logit[:, lanes] = values
        top_ = jnp.max(values, axis=0, keepdims=True)
        total_ = jnp.sum(jnp.exp(values - top_), axis=0, keepdims=True)
        token = table_base + lax.broadcasted_iota(jnp.int32, values.shape, 0)
        local_stat[i, 0:1, :] = top_ + jnp.log(total_)
        local_stat[i, 1:2, :] = jnp.sum(jnp.where(token == labels[:, lanes], values, 0.0), axis=0, keepdims=True)

    stat_rows = nz * tz // 128
    per_step = step_rows // 128
    nxc = nx * NC
    xc = x * NC + c
    for r in range(stat_rows):
        for k in range(2):
            stat_x[xc, k * stat_rows + r : k * stat_rows + r + 1, :] = local_stat[
                r // per_step, k : k + 1, (r % per_step) * 128 : (r % per_step + 1) * 128
            ]

    low_rows, high_rows = pl.ds(0, stat_rows), pl.ds(stat_rows, stat_rows)
    rounds = (
        (stat_x, nxc, xc, lambda i: at_x(i // NC, i % NC)),
        (stat_y, ny, y, at_y),
        (stat_z, nz, z, at_z),
    )

    def stat_send(k, some, out_sem, in_sem):
        ref, n, me, device_of = rounds[k]
        exchange(n, me, lambda i: ref.at[i, some], send_sem.at[out_sem + k], recv_sem.at[in_sem + k], device_of)

    def picked_of(k):
        ref, n = rounds[k][:2]
        arrived(ref.at[0 : n - 1, high_rows], recv_sem.at[17 + k])
        return sum(ref[i, stat_rows : 2 * stat_rows] for i in range(n))

    def settle():
        for i, ref in enumerate(
            (
                kv.at[0 : nz - 1],
                ctx_got,
                part.at[0 : nv - 1],
                norm_stat.at[0 : pieces - 1],
                all_a1,
                all_b1,
                all_c1,
                all_b2,
                all_c2,
                all_a3,
                all_b3,
                all_c3,
                rows.at[:, :, :, :, all_a],
                rows.at[:, :, :, :, all_b],
                rows.at[:, :, :, :, all_c],
            )
        ):
            left(ref, send_sem.at[i])
        for k, (ref, n, _, _) in enumerate(rounds[:2]):
            left(ref.at[0 : n - 1, low_rows], send_sem.at[15 + k])
            left(ref.at[0 : n - 1, high_rows], send_sem.at[18 + k])
        rows_store.wait()

    for k, (ref, n, me, _) in enumerate(rounds):
        if k > 0:
            ref[me, 0:stat_rows] = lse
        stat_send(k, low_rows, 15, 10)
        if k > 0:
            ref[me, stat_rows : 2 * stat_rows] = picked_of(k - 1)
        stat_send(k, high_rows, 18, 17)
        if k == 2:
            settle()
        arrived(ref.at[0 : n - 1, low_rows], recv_sem.at[10 + k])
        lses = [ref[i, 0:stat_rows] for i in range(n)]
        top_ = functools.reduce(jnp.maximum, lses)
        lse = top_ + jnp.log(sum(jnp.exp(s - top_) for s in lses))

    place = lax.broadcasted_iota(jnp.int32, lse.shape, 0) * 128 + lax.broadcasted_iota(jnp.int32, lse.shape, 1)
    live = place < tgt_len[0]
    row_lse = lse
    lse = jnp.where(live, lse, 1e30)
    lse = jnp.concatenate([lse[r : r + 1, :] for r in range(stat_rows)], axis=1)
    place = lax.broadcasted_iota(jnp.int32, labels.shape, 1)
    hit = jnp.where(place < tgt_len[0], labels[...] - table_base, -1)

    def grad_step(i, carry):
        some = pl.ds(i * 128, 128)
        token = i * 128 + lax.broadcasted_iota(jnp.int32, (128, nz * tz), 0)
        grad[some, :] = (jnp.exp(logit[some, :] - lse) - jnp.where(token == hit, 1.0, 0.0)).astype(BF16)
        pltpu.make_async_copy(grad.at[some], grad_out.at[some], store_sem.at[1]).start()
        return carry

    lax.fori_loop(0, table_rows // 128, grad_step, 0)

    loss_out[...] = jnp.where(live, row_lse - picked_of(2), 0.0)
    left(stat_z.at[0 : nz - 1, low_rows], send_sem.at[17])
    left(stat_z.at[0 : nz - 1, high_rows], send_sem.at[20])
    pltpu.make_async_copy(grad, grad_out, store_sem.at[1]).wait()


def grad_kernel(tgt_len, grad, rows, loss, out, loss_out):
    loss_out[...] = loss[...]
    nz, block = rows.shape[0], out.shape[1]
    tz = grad.shape[1] // nz
    cols = pl.ds(pl.multiple_of(pl.program_id(0) * block, 128), block)
    step = max(1, 256 // tz)
    live = (tgt_len[0] + step * tz - 1) // (step * tz)
    for n in range(1, nz // step + 1):

        @pl.when(jnp.clip(live, 1, nz // step) == n)
        def _():
            count = n * step * tz
            chunk = rows[0 : n * step, :, :, :, cols].reshape(count, block)
            out[...] = jnp.dot(grad[:, 0:count], chunk, preferred_element_type=F32).astype(BF16)


def body(
    cfg,
    decoder_states,
    encoder_states,
    ln_gains,
    w_query,
    w_key,
    w_value,
    w_out,
    embedding,
    labels,
    src_length,
    tgt_length,
):
    nv, nz, ng, ny, nxl = cfg
    tz, d = decoder_states.shape
    ez = encoder_states.shape[0]
    hd = w_query.shape[1]
    table_rows = embedding.shape[0]
    target = labels.shape[0]
    tg = tz // ng
    ty = tg // ny
    width = d // (nxl * NC)
    nx = ng * nxl
    half = nz // 2
    pieces = nxl * NC
    step_blocks = max(1, 256 // tz)
    stat_rows = target // 128
    hbm = pl.BlockSpec(memory_space=pl.ANY)
    vmem = pl.BlockSpec(memory_space=pltpu.VMEM)
    smem = pl.BlockSpec(memory_space=pltpu.SMEM)
    dma = pltpu.SemaphoreType.DMA
    far = [
        pltpu.with_memory_space_constraint(array, pltpu.HBM)
        for array in (
            decoder_states,
            encoder_states,
            ln_gains,
            labels.reshape(1, target),
            w_query,
            w_key,
            w_value,
            w_out,
            embedding,
        )
    ]
    loss, grad, rows = pl.pallas_call(
        functools.partial(front_kernel, cfg),
        out_shape=(
            jax.ShapeDtypeStruct((stat_rows, 128), F32),
            pltpu.VMEM((table_rows, target), BF16),
            pltpu.VMEM((nz, ng, ny, ty, d), BF16),
        ),
        in_specs=[smem, smem] + [hbm] * len(far),
        out_specs=(vmem, hbm, hbm),
        scratch_shapes=[
            pltpu.VMEM(ln_gains.shape, F32),
            pltpu.VMEM((1, target), jnp.int32),
            pltpu.VMEM((tz, d), BF16),
            pltpu.VMEM((ez, d), BF16),
            pltpu.VMEM((d, hd), BF16),
            pltpu.VMEM((d, 2 * hd), BF16),
            pltpu.VMEM((hd, d), BF16),
            pltpu.VMEM((table_rows, d), BF16),
            pltpu.VMEM((nz, 2, ez, hd), BF16),
            pltpu.VMEM((tz, hd + 128), F32),
            pltpu.VMEM((tg, hd + 128), F32),
            pltpu.VMEM((nv, ty, width), BF16),
            pltpu.VMEM((nv, ty, width), BF16),
            pltpu.VMEM((pieces, ty, 128), F32),
            pltpu.VMEM((nz, ng, ny, ty, d), BF16),
            pltpu.VMEM((table_rows, target), F32),
            pltpu.VMEM((table_rows, target), BF16),
            pltpu.VMEM((nz // step_blocks, 8, step_blocks * tz), F32),
            pltpu.VMEM((nx * NC, 2 * stat_rows, 128), F32),
            pltpu.VMEM((ny, 2 * stat_rows, 128), F32),
            pltpu.VMEM((nz, 2 * stat_rows, 128), F32),
            dma((9,)),
            dma((2,)),
            dma((2, half, 2)),
            dma((nz,)),
            dma((ny,)),
            dma((6,)),
            dma((21,)),
            dma((20,)),
        ],
        compiler_params=pltpu.CompilerParams(
            collective_id=0, has_side_effects=True, vmem_limit_bytes=40 * 1024 * 1024
        ),
    )(src_length, tgt_length, *far)
    block = 512
    grad_table, loss = pl.pallas_call(
        grad_kernel,
        out_shape=(jax.ShapeDtypeStruct((table_rows, d), BF16), jax.ShapeDtypeStruct(loss.shape, F32)),
        grid=(d // block,),
        in_specs=[smem, vmem, vmem, vmem],
        out_specs=(pl.BlockSpec((table_rows, block), lambda i: (0, i)), pl.BlockSpec(loss.shape, lambda i: (0, 0))),
        compiler_params=pltpu.CompilerParams(vmem_limit_bytes=24 * 1024 * 1024),
    )(tgt_length, *(pltpu.with_memory_space_constraint(array, pltpu.VMEM) for array in (grad, rows)), loss)
    return (loss.reshape(target), grad_table)


def solution(mesh):
    nv, nz, ng = mesh.shape["vocab"], mesh.shape["seq"], mesh.shape["grp"]
    cfg = (nv, nz, ng, NY, nv // (NY * NC))
    in_specs = (
        P("seq", None),
        P(("seq", "grp"), None),
        P(),
        P(None, "vocab"),
        P(None, "vocab"),
        P(None, "vocab"),
        P("vocab", None),
        P(("vocab", "seq", "grp"), None),
        P(),
        P(),
        P(),
    )
    out_specs = (P(), P(("vocab", "seq", "grp"), None))
    return jax.shard_map(
        functools.partial(body, cfg), mesh=mesh, in_specs=in_specs, out_specs=out_specs, check_vma=False
    )
```

```python
import functools
import math

import jax
import jax.numpy as jnp
from jax import lax
from jax.experimental import pallas as pl
from jax.experimental.pallas import tpu as pltpu
from jax.sharding import PartitionSpec as P

HEAD_DIM = 128
EPSILON = 1e-05
MESH = pl.DeviceIdType.MESH
NC = 2
NY = 4
NT = (((1,), (1,)), ((), ()))
F32, BF16 = jnp.float32, jnp.bfloat16


def front_kernel(
    cfg,
    src_len,
    tgt_len,
    dec_in,
    enc_in,
    gains_in,
    labels_in,
    wq_in,
    wk_in,
    wv_in,
    wo_in,
    emb_in,
    loss_out,
    grad_out,
    rows_out,
    gains,
    labels,
    dec,
    enc,
    wq,
    wkv,
    wo,
    emb,
    kv,
    ctx_own,
    ctx_got,
    part,
    summed,
    norm_stat,
    rows,
    logit,
    grad,
    local_stat,
    stat_x,
    stat_y,
    stat_z,
    load_sem,
    store_sem,
    kv_recv,
    a_recv,
    b_recv,
    c_recv,
    send_sem,
    recv_sem,
):
    nv, nz, ng, ny, nxl = cfg
    d = dec.shape[1]
    tz = dec.shape[0]
    ez = enc.shape[0]
    hd = wq.shape[1]
    tg = tz // ng
    ty = tg // ny
    width = d // (nxl * NC)
    wa, wb, wc = width // 4, width // 4, width // 2
    table_rows = emb.shape[0]
    nx = ng * nxl
    half = nz // 2

    v = lax.axis_index("vocab")
    z = lax.axis_index("seq")
    g = lax.axis_index("grp")
    c = v % NC
    y = (v // NC) % ny
    xl = v // (NC * ny)
    x = g * nxl + xl

    def vocab_of(xl_, y_, c_):
        return (xl_ * ny + y_) * NC + c_

    def at_x(x_, c_=None):
        return {"vocab": vocab_of(x_ % nxl, y, c if c_ is None else c_), "seq": z, "grp": x_ // nxl}

    def at_y(y_):
        return {"vocab": vocab_of(xl, y_, c), "seq": z, "grp": g}

    def at_z(z_):
        return {"vocab": v, "seq": z_, "grp": g}

    def at_v(v_):
        return {"vocab": v_, "seq": z, "grp": g}

    barrier = pltpu.get_barrier_semaphore()
    def far_first(n):
        return sorted(range(1, n), key=lambda o: -min(o, n - o))

    friends = [at_z((z + o) % nz) for o in far_first(nz)]
    friends += [{"vocab": v_, "seq": z, "grp": (g + o) % ng} for o in range(1, ng) for v_ in range(nv)]
    friends += [at_v((v + o) % nv) for o in range(1, nv)]

    loads = [
        pltpu.make_async_copy(src, dst, load_sem.at[i])
        for i, (src, dst) in enumerate(
            (
                (enc_in, enc),
                (wk_in, wkv.at[:, 0:hd]),
                (wv_in, wkv.at[:, hd : 2 * hd]),
                (dec_in, dec),
                (gains_in, gains),
                (wq_in, wq),
                (wo_in, wo),
                (labels_in, labels),
                (emb_in, emb),
            )
        )
    ]
    for load in loads[:6]:
        load.start()
    for friend in friends:
        pl.semaphore_signal(barrier, inc=1, device_id=friend, device_id_type=MESH)

    def remote(src, dst, out_sem, in_sem, device):
        return pltpu.make_async_remote_copy(
            src_ref=src, dst_ref=dst, send_sem=out_sem, recv_sem=in_sem, device_id=device, device_id_type=MESH
        )

    def arrived(ref, in_sem):
        remote(ref, ref, send_sem.at[0], in_sem, at_z((z + 1) % nz)).wait_recv()

    def left(ref, out_sem):
        remote(ref, ref, out_sem, recv_sem.at[0], at_z((z + 1) % nz)).wait_send()

    for load in loads[:3]:
        load.wait()
    for load in loads[6:]:
        load.start()
    own_kv = jnp.dot(enc[...], wkv[...], preferred_element_type=F32).astype(BF16)
    kv[z, 0] = own_kv[:, 0:hd]
    kv[z, 1] = own_kv[:, hd : 2 * hd]

    pl.semaphore_wait(barrier, len(friends))

    def kv_post(way, t, part_):
        step = (1, nz - 1)[way]
        ref = kv.at[(z + t * (nz - step)) % nz, part_]
        remote(ref, ref, send_sem.at[0], kv_recv.at[way, t, part_], at_z((z + step) % nz)).start()

    for part_ in (0, 1):
        for way in (0, 1):
            if half > 1:
                kv_post(way, 0, part_)
    for part_ in (0, 1):
        ref = kv.at[z, part_]
        remote(ref, ref, send_sem.at[0], kv_recv.at[0, half - 1, part_], at_z((z + half) % nz)).start()

    loads[3].wait()
    loads[4].wait()
    states = dec[...].astype(F32)
    centred = states - jnp.mean(states, axis=1, keepdims=True)
    variance = jnp.mean(centred * centred, axis=1, keepdims=True)
    normed = (centred * lax.rsqrt(variance + EPSILON) * gains[0:1, :]).astype(BF16)
    loads[5].wait()
    query = (jnp.dot(normed, wq[...], preferred_element_type=F32) * (1.0 / math.sqrt(hd))).astype(BF16)

    source_count = src_len[0]

    def scores_of(block):
        s = lax.dot_general(query, kv[block, 0], NT, preferred_element_type=F32)
        place = (block * ng + g) * ez + lax.broadcasted_iota(jnp.int32, s.shape, 1)
        valid = place < source_count
        return block, valid, jnp.where(valid, s, -1e30)

    scored = [scores_of(z)]
    for t in range(1, half + 1):
        for part_ in (0, 1):
            for way in (0, 1):
                if t < half or way == 0:
                    arrived(kv.at[(z + t * (nz - (1, nz - 1)[way])) % nz, part_], kv_recv.at[way, t - 1, part_])
                if t + 1 < half:
                    kv_post(way, t, part_)
        scored += [scores_of((z + o) % nz) for o in ((nz - t, t) if t < half else (half,))]
    top = functools.reduce(jnp.maximum, [s for _, _, s in scored])
    top = jnp.max(top, axis=1, keepdims=True)
    total = jnp.zeros((tz, ez), F32)
    acc = jnp.zeros((tz, hd), F32)
    for block, valid, s in scored:
        e = jnp.where(valid, jnp.exp(s - top), 0.0)
        total = total + e
        acc = acc + jnp.dot(e.astype(BF16), kv[block, 1], preferred_element_type=F32)
    total = jnp.sum(total, axis=1, keepdims=True)
    low = lax.broadcasted_iota(jnp.int32, (tz, 128), 1) < 64
    ctx_own[:, 0:hd] = acc
    ctx_own[:, hd : hd + 128] = jnp.where(low, top, total)
    remote(
        ctx_own.at[pl.ds(pl.multiple_of((1 - g) * tg, tg), tg)],
        ctx_got,
        send_sem.at[1],
        recv_sem.at[1],
        {"vocab": v, "seq": z, "grp": 1 - g},
    ).start()
    arrived(ctx_got, recv_sem.at[1])
    mine = ctx_own[pl.ds(pl.multiple_of(g * tg, tg), tg), :]
    other = ctx_got[...]
    top0, top1 = mine[:, hd : hd + 1], other[:, hd : hd + 1]
    both = jnp.maximum(top0, top1)
    f0, f1 = jnp.exp(top0 - both), jnp.exp(top1 - both)
    total = mine[:, hd + 64 : hd + 65] * f0 + other[:, hd + 64 : hd + 65] * f1
    context = ((mine[:, 0:hd] * f0 + other[:, 0:hd] * f1) / total).astype(BF16)

    def columns_of(xl_, c_):
        base = c_ * (d // NC)
        return (
            (base + xl_ * wa, wa),
            (base + nxl * wa + xl_ * wb, wb),
            (base + nxl * (wa + wb) + xl_ * wc, wc),
        )

    loads[6].wait()
    piece = xl * NC + c
    pieces = nxl * NC
    for op in [pieces // 2, *(o for o in range(pieces - 1, -1, -1) if o != pieces // 2)]:
        to_piece = (piece + op) % pieces
        weights = jnp.concatenate(
            [
                wo[:, pl.ds(pl.multiple_of(start, 128), size)]
                for start, size in columns_of(to_piece // NC, to_piece % NC)
            ],
            axis=1,
        )
        projected = jnp.dot(context, weights, preferred_element_type=F32).astype(BF16)
        for y_ in range(ny):
            part[vocab_of(to_piece // NC, y_, to_piece % NC)] = projected[y_ * ty : (y_ + 1) * ty]
        for oy in [*far_first(ny), 0]:
            if op + oy > 0:
                to = vocab_of(to_piece // NC, (y + oy) % ny, to_piece % NC)
                remote(part.at[to], summed.at[v], send_sem.at[2], recv_sem.at[2], at_v(to)).start()
    own_cols = [(pl.multiple_of(start, 128), size) for start, size in columns_of(xl, c)]
    own_row = pl.multiple_of(g * tg + y * ty, ty)
    hidden = part[v].astype(F32) + jnp.concatenate(
        [dec[pl.ds(own_row, ty), pl.ds(start, size)].astype(F32) for start, size in own_cols], axis=1
    )
    arrived(summed.at[0 : nv - 1], recv_sem.at[2])
    for o in range(1, nv):
        hidden = hidden + summed[(v + o) % nv].astype(F32)

    own_mean = jnp.mean(hidden, axis=1, keepdims=True)
    own_square = jnp.sum((hidden - own_mean) * (hidden - own_mean), axis=1, keepdims=True)
    low = lax.broadcasted_iota(jnp.int32, (ty, 128), 1) < 64
    norm_stat[piece] = jnp.where(low, own_mean, own_square)
    for o in range(1, pieces):
        to = (piece + o) % pieces
        remote(
            norm_stat.at[piece],
            norm_stat.at[piece],
            send_sem.at[3],
            recv_sem.at[3],
            at_v(vocab_of(to // NC, y, to % NC)),
        ).start()
    arrived(norm_stat.at[0 : pieces - 1], recv_sem.at[3])
    means = [norm_stat[i, :, 0:1] for i in range(pieces)]
    squares = [norm_stat[i, :, 64:65] for i in range(pieces)]
    mean = sum(means) * (1.0 / pieces)
    square = sum(squares) + width * sum((m - mean) * (m - mean) for m in means)
    scale = lax.rsqrt(square * (1.0 / d) + EPSILON)
    gain = jnp.concatenate([gains[1:2, pl.ds(start, size)] for start, size in own_cols], axis=1)
    final = ((hidden - mean) * scale * gain).astype(BF16)
    at = 0
    for start, size in own_cols:
        rows[z, g, y, :, pl.ds(start, size)] = final[:, at : at + size]
        at += size

    def cols_all(c_):
        base = pl.multiple_of(c_ * (d // NC), 128)
        return (
            pl.ds(base, nxl * wa),
            pl.ds(pl.multiple_of(base + nxl * wa, 128), nxl * wb),
            pl.ds(pl.multiple_of(base + nxl * (wa + wb), 128), nxl * wc),
        )

    def cols_piece(xl_):
        return [pl.ds(pl.multiple_of(start, 128), size) for start, size in columns_of(xl_, c)]

    _, own_b, own_c = cols_piece(xl)
    all_a, all_b, all_c = cols_all(c)

    def exchange(n, me, ref_of, out_sem, in_sem, device_of):
        ref = ref_of(me)
        for o in far_first(n):
            remote(ref, ref, out_sem, in_sem, device_of((me + o) % n)).start()

    swap = c

    def pick(here, there):
        return here + swap * (there - here)

    def place_b(i):
        return pick(x, i), pick(i, y)

    def place_c(i):
        return pick(i, x), pick(y, i)

    def at_xy(xy):
        return {"vocab": vocab_of(xy[0] % nxl, xy[1], c), "seq": z, "grp": xy[0] // nxl}

    def a1(xy):
        return rows.at[z, xy[0] // nxl, xy[1], :, cols_piece(xy[0] % nxl)[0]]

    def b1(z_):
        return rows.at[z_, g, y, :, own_b]

    def c1(z_):
        return rows.at[z_, g, y, :, own_c]

    def b2(xy):
        return rows.at[:, xy[0] // nxl, xy[1], :, cols_piece(xy[0] % nxl)[1]]

    def c2(xy):
        return rows.at[:, xy[0] // nxl, xy[1], :, cols_piece(xy[0] % nxl)[2]]

    def along_x(kind, x_):
        return rows.at[:, x_ // nxl, :, :, cols_piece(x_ % nxl)[kind]]

    def along_y(kind, y_):
        return rows.at[:, :, y_, :, cols_all(c)[kind]]

    all_a1 = rows.at[0, 0, 0, :, 0 : (nx * ny - 1) * wa]
    all_b1 = rows.at[0 : nz - 1, 0, 0, :, 0:wb]
    all_c1 = rows.at[0 : nz - 1, 0, 0, :, 0:wc]
    all_b2 = rows.at[:, 0, 0 : nx - 1, :, 0:wb]
    all_c2 = rows.at[:, 0, 0 : ny - 1, :, 0:wc]
    all_a3 = rows.at[0 : nz - 1, :, :, :, 0 : nxl * wa]
    all_b3 = rows.at[:, :, 0 : ny - 1, :, 0 : nxl * wb]
    all_c3 = rows.at[:, 0, :, :, 0 : (nx - 1) * wc]

    me_b, me_c = pick(y, x), pick(x, y)
    exchange(nz, z, c1, send_sem.at[6], recv_sem.at[6], at_z)
    exchange(nz, z, b1, send_sem.at[5], recv_sem.at[5], at_z)

    ref = a1((x, y))
    hops = [(min(o % nx, nx - o % nx) + min(o // nx, ny - o // nx), o) for o in range(1, nx * ny)]
    for _, o in sorted(hops, reverse=True):
        to = ((x + o) % nx, (y + o // nx) % ny)
        remote(ref, ref, send_sem.at[4], recv_sem.at[4], at_xy(to)).start()
    sibling = at_x(x, 1 - c)

    def share(kind, ref):
        remote(ref, ref, send_sem.at[12 + kind], recv_sem.at[7 + kind], sibling).start()

    def last(view, kind, n, me, in_sems, device_of):
        ref = view(kind, me)
        for o in far_first(n):
            remote(ref, ref, send_sem.at[9 + kind], in_sems.at[me], device_of((me + o) % n)).start()
        share(kind, ref)

    def last_in(view, kind, n, me, in_sems):
        for o in reversed(far_first(n)):
            ref = view(kind, (me + o) % n)
            arrived(ref, in_sems.at[(me + o) % n])
            share(kind, ref)

    def at_x_(i):
        return at_x(i)

    mid = nz // 2

    def half_x(kind, i, part_):
        return rows.at[part_ * mid : (part_ + 1) * mid, i // nxl, :, :, cols_piece(i % nxl)[kind]]

    def half_y(kind, i, part_):
        return rows.at[part_ * mid : (part_ + 1) * mid, :, i, :, cols_all(c)[kind]]

    relay_sems = (None, b_recv, c_recv)

    def relay_send(view, kind, block, part_, sem, to, device_of):
        ref = view(kind, block, part_)
        remote(ref, ref, send_sem.at[9 + kind], relay_sems[kind].at[sem], device_of(to)).start()

    def relay_get(view, kind, block, part_, sem):
        ref = view(kind, block, part_)
        arrived(ref, relay_sems[kind].at[sem])
        share(kind, ref)

    def relay_start(view, kind, me, device_of):
        for first in (0, 1):
            relay_send(view, kind, me, first, first, (me + 1) % nx, device_of)
            relay_send(view, kind, me, 1 - first, 3 - first, (me + nx - 1) % nx, device_of)
        for part_ in (0, 1):
            share(kind, view(kind, me, part_))

    def relay_pass(view, kind, me, device_of):
        down, up = (me + nx - 1) % nx, (me + 1) % nx
        relay_get(view, kind, down, 0, 0)
        relay_send(view, kind, down, 0, 4, up, device_of)
        relay_get(view, kind, up, 1, 3)
        relay_send(view, kind, up, 1, 5, down, device_of)

    def relay_end(view, kind, me):
        relay_get(view, kind, (me + nx - 1) % nx, 1, 1)
        relay_get(view, kind, (me + 1) % nx, 0, 2)
        relay_get(view, kind, (me + 2) % nx, 0, 4)
        relay_get(view, kind, (me + 2) % nx, 1, 5)

    def slab(kind, z_):
        return rows.at[z_, :, :, :, all_a]

    def a_post(block, o, device):
        ref = slab(0, block)
        remote(ref, ref, send_sem.at[9], a_recv.at[o], at_z(device)).start()

    def a_get(o):
        ref = slab(0, (z + o) % nz)
        arrived(ref, a_recv.at[o])
        share(0, ref)

    def a_pass():
        for o, next_o, device in ((2, 3, z + nz - 1), (nz - 2, nz - 3, z + 1)):
            arrived(slab(0, (z + o) % nz), a_recv.at[o])
            a_post((z + o) % nz, next_o, device % nz)
            share(0, slab(0, (z + o) % nz))

    arrived(all_a1, recv_sem.at[4])
    for o in (2, nz - 2, 4, 1, nz - 1):
        a_post(z, o, (z + nz - o) % nz)
    share(0, slab(0, z))
    arrived(all_c1, recv_sem.at[6])
    ref = c2((x, y))
    for o in far_first(nx):
        remote(ref, ref, send_sem.at[8], recv_sem.at[16], at_xy(place_b((me_b + o) % nx))).start()
    arrived(all_b1, recv_sem.at[5])
    ref = b2((x, y))
    for o in far_first(nx):
        remote(ref, ref, send_sem.at[7], recv_sem.at[15], at_xy(place_c((me_c + o) % nx))).start()
    arrived(all_c2, recv_sem.at[16])

    @pl.when(c == 0)
    def _():
        relay_start(half_x, 2, x, at_x_)
        arrived(all_b2, recv_sem.at[15])
        relay_start(half_y, 1, y, at_y)
        a_pass()
        relay_pass(half_x, 2, x, at_x_)
        relay_pass(half_y, 1, y, at_y)
        relay_end(half_y, 1, y)

    @pl.when(c == 1)
    def _():
        relay_start(half_y, 2, y, at_y)
        arrived(all_b2, recv_sem.at[15])
        relay_start(half_x, 1, x, at_x_)
        a_pass()
        relay_pass(half_y, 2, y, at_y)
        relay_pass(half_x, 1, x, at_x_)
        relay_end(half_x, 1, x)

    for o in (1, nz - 1, 4, 3, nz - 3):
        a_get(o)
    their_a, their_b, their_c = cols_all(1 - c)
    arrived(rows.at[:, :, :, :, their_a], recv_sem.at[7])
    arrived(rows.at[:, :, :, :, their_b], recv_sem.at[8])
    loads[7].wait()
    loads[8].wait()
    table_base = ((v * nz + z) * ng + g) * table_rows
    step_blocks = max(1, 256 // tz)
    step_rows = step_blocks * tz
    early = nxl * (wa + wb)

    def logits_of(i, starts, size):
        total_ = None
        for start in starts:
            chunk = rows[pl.ds(i * step_blocks, step_blocks), :, :, :, start : start + size].reshape(step_rows, size)
            values = lax.dot_general(emb[:, start : start + size], chunk, NT, preferred_element_type=F32)
            total_ = values if total_ is None else total_ + values
        return total_

    def lanes_of(i):
        return pl.ds(pl.multiple_of(i * step_rows, 128), step_rows)

    def early_step(i, carry):
        logit[:, lanes_of(i)] = logits_of(i, range(0, d, d // NC), early)
        return carry

    steps = nz // step_blocks

    @pl.when(c == 0)
    def _():
        relay_end(half_x, 2, x)

    @pl.when(c == 1)
    def _():
        relay_end(half_y, 2, y)

    lax.fori_loop(0, steps, early_step, 0)
    arrived(rows.at[:, :, :, :, their_c], recv_sem.at[9])
    rows_store = pltpu.make_async_copy(rows, rows_out, store_sem.at[0])
    rows_store.start()

    for i in range(steps):
        lanes = pl.ds(i * step_rows, step_rows)
        values = logit[:, lanes] + logits_of(i, range(early, d, d // NC), d // NC - early)
        logit[:, lanes] = values
        top_ = jnp.max(values, axis=0, keepdims=True)
        total_ = jnp.sum(jnp.exp(values - top_), axis=0, keepdims=True)
        token = table_base + lax.broadcasted_iota(jnp.int32, values.shape, 0)
        local_stat[i, 0:1, :] = top_ + jnp.log(total_)
        local_stat[i, 1:2, :] = jnp.sum(jnp.where(token == labels[:, lanes], values, 0.0), axis=0, keepdims=True)

    stat_rows = nz * tz // 128
    per_step = step_rows // 128
    nxc = nx * NC
    xc = x * NC + c
    for r in range(stat_rows):
        for k in range(2):
            stat_x[xc, k * stat_rows + r : k * stat_rows + r + 1, :] = local_stat[
                r // per_step, k : k + 1, (r % per_step) * 128 : (r % per_step + 1) * 128
            ]

    low_rows, high_rows = pl.ds(0, stat_rows), pl.ds(stat_rows, stat_rows)
    rounds = (
        (stat_x, nxc, xc, lambda i: at_x(i // NC, i % NC)),
        (stat_y, ny, y, at_y),
        (stat_z, nz, z, at_z),
    )

    def stat_send(k, some, out_sem, in_sem):
        ref, n, me, device_of = rounds[k]
        exchange(n, me, lambda i: ref.at[i, some], send_sem.at[out_sem + k], recv_sem.at[in_sem + k], device_of)

    def picked_of(k):
        ref, n = rounds[k][:2]
        arrived(ref.at[0 : n - 1, high_rows], recv_sem.at[17 + k])
        return sum(ref[i, stat_rows : 2 * stat_rows] for i in range(n))

    def settle():
        for i, ref in enumerate(
            (
                kv.at[0 : nz - 1],
                ctx_got,
                part.at[0 : nv - 1],
                norm_stat.at[0 : pieces - 1],
                all_a1,
                all_b1,
                all_c1,
                all_b2,
                all_c2,
                all_a3,
                all_b3,
                all_c3,
                rows.at[:, :, :, :, all_a],
                rows.at[:, :, :, :, all_b],
                rows.at[:, :, :, :, all_c],
            )
        ):
            left(ref, send_sem.at[i])
        for k, (ref, n, _, _) in enumerate(rounds[:2]):
            left(ref.at[0 : n - 1, low_rows], send_sem.at[15 + k])
            left(ref.at[0 : n - 1, high_rows], send_sem.at[18 + k])
        rows_store.wait()

    for k, (ref, n, me, _) in enumerate(rounds):
        if k > 0:
            ref[me, 0:stat_rows] = lse
        stat_send(k, low_rows, 15, 10)
        if k > 0:
            ref[me, stat_rows : 2 * stat_rows] = picked_of(k - 1)
        stat_send(k, high_rows, 18, 17)
        if k == 2:
            settle()
        arrived(ref.at[0 : n - 1, low_rows], recv_sem.at[10 + k])
        lses = [ref[i, 0:stat_rows] for i in range(n)]
        top_ = functools.reduce(jnp.maximum, lses)
        lse = top_ + jnp.log(sum(jnp.exp(s - top_) for s in lses))

    place = lax.broadcasted_iota(jnp.int32, lse.shape, 0) * 128 + lax.broadcasted_iota(jnp.int32, lse.shape, 1)
    live = place < tgt_len[0]
    row_lse = lse
    lse = jnp.where(live, lse, 1e30)
    lse = jnp.concatenate([lse[r : r + 1, :] for r in range(stat_rows)], axis=1)
    place = lax.broadcasted_iota(jnp.int32, labels.shape, 1)
    hit = jnp.where(place < tgt_len[0], labels[...] - table_base, -1)

    def grad_step(i, carry):
        some = pl.ds(i * 128, 128)
        token = i * 128 + lax.broadcasted_iota(jnp.int32, (128, nz * tz), 0)
        grad[some, :] = (jnp.exp(logit[some, :] - lse) - jnp.where(token == hit, 1.0, 0.0)).astype(BF16)
        pltpu.make_async_copy(grad.at[some], grad_out.at[some], store_sem.at[1]).start()
        return carry

    lax.fori_loop(0, table_rows // 128, grad_step, 0)

    loss_out[...] = jnp.where(live, row_lse - picked_of(2), 0.0)
    left(stat_z.at[0 : nz - 1, low_rows], send_sem.at[17])
    left(stat_z.at[0 : nz - 1, high_rows], send_sem.at[20])
    pltpu.make_async_copy(grad, grad_out, store_sem.at[1]).wait()


def grad_kernel(tgt_len, grad, rows, loss, out, loss_out):
    loss_out[...] = loss[...]
    nz, block = rows.shape[0], out.shape[1]
    tz = grad.shape[1] // nz
    cols = pl.ds(pl.multiple_of(pl.program_id(0) * block, 128), block)
    step = max(1, 256 // tz)
    live = (tgt_len[0] + step * tz - 1) // (step * tz)
    for n in range(1, nz // step + 1):

        @pl.when(jnp.clip(live, 1, nz // step) == n)
        def _():
            count = n * step * tz
            chunk = rows[0 : n * step, :, :, :, cols].reshape(count, block)
            out[...] = jnp.dot(grad[:, 0:count], chunk, preferred_element_type=F32).astype(BF16)


def body(
    cfg,
    decoder_states,
    encoder_states,
    ln_gains,
    w_query,
    w_key,
    w_value,
    w_out,
    embedding,
    labels,
    src_length,
    tgt_length,
):
    nv, nz, ng, ny, nxl = cfg
    tz, d = decoder_states.shape
    ez = encoder_states.shape[0]
    hd = w_query.shape[1]
    table_rows = embedding.shape[0]
    target = labels.shape[0]
    tg = tz // ng
    ty = tg // ny
    width = d // (nxl * NC)
    nx = ng * nxl
    half = nz // 2
    pieces = nxl * NC
    step_blocks = max(1, 256 // tz)
    stat_rows = target // 128
    hbm = pl.BlockSpec(memory_space=pl.ANY)
    vmem = pl.BlockSpec(memory_space=pltpu.VMEM)
    smem = pl.BlockSpec(memory_space=pltpu.SMEM)
    dma = pltpu.SemaphoreType.DMA
    far = [
        pltpu.with_memory_space_constraint(array, pltpu.HBM)
        for array in (
            decoder_states,
            encoder_states,
            ln_gains,
            labels.reshape(1, target),
            w_query,
            w_key,
            w_value,
            w_out,
            embedding,
        )
    ]
    loss, grad, rows = pl.pallas_call(
        functools.partial(front_kernel, cfg),
        out_shape=(
            jax.ShapeDtypeStruct((stat_rows, 128), F32),
            pltpu.VMEM((table_rows, target), BF16),
            pltpu.VMEM((nz, ng, ny, ty, d), BF16),
        ),
        in_specs=[smem, smem] + [hbm] * len(far),
        out_specs=(vmem, hbm, hbm),
        scratch_shapes=[
            pltpu.VMEM(ln_gains.shape, F32),
            pltpu.VMEM((1, target), jnp.int32),
            pltpu.VMEM((tz, d), BF16),
            pltpu.VMEM((ez, d), BF16),
            pltpu.VMEM((d, hd), BF16),
            pltpu.VMEM((d, 2 * hd), BF16),
            pltpu.VMEM((hd, d), BF16),
            pltpu.VMEM((table_rows, d), BF16),
            pltpu.VMEM((nz, 2, ez, hd), BF16),
            pltpu.VMEM((tz, hd + 128), F32),
            pltpu.VMEM((tg, hd + 128), F32),
            pltpu.VMEM((nv, ty, width), BF16),
            pltpu.VMEM((nv, ty, width), BF16),
            pltpu.VMEM((pieces, ty, 128), F32),
            pltpu.VMEM((nz, ng, ny, ty, d), BF16),
            pltpu.VMEM((table_rows, target), F32),
            pltpu.VMEM((table_rows, target), BF16),
            pltpu.VMEM((nz // step_blocks, 8, step_blocks * tz), F32),
            pltpu.VMEM((nx * NC, 2 * stat_rows, 128), F32),
            pltpu.VMEM((ny, 2 * stat_rows, 128), F32),
            pltpu.VMEM((nz, 2 * stat_rows, 128), F32),
            dma((9,)),
            dma((2,)),
            dma((2, half, 2)),
            dma((nz,)),
            dma((6,)),
            dma((6,)),
            dma((21,)),
            dma((20,)),
        ],
        compiler_params=pltpu.CompilerParams(
            collective_id=0, has_side_effects=True, vmem_limit_bytes=40 * 1024 * 1024
        ),
    )(src_length, tgt_length, *far)
    block = 512
    grad_table, loss = pl.pallas_call(
        grad_kernel,
        out_shape=(jax.ShapeDtypeStruct((table_rows, d), BF16), jax.ShapeDtypeStruct(loss.shape, F32)),
        grid=(d // block,),
        in_specs=[smem, vmem, vmem, vmem],
        out_specs=(pl.BlockSpec((table_rows, block), lambda i: (0, i)), pl.BlockSpec(loss.shape, lambda i: (0, 0))),
        compiler_params=pltpu.CompilerParams(vmem_limit_bytes=24 * 1024 * 1024),
    )(tgt_length, *(pltpu.with_memory_space_constraint(array, pltpu.VMEM) for array in (grad, rows)), loss)
    return (loss.reshape(target), grad_table)


def solution(mesh):
    nv, nz, ng = mesh.shape["vocab"], mesh.shape["seq"], mesh.shape["grp"]
    cfg = (nv, nz, ng, NY, nv // (NY * NC))
    in_specs = (
        P("seq", None),
        P(("seq", "grp"), None),
        P(),
        P(None, "vocab"),
        P(None, "vocab"),
        P(None, "vocab"),
        P("vocab", None),
        P(("vocab", "seq", "grp"), None),
        P(),
        P(),
        P(),
    )
    out_specs = (P(), P(("vocab", "seq", "grp"), None))
    return jax.shard_map(
        functools.partial(body, cfg), mesh=mesh, in_specs=in_specs, out_specs=out_specs, check_vma=False
    )
```
